128 devices in a mesh: wide: 8 (over y, core), narrow: 16 (over z, x).
Axes of the slice: x: 4, y: 4, z: 4, core: 2. Of those that a mesh axis runs over, the one named last changes fastest.
Arguments:
- token_ids: int32 [2, 16, 1024], P(None, 'narrow'), may hold values from 0 to 49151
- target_ids: int32 [2, 16, 1024], P(None, 'narrow'), may hold values from 0 to 49151
- prefix_lengths: int32 [2, 16], P(None, 'narrow'), may hold values from 102 to 512
- loss_positions: int32 [2, 16, 128], P(None, 'narrow'), may hold values from 0 to 1023, as said below
- w_input: float32 [1, 960, 1600], P(None, 'wide', 'narrow'), may hold values from -0.1875 to 0.1875
- w_output: float32 [1, 960, 960], P(None, 'wide', 'narrow'), may hold values from -0.375 to 0.375
- w_gate_up: float32 [1, 960, 5120], P(None, 'wide', 'narrow'), may hold values from -0.1875 to 0.1875
- w_down: float32 [1, 960, 2560], P(None, 'wide', 'narrow'), may hold values from -0.125 to 0.125
- norm_gains: float32 [3, 960], replicated, may hold values from 0.35 to 2.55
- embed_table: float32 [49152, 960], P(('wide', 'narrow')), may hold values from -0.5163978 to 0.5163978
- moment_input: float32 [1, 960, 1600], P(None, 'wide', 'narrow'), may hold values from -1.5258789e-05 to 1.5258789e-05
- moment_output: float32 [1, 960, 960], P(None, 'wide', 'narrow'), may hold values from -1.5258789e-05 to 1.5258789e-05
- moment_gate_up: float32 [1, 960, 5120], P(None, 'wide', 'narrow'), may hold values from -1.5258789e-05 to 1.5258789e-05
- moment_down: float32 [1, 960, 2560], P(None, 'wide', 'narrow'), may hold values from -1.5258789e-05 to 1.5258789e-05
- table_first: float32 [49152, 960], P(('wide', 'narrow')), may hold values from -1.66893e-06 to 1.66893e-06
- table_second: float32 [49152, 960], P(('wide', 'narrow')), may hold values from 3.68297e-13 to 1.473188e-12
- gains_first: float32 [3, 960], replicated, may hold values from -1.5258789e-05 to 1.5258789e-05
- gains_second: float32 [3, 960], replicated, may hold values from 3.68297e-11 to 1.473188e-10
Outputs:
- loss_sum: float32 [], replicated
- loss_count: float32 [], replicated
- grad_norm: float32 [], replicated
- new_moment_input: float32 [1, 960, 1600], P(None, 'wide', 'narrow')
- new_moment_output: float32 [1, 960, 960], P(None, 'wide', 'narrow')
- new_moment_gate_up: float32 [1, 960, 5120], P(None, 'wide', 'narrow')
- new_moment_down: float32 [1, 960, 2560], P(None, 'wide', 'narrow')
- new_w_input: float32 [1, 960, 1600], P(None, 'wide', 'narrow')
- new_w_output: float32 [1, 960, 960], P(None, 'wide', 'narrow')
- new_w_gate_up: float32 [1, 960, 5120], P(None, 'wide', 'narrow')
- new_w_down: float32 [1, 960, 2560], P(None, 'wide', 'narrow')
- low_w_input: bfloat16 [1, 960, 1600], P(None, 'wide', 'narrow')
- low_w_output: bfloat16 [1, 960, 960], P(None, 'wide', 'narrow')
- low_w_gate_up: bfloat16 [1, 960, 5120], P(None, 'wide', 'narrow')
- low_w_down: bfloat16 [1, 960, 2560], P(None, 'wide', 'narrow')
- new_table_first: float32 [49152, 960], P(('wide', 'narrow'))
- new_table_second: float32 [49152, 960], P(('wide', 'narrow'))
- new_table: float32 [49152, 960], P(('wide', 'narrow'))
- low_table: bfloat16 [49152, 960], P(('wide', 'narrow'))
- new_gains_first: float32 [3, 960], replicated
- new_gains_second: float32 [3, 960], replicated
- new_gains: float32 [3, 960], replicated
The draws below stay inside these ranges and needn't reach their ends.
Inputs may be any that keep to these rules, and one draw needn't show every extreme that they name: Entry j of loss_positions[m, s] lies among positions (j // 16) * 128 to (j // 16) * 128 + 127.
All inputs are finite; a program needn't handle non-finite values.
Results may differ from the reference program's by a relative error of at most 0.007.
The reference program's roundings to bfloat16 on the way count: a program that leaves them out, or rounds other values in their place, can miss the bound.
Values may be sent and summed in bfloat16 or wider, within the bound.
A program may use at most 320 MiB of HBM per device.

```python
import math
import jax
import jax.numpy as jnp
import numpy as np
from jax import lax

D = 960
H = 15
KVH = 5
HD = 64
FF = 2560
V = 49152
LAYERS = 1
MB = 2
SEQ = 1024
ITERS = 5
STEP = 10
SEQS = 16
ROWS = 128
PICK = 16
PICKS = 128
GAINS = 3
QKV = 1600
PARAMS = 57019200


def draw_loss_positions(key, part):
    key = jax.random.fold_in(key, 11)
    offsets = jax.random.randint(key, (MB, SEQS, PICKS), 0, ROWS)
    starts = jnp.arange(PICKS) // PICK * ROWS
    return (offsets + starts[None, None, :]).astype(jnp.int32)


def draw_norm_gains(key, part):
    key = jax.random.fold_in(key, 12)
    ramp = 0.6 + 1.2 * jnp.arange(D).astype(jnp.float32) / D
    spread = jax.random.uniform(key, (GAINS, D), jnp.float32, 0.8, 1.2)
    return ramp[None, :] * spread


def draw_embed_table(key, part):
    key = jax.random.fold_in(key, 13)
    places = jnp.arange(V).astype(jnp.float32)[:, None] / V
    direction = jax.random.truncated_normal(jax.random.fold_in(key, 7), -3.0, 3.0, (D,), jnp.float32) * 0.57
    common = (0.3 + 1.5 * places) * direction[None, :]
    base = jax.random.truncated_normal(key, -4.0, 4.0, (V, D), jnp.float32)
    factor = 1.0 + 2.0 * places
    return (base * factor + common) / math.sqrt(D)


def plant(values, own_key, least, largest):
    longest = values.shape.index(max(values.shape))
    spots = []
    for shift in (0, 1):
        where = [jax.random.randint(jax.random.fold_in(own_key, axis), (), 0, length) for axis, length in enumerate(values.shape)]
        where[longest] = (where[longest] + shift) % values.shape[longest]
        spots.append(tuple(where))
    return values.at[spots[0]].set(least).at[spots[1]].set(largest)


def levels(key, dims, cuts, low, high):
    factor_of, own = 1.0, jax.random.fold_in(key, 6)
    for axis_at, shards_of in cuts:
        heights = jnp.exp(jax.random.uniform(jax.random.fold_in(own, axis_at), (shards_of,), jnp.float32, low / len(cuts), high / len(cuts)))
        factor_of = factor_of * jnp.repeat(heights, dims[axis_at] // shards_of).reshape([-1 if axis == axis_at else 1 for axis in range(len(dims))])
    return factor_of


def cumulative_ranks(amount, slope):
    weights = [(1 << 20) // math.isqrt(grade ** slope) + 1 for grade in range(1, amount + 1)]
    scale = 1 + sum(weights) // (1 << 30)
    return np.cumsum(np.array([max(1, weight // scale) for weight in weights]))


def skewed_ids(own_key, dims, count, skew):
    grid = cumulative_ranks(count, skew)
    pick = jax.random.randint(jax.random.fold_in(own_key, 1), dims, 0, int(grid[count - 1]))
    standing = jnp.searchsorted(jnp.asarray(grid, jnp.int32), pick, side="right")
    return jax.random.permutation(jax.random.fold_in(own_key, 2), count)[standing].astype(jnp.int32)


def bell_draw(key, shape, width, reach, cuts=(), kind=jnp.bfloat16):
    level = levels(key, shape, cuts, -0.22, 0.18) if cuts else 1.0
    result = jax.random.normal(key, shape, jnp.float32) * width * level
    return jnp.minimum(jnp.maximum(result, -reach), reach).astype(kind)


def setup_inputs(seed: int = 0) -> dict:
    key_list = jax.random.split(jax.random.key(seed), 19)
    token_ids = plant(skewed_ids(key_list[0], (MB, SEQS, SEQ), V, 2), jax.random.fold_in(key_list[0], 3), 0, V - 1).astype(jnp.int32)
    target_ids = plant(skewed_ids(key_list[1], (MB, SEQS, SEQ), V, 2), jax.random.fold_in(key_list[1], 3), 0, V - 1).astype(jnp.int32)
    prefix_lengths = plant(jax.random.randint(key_list[2], (MB, SEQS), SEQ // 10, SEQ // 2 + 1), jax.random.fold_in(key_list[2], 1), SEQ // 10, (SEQ // 2 + 1) - 1).astype(jnp.int32)
    loss_positions = draw_loss_positions(jax.random.fold_in(key_list[18], 71), 0)
    w_input = bell_draw(key_list[4], (LAYERS, D, QKV), D ** -0.5, 0.1875, ((1, 8), (2, 16)), jnp.float32)
    w_output = bell_draw(key_list[5], (LAYERS, D, D), (D // 4) ** -0.5, 0.375, ((1, 8), (2, 16)), jnp.float32)
    w_gate_up = bell_draw(key_list[6], (LAYERS, D, 2 * FF), D ** -0.5, 0.1875, ((1, 8), (2, 16)), jnp.float32)
    w_down = bell_draw(key_list[7], (LAYERS, D, FF), FF ** -0.5, 0.125, ((1, 8), (2, 16)), jnp.float32)
    norm_gains = draw_norm_gains(jax.random.fold_in(key_list[18], 71), 0)
    embed_table = draw_embed_table(jax.random.fold_in(key_list[18], 71), 0)
    moment_input = bell_draw(key_list[10], (LAYERS, D, QKV), (0.02 / PARAMS ** 0.5), 1.52587890625e-05, ((1, 8), (2, 16)), jnp.float32)
    moment_output = bell_draw(key_list[11], (LAYERS, D, D), (0.02 / PARAMS ** 0.5), 1.52587890625e-05, ((1, 8), (2, 16)), jnp.float32)
    moment_gate_up = bell_draw(key_list[12], (LAYERS, D, 2 * FF), (0.02 / PARAMS ** 0.5), 1.52587890625e-05, ((1, 8), (2, 16)), jnp.float32)
    moment_down = bell_draw(key_list[13], (LAYERS, D, FF), (0.02 / PARAMS ** 0.5), 1.52587890625e-05, ((1, 8), (2, 16)), jnp.float32)
    table_first = bell_draw(key_list[14], (V, D), (0.0022 / PARAMS ** 0.5), 1.6689300537109375e-06, ((0, 128),), jnp.float32)
    table_second = jnp.clip(jnp.exp(math.log(1.473187999541381e-12) - 1.3862944 * jax.random.uniform(key_list[15], (V, D), jnp.float32) ** levels(key_list[15], (V, D), ((0, 128),), -0.2, 0.2)), 3.6829699988534526e-13, 1.473187999541381e-12)
    gains_first = bell_draw(key_list[16], (GAINS, D), (0.022 / PARAMS ** 0.5), 1.52587890625e-05, (), jnp.float32)
    gains_second = jnp.clip(jnp.exp(jax.random.uniform(key_list[17], (GAINS, D), jnp.float32, math.log(3.682969901275257e-11), math.log(1.4731879605101028e-10))), 3.682969901275257e-11, 1.4731879605101028e-10)
    return dict(token_ids=token_ids, target_ids=target_ids, prefix_lengths=prefix_lengths, loss_positions=loss_positions, w_input=w_input, w_output=w_output, w_gate_up=w_gate_up, w_down=w_down, norm_gains=norm_gains, embed_table=embed_table, moment_input=moment_input, moment_output=moment_output, moment_gate_up=moment_gate_up, moment_down=moment_down, table_first=table_first, table_second=table_second, gains_first=gains_first, gains_second=gains_second)


HIGHEST_PRECISION = lax.Precision.HIGHEST
NORM_EPS = 1e-05
ROPE_THETA = 100000.0
SMOOTH = 0.1
ZLOSS_WEIGHT = 0.0001
CLIP_NORM = 0.02
MOMENTUM = 0.95
NS_A = 3.4445
NS_B = -4.775
NS_C = 2.0315
MUON_RATE = 0.1
WEIGHT_DECAY = 0.1
BETA_ONE = 0.9
BETA_TWO = 0.95
TABLE_RATE = 0.03
GAIN_RATE = 0.4
ADAM_EPS = 1e-08
NEGATIVE = -1e+30

@jax.custom_vjp
def low(v):
    return lax.optimization_barrier(v.astype(jnp.bfloat16)).astype(jnp.float32)

@jax.custom_vjp
def low_back(v):
    return v

def low_keep(v):
    return (low(v), None)

def low_pass(kept, grad):
    return (grad,)

def back_keep(v):
    return (v, None)

def back_low(kept, grad):
    return (low(grad),)
low.defvjp(low_keep, low_pass)
low_back.defvjp(back_keep, back_low)

def matmul(left_side, right_side):
    return jnp.dot(left_side, right_side, precision=HIGHEST_PRECISION, preferred_element_type=jnp.float32)

def rms_norm(values, gain_row):
    return values * lax.rsqrt(lax.optimization_barrier(jnp.mean(values * values, axis=-1, keepdims=True)) + NORM_EPS) * gain_row

def rotate(values, places):
    half_width = HD // 2
    frequency = ROPE_THETA ** (-2.0 * jnp.arange(half_width).astype(jnp.float32) / HD)
    angles = places.astype(jnp.float32)[:, None] * frequency[None, :]
    cosine = jnp.concatenate([jnp.cos(angles), jnp.cos(angles)], axis=-1)[:, None, :]
    sine_part = jnp.concatenate([jnp.sin(angles), jnp.sin(angles)], axis=-1)[:, None, :]
    turned = jnp.concatenate([-values[..., half_width:], values[..., :half_width]], axis=-1)
    return values * cosine + turned * sine_part

def layer_pass(hidden, lowered, layer_idx, places, allowed):
    proj_in = lowered[0][layer_idx]
    proj_out = lowered[1][layer_idx]
    proj_gate = lowered[2][layer_idx]
    proj_down = lowered[3][layer_idx]
    gains = lowered[4]
    length = hidden.shape[0]
    group_size = H // KVH
    normed = low(rms_norm(hidden, gains[2 * layer_idx]))
    projected = low_back(matmul(normed, proj_in))
    query = low(rotate(projected[:, :H * HD].reshape(length, H, HD), places)).reshape(length, KVH, group_size, HD)
    key_rows = low(rotate(projected[:, H * HD:(H + KVH) * HD].reshape(length, KVH, HD), places))
    value_rows = low(projected[:, (H + KVH) * HD:].reshape(length, KVH, HD))
    scores = low_back(jnp.einsum('qkgd,tkd->kgqt', query, key_rows, precision=HIGHEST_PRECISION) * HD ** (-0.5))
    scores = jnp.where(allowed, scores, NEGATIVE)
    attn_probs = jax.nn.softmax(scores, axis=-1)
    attn_mixed = jnp.einsum('kgqt,tkd->qkgd', low(attn_probs), value_rows, precision=HIGHEST_PRECISION)
    attn_mixed = low_back(low(attn_mixed)).reshape(length, H * HD)
    middle = hidden + low_back(matmul(attn_mixed, proj_out))
    normed_mid = low(rms_norm(middle, gains[2 * layer_idx + 1]))
    gate_up = low_back(matmul(normed_mid, proj_gate))
    activated = low(gate_up[:, :FF] * jax.nn.sigmoid(gate_up[:, :FF]) * gate_up[:, FF:])
    return middle + low_back(matmul(activated, proj_down.T))

def sequence_loss(lowered, tokens, targets, prefix, positions):
    table = lowered[5]
    gains = lowered[4]
    places = jnp.arange(SEQ)
    allowed = (places[None, :] <= places[:, None]) | (places[None, :] < prefix)
    hidden = low_back(table[tokens])
    for layer_idx in range(LAYERS):
        hidden = layer_pass(hidden, lowered, layer_idx, places, allowed)
    final_rows = low(rms_norm(hidden, gains[2 * LAYERS]))
    logits = low_back(matmul(final_rows[positions], table.T))
    log_total = jax.nn.logsumexp(logits, axis=-1)
    target_logit = jnp.take_along_axis(logits, targets[positions][:, None], axis=-1)[:, 0]
    per_row = (1.0 - SMOOTH) * (log_total - target_logit) + SMOOTH * (log_total - lax.optimization_barrier(jnp.mean(logits, axis=-1))) + ZLOSS_WEIGHT * log_total * log_total
    counted = (positions >= prefix).astype(jnp.float32)
    return jnp.sum(per_row * counted)

def total_loss(proj_in, proj_out, proj_gate, proj_down, gains, table, tokens, targets, prefix, positions):
    lowered = (low(proj_in), low(proj_out), low(proj_gate), low(proj_down), gains, low(table))
    sequences = (tokens.reshape(MB * SEQS, SEQ), targets.reshape(MB * SEQS, SEQ), prefix.reshape(MB * SEQS), positions.reshape(MB * SEQS, PICKS))

    def one_sequence(running, sequence):
        return (running + jax.checkpoint(sequence_loss)(lowered, sequence[0], sequence[1], sequence[2], sequence[3]), None)
    loss_total, unused = lax.scan(one_sequence, jnp.zeros((), jnp.float32), sequences)
    return loss_total

def orthogonalize(matrix):
    current = matrix / (jnp.sqrt(jnp.sum(matrix * matrix)) + 1e-07)
    for ns_step in range(ITERS):
        gram_matrix = matmul(current, current.T)
        applied = matmul(gram_matrix, current)
        applied_twice = matmul(gram_matrix, applied)
        current = NS_A * current + NS_B * applied + NS_C * applied_twice
    return current

def adam_update(weight, first_moment, second_moment, gradient, step_rate, decay_rate):
    first_new = BETA_ONE * first_moment + (1.0 - BETA_ONE) * gradient
    second_new = BETA_TWO * second_moment + (1.0 - BETA_TWO) * gradient * gradient
    update = first_new / (1.0 - BETA_ONE ** STEP) / (jnp.sqrt(second_new / (1.0 - BETA_TWO ** STEP)) + ADAM_EPS)
    return (first_new, second_new, weight * (1.0 - step_rate * decay_rate) - step_rate * update)

def reference(token_ids, target_ids, prefix_lengths, loss_positions, w_input, w_output, w_gate_up, w_down, norm_gains, embed_table, moment_input, moment_output, moment_gate_up, moment_down, table_first, table_second, gains_first, gains_second):

    def objective(proj_in, proj_out, proj_gate, proj_down, gains, table):
        return total_loss(proj_in, proj_out, proj_gate, proj_down, gains, table, token_ids, target_ids, prefix_lengths, loss_positions)
    loss_sum, pull = jax.vjp(objective, w_input, w_output, w_gate_up, w_down, norm_gains, embed_table)
    gradients = pull(jnp.ones((), jnp.float32))
    token_count = jnp.sum((loss_positions >= prefix_lengths[:, :, None]).astype(jnp.float32))
    gradients = tuple((gradient / token_count for gradient in gradients))
    grad_norm = jnp.sqrt(sum((jnp.sum(gradient * gradient) for gradient in gradients)))
    clip_factor = jnp.minimum(1.0, CLIP_NORM / grad_norm)
    clipped = tuple((clip_factor * gradient for gradient in gradients))
    masters = (w_input, w_output, w_gate_up, w_down)
    moments = (moment_input, moment_output, moment_gate_up, moment_down)
    new_moments = []
    new_weights = []
    for kind_idx in range(4):
        moment_new = MOMENTUM * moments[kind_idx] + clipped[kind_idx]
        ortho = jnp.stack([orthogonalize(moment_new[layer_idx]) for layer_idx in range(LAYERS)])
        column_count = masters[kind_idx].shape[2]
        new_moments.append(moment_new)
        new_weights.append(masters[kind_idx] * (1.0 - MUON_RATE * WEIGHT_DECAY) - MUON_RATE * 0.2 * math.sqrt(column_count) * ortho)
    table_m, table_v, table_new = adam_update(embed_table, table_first, table_second, clipped[5], TABLE_RATE, WEIGHT_DECAY)
    gains_m, gains_v, gains_new = adam_update(norm_gains, gains_first, gains_second, clipped[4], GAIN_RATE, 0.0)
    return (loss_sum, token_count, grad_norm, new_moments[0], new_moments[1], new_moments[2], new_moments[3], new_weights[0], new_weights[1], new_weights[2], new_weights[3], new_weights[0].astype(jnp.bfloat16), new_weights[1].astype(jnp.bfloat16), new_weights[2].astype(jnp.bfloat16), new_weights[3].astype(jnp.bfloat16), table_m, table_v, table_new, table_new.astype(jnp.bfloat16), gains_m, gains_v, gains_new)
```

```python
import functools
import math

import jax
import jax.numpy as jnp
from jax import lax
from jax.experimental import pallas as pl
from jax.experimental.pallas import tpu as pltpu
from jax.sharding import PartitionSpec as P

D = 960
H = 15
KVH = 5
HD = 64
FF = 2560
V = 49152
QKV = 1600
ITERS = 5
STEP = 10
MB = 2
SEQ = 1024
ROWS = 128
PICK = 16
DP = 1024

NORM_EPS = 1e-05
ROPE_THETA = 100000.0
SMOOTH = 0.1
ZLOSS_WEIGHT = 0.0001
CLIP_NORM = 0.02
MOMENTUM = 0.95
NS_A = 3.4445
NS_B = -4.775
NS_C = 2.0315
MUON_RATE = 0.1
WEIGHT_DECAY = 0.1
BETA_ONE = 0.9
BETA_TWO = 0.95
TABLE_RATE = 0.03
GAIN_RATE = 0.4
ADAM_EPS = 1e-08
NEGATIVE = -1e30

HIGHEST = lax.Precision.HIGHEST
HIGH = lax.Precision.HIGH
F32 = jnp.float32
BF16 = jnp.bfloat16
MESH = pl.DeviceIdType.MESH
ANY = pl.BlockSpec(memory_space=pl.ANY)
VMEM = pl.BlockSpec(memory_space=pltpu.VMEM)

RI, RO, RG, RD = 112, 64, 320, 160


def my_place():
    wide = lax.axis_index("wide")
    narrow = lax.axis_index("narrow")
    return {
        "y": lax.div(wide, 2),
        "c": lax.rem(wide, 2),
        "z": lax.div(narrow, 4),
        "x": lax.rem(narrow, 4),
    }


def device(place):
    return (place["y"] * 2 + place["c"], place["z"] * 4 + place["x"])


def at_step(place, axis, step):
    return {**place, axis: lax.rem(place[axis] + step, 4)}


def other_core(place):
    return {**place, "c": 1 - place["c"]}


def greet(targets):
    barrier = pltpu.get_barrier_semaphore()
    for target in targets:
        pl.semaphore_signal(barrier, inc=1, device_id=device(target), device_id_type=MESH)
    pl.semaphore_wait(barrier, len(targets))


class Net:
    def __init__(self, send, recv):
        self.send = send
        self.recv = recv
        self.copies = []

    def put(self, src, dst, target):
        k = len(self.copies)
        copy = pltpu.make_async_remote_copy(
            src_ref=src,
            dst_ref=dst,
            send_sem=self.send.at[k],
            recv_sem=self.recv.at[k],
            device_id=device(target),
            device_id_type=MESH,
        )
        copy.start()
        self.copies.append(copy)
        return copy

    def finish(self):
        for copy in self.copies:
            copy.wait_send()


def gather_streams(net, place, streams, with_core):
    states = [{"sel": dict(place), "core": []} for _ in streams]
    phases = max(len(axes) for axes, _ in streams)
    for phase in range(phases):
        last = phase == phases - 1
        for (axes, items), state in zip(streams, states):
            axis = axes[phase]
            up, down = at_step(place, axis, 1), at_step(place, axis, 3)
            state["first"], state["second"] = [], []
            for first_half in (0, 1):
                for region, halves in items:
                    for target, half, way in ((up, first_half, 0), (down, 1 - first_half, 1)):
                        if halves[half] is None:
                            continue
                        ref = region(state["sel"], halves[half])
                        group = "first" if first_half == 0 else "second"
                        state[group].append((net.put(ref, ref, target), way, region, halves[half]))
            if last and with_core:
                for region, halves in items:
                    for half in halves:
                        if half is not None:
                            ref = region(state["sel"], half)
                            state["core"].append(net.put(ref, ref, other_core(place)))
        for (axes, items), state in zip(streams, states):
            axis = axes[phase]
            up, down = at_step(place, axis, 1), at_step(place, axis, 3)
            state["onward"] = []
            for copy, way, region, half in state["first"]:
                copy.wait_recv()
                origin, target = (down, up) if way == 0 else (up, down)
                ref = region({**state["sel"], axis: origin[axis]}, half)
                state["onward"].append((net.put(ref, ref, target), region, half))
                if last and with_core:
                    state["core"].append(net.put(ref, ref, other_core(place)))
        for (axes, items), state in zip(streams, states):
            axis = axes[phase]
            up, down = at_step(place, axis, 1), at_step(place, axis, 3)
            for copy, way, region, half in state["second"]:
                copy.wait_recv()
                if last and with_core:
                    origin = down if way == 0 else up
                    ref = region({**state["sel"], axis: origin[axis]}, half)
                    state["core"].append(net.put(ref, ref, other_core(place)))
        for (axes, items), state in zip(streams, states):
            axis = axes[phase]
            across = at_step(place, axis, 2)
            for copy, region, half in state["onward"]:
                copy.wait_recv()
                if last and with_core:
                    ref = region({**state["sel"], axis: across[axis]}, half)
                    state["core"].append(net.put(ref, ref, other_core(place)))
            state["sel"] = {**state["sel"], axis: None}
    for state in states:
        for copy in state["core"]:
            copy.wait_recv()


def pick(index):
    return slice(None) if index is None else index


def lanes_of(sel):
    if sel["y"] is None:
        return pl.ds(pl.multiple_of(sel["c"] * 512, 512), 512)
    return pl.ds(pl.multiple_of((sel["c"] * 4 + sel["y"]) * 128, 128), 128)


def halved(low, high):
    cut = low + (high - low) // 32 * 16
    return ((low, cut - low), (cut, high - cut))


def neighbours(place, axes=("x", "y", "z"), core=True):
    found = [at_step(place, axis, step) for axis in axes for step in (1, 3)]
    return found + ([other_core(place)] if core else [])


def weights_kernel(gi, go, gg, gd, meta, wi, wo, wg, wd, info, send, recv, local):
    place = my_place()
    greet(neighbours(place))

    def in_wi(sel, rows):
        return wi.at[pick(sel["z"]), pick(sel["x"]), pl.ds(*rows), lanes_of(sel)]

    def in_wo(sel, rows):
        z, x = sel["z"], sel["x"]
        xh, xl = (None, None) if x is None else (lax.div(x, 2), lax.rem(x, 2))
        return wo.at[pick(xh), pick(z), pick(xl), pl.ds(*rows), lanes_of(sel)]

    def in_wg(half):
        def region(sel, rows):
            z, x = sel["z"], sel["x"]
            zh, zl = (None, None) if z is None else (lax.div(z, 2), lax.rem(z, 2))
            return wg.at[pick(zh), half, pick(zl), pick(x), pl.ds(*rows), lanes_of(sel)]

        return region

    def in_wd(sel, rows):
        z, x = sel["z"], sel["x"]
        xh, xl = (None, None) if x is None else (lax.div(x, 2), lax.rem(x, 2))
        return wd.at[pick(xl), pick(z), pick(xh), pl.ds(*rows), lanes_of(sel)]

    def in_info(sel, rows):
        return info.at[pick(sel["z"]), pick(sel["x"]), pick(sel["y"]), sel["c"], :, :]

    owns = [
        (gi, in_wi(place, (0, RI))),
        (go, in_wo(place, (0, RO))),
        (gg.at[pl.ds(0, 160)], in_wg(0)(place, (0, 160))),
        (gg.at[pl.ds(160, 160)], in_wg(1)(place, (0, 160))),
        (gd, in_wd(place, (0, RD))),
        (meta, in_info(place, None)),
    ]
    copies = [pltpu.make_async_copy(src, dst, local.at[k]) for k, (src, dst) in enumerate(owns)]
    for copy in copies:
        copy.start()
    for copy in copies:
        copy.wait()
    streams = [
        (("x", "z", "y"), [(in_wg(0), halved(0, 160)), (in_wo, halved(0, 64))]),
        (("z", "y", "x"), [(in_wg(1), halved(0, 160)), (in_wi, halved(0, 64))]),
        (
            ("y", "x", "z"),
            [(in_wd, halved(0, 160)), (in_wi, halved(64, 112)), (in_info, ((0, 8), None))],
        ),
    ]
    net = Net(send, recv)
    gather_streams(net, place, streams, True)
    net.finish()


def gather_weights(gi, go, gg, gd, meta):
    shapes = [
        jax.ShapeDtypeStruct((4, 4, RI, DP), BF16),
        jax.ShapeDtypeStruct((2, 4, 2, RO, DP), BF16),
        jax.ShapeDtypeStruct((2, 2, 2, 4, 160, DP), BF16),
        jax.ShapeDtypeStruct((2, 4, 2, 160, DP), BF16),
        jax.ShapeDtypeStruct((4, 4, 4, 2, 8, 128), jnp.int32),
    ]
    count = 176
    return pl.pallas_call(
        weights_kernel,
        out_shape=shapes,
        in_specs=[ANY] * 5,
        out_specs=[ANY] * 5,
        scratch_shapes=[
            pltpu.SemaphoreType.DMA((count,)),
            pltpu.SemaphoreType.DMA((count,)),
            pltpu.SemaphoreType.DMA((6,)),
        ],
        compiler_params=pltpu.CompilerParams(collective_id=0, has_side_effects=True),
        name="gather_weights",
    )(gi, go, gg, gd, meta)


LANE_PARTS = ((0, 384), (384, 384), (768, 256))
ORDERS = (("x", "z", "y"), ("z", "y", "x"), ("y", "x", "z"))


def rows_kernel(own, rows, send, recv, local):
    place = my_place()
    greet(neighbours(place))

    def in_rows(lanes):
        def region(sel, part):
            return rows.at[
                pick(sel["z"]), pick(sel["x"]), pick(sel["y"]), sel["c"], pl.ds(*part), pl.ds(*lanes)
            ]

        return region

    copy = pltpu.make_async_copy(
        own, rows.at[place["z"], place["x"], place["y"], place["c"]], local
    )
    copy.start()
    copy.wait()
    streams = [
        (axes, [(in_rows(lanes), ((0, 16), (16, 16)))]) for axes, lanes in zip(ORDERS, LANE_PARTS)
    ]
    net = Net(send, recv)
    gather_streams(net, place, streams, True)
    net.finish()


def gather_rows(own):
    count = 90
    return pl.pallas_call(
        rows_kernel,
        out_shape=jax.ShapeDtypeStruct((4, 4, 4, 2, 32, DP), BF16),
        in_specs=[ANY],
        out_specs=ANY,
        scratch_shapes=[
            pltpu.SemaphoreType.DMA((count,)),
            pltpu.SemaphoreType.DMA((count,)),
            pltpu.SemaphoreType.DMA,
        ],
        compiler_params=pltpu.CompilerParams(collective_id=1, has_side_effects=True),
        name="gather_rows",
    )(own)


HOPS = (("c", 2), ("x", 4), ("y", 4), ("z", 4))


def small_kernel(combine, last, own, out, held, slots, send, recv):
    place = my_place()
    peers = [other_core(place)] + [
        at_step(place, axis, step) for axis, _ in HOPS[1:] for step in (1, 2, 3)
    ]
    greet(peers)
    held[0] = own[...]
    net = Net(send, recv)
    for hop, (axis, size) in enumerate(HOPS):
        targets = (
            [other_core(place)]
            if axis == "c"
            else [at_step(place, axis, step) for step in (1, 2, 3)]
        )
        copies = [net.put(held.at[hop], slots.at[hop, place[axis]], target) for target in targets]
        slots[hop, place[axis]] = held[hop]
        for copy in copies:
            copy.wait_recv()
        total = slots[hop, 0]
        for index in range(1, size):
            total = combine(total, slots[hop, index])
        held[hop + 1] = total
    out[...] = last(held[len(HOPS)])
    net.finish()


def small_all(value, combine, last, out_shape, collective_id, name):
    shape = value.shape
    count = 10
    return pl.pallas_call(
        functools.partial(small_kernel, combine, last),
        out_shape=jax.ShapeDtypeStruct(out_shape, F32),
        in_specs=[VMEM],
        out_specs=VMEM,
        scratch_shapes=[
            pltpu.VMEM((len(HOPS) + 1,) + shape, F32),
            pltpu.VMEM((len(HOPS), 4) + shape, F32),
            pltpu.SemaphoreType.DMA((count,)),
            pltpu.SemaphoreType.DMA((count,)),
        ],
        compiler_params=pltpu.CompilerParams(collective_id=collective_id, has_side_effects=True),
        name=name,
    )(value)


def combine_stats(one, two):
    highest = jnp.maximum(one[0], two[0])
    total = one[1] * jnp.exp(one[0] - highest) + two[1] * jnp.exp(two[0] - highest)
    return jnp.stack([highest, total])


def log_of_stats(stats):
    return stats[0] + jnp.log(stats[1])


def add_up(dst, index, parts):
    total = parts[0][...].astype(F32)
    for part in parts[1:]:
        total = total + part[...].astype(F32)
    dst[index] = total.astype(dst.dtype)


def scatter_sum(net, place, orders, sources, works, outs):
    def block(ref, sel, rows):
        return ref.at[pick(sel["z"]), pick(sel["x"]), pick(sel["y"]), pl.ds(*rows)]

    jobs = []
    for order, source, work, out in zip(orders, sources, works, outs):
        rows = source.shape[3] // 2
        jobs.append(
            {
                "order": order,
                "source": source,
                "work": work,
                "out": out,
                "halves": ((0, rows), (rows, rows)),
                "steps": [
                    [at_step(place, axis, step) for step in range(4)] for axis in order
                ],
            }
        )

    def everywhere():
        return {"z": None, "x": None, "y": None}

    def first_view(job, one, two, half):
        a, b, _ = job["order"]
        sel = {**everywhere(), a: one, b: two}
        return block(job["source"], sel, job["halves"][half])

    sequence = (2, 1, 3, 0)
    for sub, far in enumerate(sequence):
        for job in jobs:
            a, b, _ = job["order"]
            own = job["steps"][0]
            two = job["steps"][1][far][b]
            got = job["work"]["got1"]
            job.setdefault("c1", []).append(
                {
                    "ra": net.put(first_view(job, own[2][a], two, 0), got.at[sub, 0], own[1]),
                    "rb": net.put(first_view(job, own[2][a], two, 1), got.at[sub, 1], own[3]),
                }
            )
    for sub, far in enumerate(sequence):
        for job in jobs:
            a, b, _ = job["order"]
            own = job["steps"][0]
            two = job["steps"][1][far][b]
            got = job["work"]["got1"]
            copies = job["c1"][sub]
            copies["p1"] = net.put(first_view(job, own[1][a], two, 1), got.at[sub, 2], own[1])
            copies["m0"] = net.put(first_view(job, own[3][a], two, 0), got.at[sub, 3], own[3])
    for sub, far in enumerate(sequence):
        for job in jobs:
            a, b, _ = job["order"]
            own = job["steps"][0]
            two = job["steps"][1][far][b]
            got, mid = job["work"]["got1"], job["work"]["mid1"]
            copies = job["c1"][sub]
            copies["ra"].wait_recv()
            add_up(mid, (sub, 0), [first_view(job, own[1][a], two, 0), got.at[sub, 0]])
            copies["p0"] = net.put(mid.at[sub, 0], got.at[sub, 4], own[1])
            copies["rb"].wait_recv()
            add_up(mid, (sub, 1), [first_view(job, own[3][a], two, 1), got.at[sub, 1]])
            copies["m1"] = net.put(mid.at[sub, 1], got.at[sub, 5], own[3])
    def second_view(job, two, half):
        return job["work"]["acc1"].at[two, :, pl.ds(*job["halves"][half])]

    for sub, far in enumerate(sequence):
        for job in jobs:
            a, b, _ = job["order"]
            own = job["steps"][0]
            next_own = job["steps"][1]
            two = next_own[far][b]
            got = job["work"]["got1"]
            copies = job["c1"][sub]
            for name in ("p1", "m0", "p0", "m1"):
                copies[name].wait_recv()
            acc = job["work"]["acc1"]
            for half, (one, other) in enumerate(((4, 3), (2, 5))):
                add_up(
                    acc,
                    (two, slice(None), pl.ds(*job["halves"][half])),
                    [first_view(job, own[0][a], two, half), got.at[sub, one], got.at[sub, other]],
                )
            got2 = job["work"]["got2"]
            if far == 2:
                job["c2"] = {
                    "ra": net.put(second_view(job, two, 0), got2.at[0], next_own[1]),
                    "rb": net.put(second_view(job, two, 1), got2.at[1], next_own[3]),
                }
            if far == 1:
                job["c2"]["p1"] = net.put(second_view(job, two, 1), got2.at[2], next_own[1])
            if far == 3:
                job["c2"]["m0"] = net.put(second_view(job, two, 0), got2.at[3], next_own[3])
    for job in jobs:
        b = job["order"][1]
        own = job["steps"][1]
        got, mid, copies = job["work"]["got2"], job["work"]["mid2"], job["c2"]
        copies["ra"].wait_recv()
        add_up(mid, 0, [second_view(job, own[1][b], 0), got.at[0]])
        copies["p0"] = net.put(mid.at[0], got.at[4], own[1])
        copies["rb"].wait_recv()
        add_up(mid, 1, [second_view(job, own[3][b], 1), got.at[1]])
        copies["m1"] = net.put(mid.at[1], got.at[5], own[3])

    def third_view(job, three, half):
        return job["work"]["acc2"].at[three, pl.ds(*job["halves"][half])]

    for job in jobs:
        b = job["order"][1]
        own = job["steps"][1]
        got, acc, copies = job["work"]["got2"], job["work"]["acc2"], job["c2"]
        for name in ("p1", "m0", "p0", "m1"):
            copies[name].wait_recv()
        for half, (one, other) in enumerate(((4, 3), (2, 5))):
            add_up(
                acc,
                (slice(None), pl.ds(*job["halves"][half])),
                [second_view(job, own[0][b], half), got.at[one], got.at[other]],
            )
        third = job["order"][2]
        own = job["steps"][2]
        got = job["work"]["got3"]
        job["c3"] = {
            "ra": net.put(third_view(job, own[2][third], 0), got.at[0], own[1]),
            "rb": net.put(third_view(job, own[2][third], 1), got.at[1], own[3]),
            "p1": net.put(third_view(job, own[1][third], 1), got.at[2], own[1]),
            "m0": net.put(third_view(job, own[3][third], 0), got.at[3], own[3]),
        }
    for job in jobs:
        third = job["order"][2]
        own = job["steps"][2]
        got, mid, copies = job["work"]["got3"], job["work"]["mid3"], job["c3"]
        copies["ra"].wait_recv()
        add_up(mid, 0, [third_view(job, own[1][third], 0), got.at[0]])
        copies["p0"] = net.put(mid.at[0], got.at[4], own[1])
        copies["rb"].wait_recv()
        add_up(mid, 1, [third_view(job, own[3][third], 1), got.at[1]])
        copies["m1"] = net.put(mid.at[1], got.at[5], own[3])
    for job in jobs:
        third = job["order"][2]
        own = job["steps"][2]
        got, copies = job["work"]["got3"], job["c3"]
        for name in ("p1", "m0", "p0", "m1"):
            copies[name].wait_recv()
        for half, (one, other) in enumerate(((4, 3), (2, 5))):
            add_up(
                job["out"],
                (pl.ds(*job["halves"][half]),),
                [third_view(job, own[0][third], half), got.at[one], got.at[other]],
            )


WORK_NAMES = ("got1", "mid1", "acc1", "got2", "mid2", "acc2", "got3", "mid3")


def work_shapes(rows, lanes, first, later):
    half = rows // 2
    return [
        pltpu.VMEM((4, 6, 4, half, lanes), first),
        pltpu.VMEM((4, 2, 4, half, lanes), first),
        pltpu.VMEM((4, 4, rows, lanes), later),
        pltpu.VMEM((6, 4, half, lanes), later),
        pltpu.VMEM((2, 4, half, lanes), later),
        pltpu.VMEM((4, rows, lanes), later),
        pltpu.VMEM((6, half, lanes), later),
        pltpu.VMEM((2, half, lanes), later),
    ]


SUM_COPIES = 3 * (24 + 6 + 6)


def grads_kernel(di, do, dg, dd, out, *scratch):
    held = scratch[0:3]
    works = [dict(zip(WORK_NAMES, scratch[3 + 8 * k : 11 + 8 * k])) for k in range(3)]
    send, recv, local = scratch[27:]
    place = my_place()
    moves = []
    for y in range(4):
        lanes = pl.ds(y * 128, 128)
        for z in range(4):
            for half in range(2):
                moves.append(
                    (
                        dg.at[z // 2, half, z % 2, :, :, lanes],
                        held[half].at[z, :, y, pl.ds(0, 160)],
                    )
                )
        for x in range(4):
            moves.append((dd.at[x % 2, :, x // 2, :, lanes], held[2].at[:, x, y, pl.ds(0, 160)]))
            moves.append((do.at[x // 2, :, x % 2, :, lanes], held[0].at[:, x, y, pl.ds(160, 64)]))
        for z in range(4):
            moves.append(
                (di.at[z, :, pl.ds(0, 64), lanes], held[1].at[z, :, y, pl.ds(160, 64)])
            )
            moves.append(
                (di.at[z, :, pl.ds(64, 48), lanes], held[2].at[z, :, y, pl.ds(160, 48)])
            )
    copies = [pltpu.make_async_copy(src, dst, local.at[k]) for k, (src, dst) in enumerate(moves)]
    for copy in copies:
        copy.start()
    held[2][:, :, :, 208:224, :] = jnp.zeros((4, 4, 4, 16, 128), held[2].dtype)
    greet(neighbours(place, core=False))
    for copy in copies:
        copy.wait()
    net = Net(send, recv)
    scatter_sum(net, place, ORDERS, held, works, [out.at[k] for k in range(3)])
    net.finish()


def scatter_grads(di, do, dg, dd, first, later):
    rows, lanes = 224, 128
    scratch = [pltpu.VMEM((4, 4, 4, rows, lanes), first)] * 3
    for _ in range(3):
        scratch += work_shapes(rows, lanes, first, later)
    scratch += [
        pltpu.SemaphoreType.DMA((SUM_COPIES,)),
        pltpu.SemaphoreType.DMA((SUM_COPIES,)),
        pltpu.SemaphoreType.DMA((96,)),
    ]
    return pl.pallas_call(
        grads_kernel,
        out_shape=jax.ShapeDtypeStruct((3, rows, lanes), F32),
        in_specs=[ANY] * 4,
        out_specs=VMEM,
        scratch_shapes=scratch,
        compiler_params=pltpu.CompilerParams(
            collective_id=2, has_side_effects=True, vmem_limit_bytes=56 << 20
        ),
        name="scatter_grads",
    )(di, do, dg, dd)


def row_sums_kernel(part, out, *scratch):
    held = scratch[0:3]
    works = [dict(zip(WORK_NAMES, scratch[3 + 8 * k : 11 + 8 * k])) for k in range(3)]
    send, recv, local = scratch[27:]
    place = my_place()
    copies = [
        pltpu.make_async_copy(part.at[:, :, :, :, pl.ds(*lanes)], held[k], local.at[k])
        for k, lanes in enumerate(LANE_PARTS)
    ]
    for copy in copies:
        copy.start()
    greet(neighbours(place, core=False))
    for copy in copies:
        copy.wait()
    net = Net(send, recv)
    outs = [out.at[:, pl.ds(*lanes)] for lanes in LANE_PARTS]
    scatter_sum(net, place, ORDERS, held, works, outs)
    net.finish()


def scatter_rows(part, first, later):
    scratch = [pltpu.VMEM((4, 4, 4, 32, lanes), first) for _, lanes in LANE_PARTS]
    for _, lanes in LANE_PARTS:
        scratch += work_shapes(32, lanes, first, later)
    scratch += [
        pltpu.SemaphoreType.DMA((SUM_COPIES,)),
        pltpu.SemaphoreType.DMA((SUM_COPIES,)),
        pltpu.SemaphoreType.DMA((3,)),
    ]
    return pl.pallas_call(
        row_sums_kernel,
        out_shape=jax.ShapeDtypeStruct((32, DP), F32),
        in_specs=[ANY],
        out_specs=VMEM,
        scratch_shapes=scratch,
        compiler_params=pltpu.CompilerParams(
            collective_id=3, has_side_effects=True, vmem_limit_bytes=56 << 20
        ),
        name="scatter_rows",
    )(part)


def pad_features(values):
    lead = values.shape[:-1]
    blocks = values.reshape(lead + (4, 2, 2, 60))
    blocks = jnp.moveaxis(blocks, -3, -4)
    blocks = jnp.pad(blocks, [(0, 0)] * (len(lead) + 3) + [(0, 4)])
    return blocks.reshape(lead + (DP,))


def feature_table():
    feature = lax.broadcasted_iota(jnp.int32, (D, DP), 0)
    place = lax.broadcasted_iota(jnp.int32, (D, DP), 1)
    wide, rest = feature // 120, feature % 120
    where = ((wide % 2) * 4 + wide // 2) * 128 + (rest // 60) * 64 + rest % 60
    return (where == place).astype(BF16)


def column_table():
    column = lax.broadcasted_iota(jnp.int32, (QKV, 16 * RI), 0)
    place = lax.broadcasted_iota(jnp.int32, (QKV, 16 * RI), 1)
    return ((column // 100) * RI + column % 100 == place).astype(BF16)


def to_shard(matrix, rows):
    columns = matrix.shape[1]
    turned = matrix.T.reshape(columns, 2, 60)
    turned = jnp.pad(turned, ((0, rows - columns), (0, 0), (0, 4)))
    return turned.reshape(rows, 128)


def from_shard(shard, columns):
    return shard[:columns].reshape(columns, 2, 64)[:, :, :60].reshape(columns, 120).T


def dot(left, right, left_axis, right_axis, precision=None):
    return lax.dot_general(
        left,
        right,
        (((left_axis,), (right_axis,)), ((), ())),
        preferred_element_type=F32,
        precision=precision,
    )


def rms_norm(values, gain_row):
    mean = jnp.sum(values * values, axis=-1, keepdims=True) * (1.0 / D)
    return values * lax.rsqrt(mean + NORM_EPS) * gain_row


def rotate(values, places):
    half_width = HD // 2
    frequency = ROPE_THETA ** (-2.0 * jnp.arange(half_width).astype(F32) / HD)
    angles = places.astype(F32)[:, None] * frequency[None, :]
    cosine = jnp.concatenate([jnp.cos(angles), jnp.cos(angles)], axis=-1)[:, None, :]
    sine_part = jnp.concatenate([jnp.sin(angles), jnp.sin(angles)], axis=-1)[:, None, :]
    turned = jnp.concatenate([-values[..., half_width:], values[..., :half_width]], axis=-1)
    return values * cosine + turned * sine_part


def gated(gate_up):
    return gate_up[:, :FF] * jax.nn.sigmoid(gate_up[:, :FF]) * gate_up[:, FF:]


def adam_update(weight, first_moment, second_moment, gradient, step_rate, decay_rate):
    first_new = BETA_ONE * first_moment + (1.0 - BETA_ONE) * gradient
    second_new = BETA_TWO * second_moment + (1.0 - BETA_TWO) * gradient * gradient
    update = (
        first_new
        / (1.0 - BETA_ONE**STEP)
        / (jnp.sqrt(second_new / (1.0 - BETA_TWO**STEP)) + ADAM_EPS)
    )
    return (first_new, second_new, weight * (1.0 - step_rate * decay_rate) - step_rate * update)


def partner(value):
    return lax.ppermute(value, "wide", [(k, k ^ 1) for k in range(8)])


def body(
    token_ids,
    target_ids,
    prefix_lengths,
    loss_positions,
    w_input,
    w_output,
    w_gate_up,
    w_down,
    norm_gains,
    embed_table,
    moment_input,
    moment_output,
    moment_gate_up,
    moment_down,
    table_first,
    table_second,
    gains_first,
    gains_second,
):
    wide = lax.axis_index("wide")
    narrow = lax.axis_index("narrow")
    core = wide % 2
    masters = (w_input[0], w_output[0], w_gate_up[0], w_down[0])
    moments = (moment_input[0], moment_output[0], moment_gate_up[0], moment_down[0])
    group_size = H // KVH
    kv_width = KVH * HD
    scale_factor = HD ** (-0.5)
    features = feature_table()
    columns = column_table()
    gains = pad_features(norm_gains)
    own_places = wide * ROWS + jnp.arange(ROWS)
    key_places = jnp.arange(SEQ)
    tokens = token_ids[:, 0]
    targets = target_ids[:, 0]
    prefixes = prefix_lengths[:, 0]
    positions = loss_positions[:, 0]

    own_positions = lax.dynamic_slice_in_dim(positions, wide * PICK, PICK, axis=1)
    own_targets = jnp.take_along_axis(targets, own_positions, axis=1).reshape(MB * PICK)
    own_counted = (own_positions >= prefixes[:, None]).astype(jnp.int32).reshape(MB * PICK)
    meta = jnp.pad(jnp.stack([own_targets, own_counted]), ((0, 6), (0, 128 - MB * PICK)))

    table_low = dot(embed_table.astype(BF16), features, 1, 0).astype(BF16)
    slab = lax.all_gather(table_low, "narrow", axis=0, tiled=True)
    table_other = partner(table_low)

    shards = [
        to_shard(master.astype(BF16), rows) for master, rows in zip(masters, (RI, RO, RG, RD))
    ]
    wi, wo, wg, wd, info = gather_weights(*shards, meta)
    wi = wi.reshape(16, RI, DP)[:, :100].reshape(QKV, DP)
    wo = wo.reshape(DP, DP)
    wg = wg.reshape(2 * FF, DP)
    wd = wd.reshape(FF, DP)
    info = info.reshape(128, 8, 128)
    all_targets = info[:, 0, : MB * PICK].reshape(4096)
    all_counted = info[:, 1, : MB * PICK].reshape(4096).astype(F32)

    slab_rows = slab.shape[0]
    ordered = tokens.reshape(MB, 8, ROWS).swapaxes(0, 1).reshape(2048)
    local_ids = ordered - wide * slab_rows
    inside = (local_ids >= 0) & (local_ids < slab_rows)
    safe_ids = jnp.clip(local_ids, 0, slab_rows - 1)
    looked_up = jnp.where(inside[:, None], slab[safe_ids], jnp.zeros((), BF16))
    x0 = lax.psum_scatter(looked_up, "wide", scatter_dimension=0, tiled=True).astype(F32)

    a = rms_norm(x0, gains[0]).astype(BF16)
    projected = dot(a, wi, 1, 1)
    places_all = jnp.concatenate([own_places, own_places])
    rows_count = MB * ROWS
    query = rotate(projected[:, : H * HD].reshape(rows_count, H, HD), places_all).astype(BF16)
    key_own = rotate(
        projected[:, H * HD : H * HD + kv_width].reshape(rows_count, KVH, HD), places_all
    ).astype(BF16)
    value_own = projected[:, H * HD + kv_width :].astype(BF16)
    kv_own = jnp.concatenate([key_own.reshape(rows_count, kv_width), value_own], axis=1)
    kv_all = lax.all_gather(kv_own, "wide", axis=0, tiled=False)
    kv_all = kv_all.reshape(8, MB, ROWS, 2 * kv_width)

    def allowed_of(batch):
        return (key_places[None, :] <= own_places[:, None]) | (
            key_places[None, :] < prefixes[batch]
        )

    kept = []
    mixed_parts = []
    for batch in range(MB):
        q = query.reshape(MB, ROWS, KVH, group_size, HD)[batch]
        k = kv_all[:, batch, :, :kv_width].reshape(SEQ, KVH, HD)
        v = kv_all[:, batch, :, kv_width:].reshape(SEQ, KVH, HD)
        scores = jnp.einsum("qkgd,tkd->kgqt", q, k, preferred_element_type=F32) * scale_factor
        scores = jnp.where(allowed_of(batch), scores, NEGATIVE)
        highest = jnp.max(scores, axis=-1, keepdims=True)
        exp_part = jnp.exp(scores - highest)
        exp_total = jnp.sum(exp_part, axis=-1, keepdims=True)
        log_total = highest + jnp.log(exp_total)
        probs = (exp_part / exp_total).astype(BF16)
        mixed = jnp.einsum("kgqt,tkd->qkgd", probs, v, preferred_element_type=F32)
        mixed_parts.append(mixed.reshape(ROWS, H * HD).astype(BF16))
        kept.append((q, k, v, log_total))
    o_pad = dot(jnp.concatenate(mixed_parts), features, 1, 0).astype(BF16)
    x1 = x0 + dot(o_pad, wo, 1, 1)

    b = rms_norm(x1, gains[1]).astype(BF16)
    gate_up = dot(b, wg, 1, 1)
    activated = gated(gate_up).astype(BF16)
    x2 = x1 + dot(activated, wd, 1, 0)

    final = rms_norm(x2, gains[2]).astype(BF16)
    own_offsets = (own_positions - wide * ROWS + jnp.arange(MB)[:, None] * ROWS).reshape(-1)
    all_rows = gather_rows(final[own_offsets]).reshape(4096, DP)
    logits = dot(all_rows, table_low, 1, 1)
    vocab_start = (wide * 16 + narrow) * 384
    hit = jnp.arange(384)[None, :] == (all_targets - vocab_start)[:, None]
    highest = jnp.max(logits, axis=-1)
    exp_total = jnp.sum(jnp.exp(logits - highest[:, None]), axis=-1)
    stats = jnp.stack([highest.reshape(32, 128), exp_total.reshape(32, 128)])
    log_total = small_all(stats, combine_stats, log_of_stats, (32, 128), 4, "row_totals")
    log_total = log_total.reshape(4096)
    hit_sum = jnp.sum(jnp.where(hit, logits, 0.0) * all_counted[:, None])
    logit_sum = jnp.sum(logits * all_counted[:, None])
    token_count = jnp.sum(all_counted)
    loss_known = jnp.sum(all_counted * (log_total + ZLOSS_WEIGHT * log_total * log_total))
    d_logits = (
        all_counted[:, None]
        * (
            (1.0 + 2.0 * ZLOSS_WEIGHT * log_total)[:, None] * jnp.exp(logits - log_total[:, None])
            - (1.0 - SMOOTH) * hit.astype(F32)
            - SMOOTH / V
        )
    ).astype(BF16)
    table_grad_rows = dot(d_logits, all_rows, 0, 0)
    d_by_core = d_logits.reshape(64, 2, 32, 384)
    d_mine = lax.dynamic_index_in_dim(d_by_core, core, 1, keepdims=False).reshape(2048, 384)
    d_theirs = lax.dynamic_index_in_dim(d_by_core, 1 - core, 1, keepdims=False).reshape(2048, 384)
    d_theirs = partner(d_theirs)
    row_part = dot(d_mine, table_low, 1, 0) + dot(d_theirs, table_other, 1, 0)
    d_rows = scatter_rows(row_part.reshape(4, 4, 4, 32, DP), F32, F32)

    d_final = jnp.zeros((rows_count, DP), F32).at[own_offsets].add(d_rows)
    d_x2, d_gain_final = jax.vjp(rms_norm, x2, gains[2])[1](d_final)
    d_branch = d_x2.astype(BF16)
    d_activated = dot(d_branch, wd, 1, 1)
    d_gate_up = jax.vjp(gated, gate_up)[1](d_activated)[0].astype(BF16)
    d_b = dot(d_gate_up, wg, 1, 0)
    d_x1_part, d_gain_mlp = jax.vjp(rms_norm, x1, gains[1])[1](d_b)
    d_x1 = d_x2 + d_x1_part
    d_out = d_x1.astype(BF16)
    d_mixed_pad = dot(d_out, wo, 1, 0).astype(BF16)
    d_mixed = dot(d_mixed_pad, features, 1, 1).astype(BF16)
    d_queries, d_kv = [], []
    for batch in range(MB):
        q, k, v, log_sum = kept[batch]
        d_m = d_mixed.reshape(MB, ROWS, KVH, group_size, HD)[batch]
        scores = jnp.einsum("qkgd,tkd->kgqt", q, k, preferred_element_type=F32) * scale_factor
        scores = jnp.where(allowed_of(batch), scores, NEGATIVE)
        probs = jnp.exp(scores - log_sum)
        d_probs = jnp.einsum("qkgd,tkd->kgqt", d_m, v, preferred_element_type=F32)
        d_scores = (
            probs * (d_probs - jnp.sum(probs * d_probs, axis=-1, keepdims=True))
        ).astype(BF16)
        d_q = jnp.einsum("kgqt,tkd->qkgd", d_scores, k, preferred_element_type=F32) * scale_factor
        d_k = jnp.einsum("kgqt,qkgd->tkd", d_scores, q, preferred_element_type=F32) * scale_factor
        d_v = jnp.einsum(
            "kgqt,qkgd->tkd", probs.astype(BF16), d_m, preferred_element_type=F32
        )
        d_queries.append(d_q.reshape(ROWS, H, HD))
        d_kv.append(
            jnp.concatenate(
                [d_k.reshape(8, ROWS, kv_width), d_v.reshape(8, ROWS, kv_width)], axis=2
            )
        )
    d_kv_all = jnp.stack(d_kv, axis=1).reshape(8 * rows_count, 2 * kv_width)
    d_kv_own = lax.psum_scatter(d_kv_all, "wide", scatter_dimension=0, tiled=True)

    def unrotate(gradient, heads):
        primal = jnp.zeros((rows_count, heads, HD), F32)
        return jax.vjp(lambda values: rotate(values, places_all), primal)[1](gradient)[0]

    d_projected = jnp.concatenate(
        [
            unrotate(jnp.concatenate(d_queries), H).reshape(rows_count, H * HD),
            unrotate(d_kv_own[:, :kv_width].reshape(rows_count, KVH, HD), KVH).reshape(
                rows_count, kv_width
            ),
            d_kv_own[:, kv_width:],
        ],
        axis=1,
    ).astype(BF16)
    d_a = dot(d_projected, wi, 1, 0)
    d_x0_part, d_gain_attn = jax.vjp(rms_norm, x0, gains[0])[1](d_a)
    d_x0 = (d_x1 + d_x0_part).astype(BF16)

    def half_pair(value):
        mine = lax.dynamic_slice_in_dim(value, core * 512, 512, axis=1)
        theirs = lax.dynamic_slice_in_dim(value, (1 - core) * 512, 512, axis=1)
        return jnp.concatenate([mine, partner(theirs)])

    def both(value):
        return jnp.concatenate([value, partner(value)])

    d_projected_pad = dot(d_projected, columns, 1, 0).astype(BF16)
    grad_wd = dot(both(activated), half_pair(d_branch), 0, 0).astype(BF16)
    grad_wg = dot(both(d_gate_up), half_pair(b), 0, 0).astype(BF16)
    grad_wo = dot(both(d_out), half_pair(o_pad), 0, 0).astype(BF16)
    grad_wi = dot(both(d_projected_pad), half_pair(a), 0, 0).astype(BF16)
    summed_grads = scatter_grads(
        grad_wi.reshape(4, 4, RI, 512),
        grad_wo.reshape(2, 4, 2, RO, 512),
        grad_wg.reshape(2, 2, 2, 4, 160, 512),
        grad_wd.reshape(2, 4, 2, 160, 512),
        BF16,
        F32,
    )
    grad_shards = (
        jnp.concatenate([summed_grads[1, 160:224], summed_grads[2, 160:208]]),
        summed_grads[0, 160:224],
        jnp.concatenate([summed_grads[0, :160], summed_grads[1, :160]]),
        summed_grads[2, :160],
    )

    d_embed = lax.all_gather(d_x0, "wide", axis=0, tiled=True)
    onehot = (
        lax.broadcasted_iota(jnp.int32, (slab_rows, 2048), 0) == local_ids[None, :]
    ).astype(BF16)
    table_grad = lax.psum_scatter(
        dot(onehot, d_embed, 1, 0), "narrow", scatter_dimension=0, tiled=True
    )
    table_grad = dot(table_grad + table_grad_rows, features, 1, 1, HIGHEST)

    squares = sum(jnp.sum(shard * shard) for shard in grad_shards) + jnp.sum(
        table_grad * table_grad
    )
    gain_grads = jnp.stack([d_gain_attn, d_gain_mlp, d_gain_final]).reshape(24, 128)
    scalars = jnp.pad(jnp.stack([squares, hit_sum, logit_sum]), (0, 125))
    packed = jnp.pad(jnp.concatenate([gain_grads, scalars[None]]), ((0, 7), (0, 0)))
    summed = small_all(packed, jnp.add, lambda v: v, (32, 128), 5, "global_sums")
    gain_grad = dot(summed[:24].reshape(3, DP), features, 1, 1, HIGHEST)
    loss_total = loss_known - (1.0 - SMOOTH) * summed[24, 1] - SMOOTH / V * summed[24, 2]
    grad_norm = jnp.sqrt(summed[24, 0] + jnp.sum(gain_grad * gain_grad)) / token_count
    factor = jnp.minimum(1.0, CLIP_NORM / grad_norm) / token_count

    new_shards = [
        MOMENTUM * to_shard(moment, rows) + factor * grad
        for moment, rows, grad in zip(moments, (RI, RO, RG, RD), grad_shards)
    ]
    pieces = jnp.stack(
        [
            jnp.pad(part, ((0, 160 - part.shape[0]), (0, 0)))
            for shard in new_shards
            for part in jnp.split(shard, 2)
        ]
    )
    pieces = lax.all_to_all(pieces, "wide", split_axis=0, concat_axis=0)
    turned = pieces.reshape(4, 2, 160, 128).transpose(2, 1, 0, 3).reshape(160, DP)
    gram = dot(turned, turned, 0, 0, HIGHEST)
    gram = lax.psum(gram + partner(gram), "narrow")
    norm = jnp.sqrt(jnp.trace(gram)) + 1e-07
    current = turned / norm
    gram = gram / norm / norm
    identity = jnp.eye(DP, dtype=F32)
    for ns_step in range(ITERS):
        if ns_step < ITERS - 1:
            square = dot(gram, gram, 1, 0, HIGH)
            step_matrix = NS_A * identity + NS_B * gram + NS_C * square
            current = dot(current, step_matrix, 1, 0, HIGH)
            gram = dot(dot(step_matrix, gram, 1, 0, HIGH), step_matrix, 1, 0, HIGH)
        else:
            applied = dot(current, gram, 1, 0, HIGH)
            current = NS_A * current + NS_B * applied + NS_C * dot(applied, gram, 1, 0, HIGH)
    pieces = current.reshape(160, 2, 4, 128).transpose(2, 1, 0, 3).reshape(8, 160, 128)
    pieces = lax.all_to_all(pieces, "wide", split_axis=0, concat_axis=0)
    new_moments, new_weights = [], []
    for kind, rows in enumerate((RI, RO, RG, RD)):
        count = masters[kind].shape[1]
        ortho = jnp.concatenate([pieces[2 * kind, : rows // 2], pieces[2 * kind + 1, : rows // 2]])
        new_moments.append(from_shard(new_shards[kind], count)[None])
        new_weights.append(
            (
                masters[kind] * (1.0 - MUON_RATE * WEIGHT_DECAY)
                - MUON_RATE * 0.2 * math.sqrt(count * 16) * from_shard(ortho, count)
            )[None]
        )
    table_m, table_v, table_new = adam_update(
        embed_table, table_first, table_second, factor * table_grad, TABLE_RATE, WEIGHT_DECAY
    )
    gains_m, gains_v, gains_new = adam_update(
        norm_gains, gains_first, gains_second, factor * gain_grad, GAIN_RATE, 0.0
    )
    return (
        loss_total,
        token_count,
        grad_norm,
        *new_moments,
        *new_weights,
        *[weight.astype(BF16) for weight in new_weights],
        table_m,
        table_v,
        table_new,
        table_new.astype(BF16),
        gains_m,
        gains_v,
        gains_new,
    )


def solution(mesh):
    whole = P()
    by_sequence = P(None, "narrow", None)
    matrix = P(None, "wide", "narrow")
    table = P(("wide", "narrow"), None)
    return jax.shard_map(
        body,
        mesh=mesh,
        in_specs=(
            (by_sequence, by_sequence, P(None, "narrow"), by_sequence)
            + (matrix,) * 4
            + (whole, table)
            + (matrix,) * 4
            + (table, table, whole, whole)
        ),
        out_specs=(whole,) * 3 + (matrix,) * 12 + (table,) * 4 + (whole,) * 3,
        check_vma=False,
    )
```

```python
import functools
import math

import jax
import jax.numpy as jnp
from jax import lax
from jax.experimental import pallas as pl
from jax.experimental.pallas import tpu as pltpu
from jax.sharding import PartitionSpec as P

D = 960
H = 15
KVH = 5
HD = 64
FF = 2560
V = 49152
QKV = 1600
ITERS = 5
STEP = 10
MB = 2
SEQ = 1024
ROWS = 128
PICK = 16
DP = 1024

NORM_EPS = 1e-05
ROPE_THETA = 100000.0
SMOOTH = 0.1
ZLOSS_WEIGHT = 0.0001
CLIP_NORM = 0.02
MOMENTUM = 0.95
NS_A = 3.4445
NS_B = -4.775
NS_C = 2.0315
MUON_RATE = 0.1
WEIGHT_DECAY = 0.1
BETA_ONE = 0.9
BETA_TWO = 0.95
TABLE_RATE = 0.03
GAIN_RATE = 0.4
ADAM_EPS = 1e-08
NEGATIVE = -1e30

HIGHEST = lax.Precision.HIGHEST
HIGH = lax.Precision.HIGH
F32 = jnp.float32
BF16 = jnp.bfloat16
MESH = pl.DeviceIdType.MESH
ANY = pl.BlockSpec(memory_space=pl.ANY)
VMEM = pl.BlockSpec(memory_space=pltpu.VMEM)

RI, RO, RG, RD = 112, 64, 320, 160


def my_place():
    wide = lax.axis_index("wide")
    narrow = lax.axis_index("narrow")
    return {
        "y": lax.div(wide, 2),
        "c": lax.rem(wide, 2),
        "z": lax.div(narrow, 4),
        "x": lax.rem(narrow, 4),
    }


def device(place):
    return (place["y"] * 2 + place["c"], place["z"] * 4 + place["x"])


def at_step(place, axis, step):
    return {**place, axis: lax.rem(place[axis] + step, 4)}


def other_core(place):
    return {**place, "c": 1 - place["c"]}


def greet(targets):
    barrier = pltpu.get_barrier_semaphore()
    for target in targets:
        pl.semaphore_signal(barrier, inc=1, device_id=device(target), device_id_type=MESH)
    pl.semaphore_wait(barrier, len(targets))


class Net:
    def __init__(self, send, recv):
        self.send = send
        self.recv = recv
        self.copies = []

    def put(self, src, dst, target):
        k = len(self.copies)
        copy = pltpu.make_async_remote_copy(
            src_ref=src,
            dst_ref=dst,
            send_sem=self.send.at[k],
            recv_sem=self.recv.at[k],
            device_id=device(target),
            device_id_type=MESH,
        )
        copy.start()
        self.copies.append(copy)
        return copy

    def finish(self):
        for copy in self.copies:
            copy.wait_send()


def gather_streams(net, place, streams, with_core):
    states = [{"sel": dict(place), "core": []} for _ in streams]
    phases = max(len(axes) for axes, _ in streams)
    for phase in range(phases):
        last = phase == phases - 1
        for (axes, items), state in zip(streams, states):
            axis = axes[phase]
            up, down = at_step(place, axis, 1), at_step(place, axis, 3)
            state["first"], state["second"] = [], []
            for first_half in (0, 1):
                for region, halves in items:
                    for target, half, way in ((up, first_half, 0), (down, 1 - first_half, 1)):
                        if halves[half] is None:
                            continue
                        ref = region(state["sel"], halves[half])
                        group = "first" if first_half == 0 else "second"
                        state[group].append((net.put(ref, ref, target), way, region, halves[half]))
            if last and with_core:
                for region, halves in items:
                    for half in halves:
                        if half is not None:
                            ref = region(state["sel"], half)
                            state["core"].append(net.put(ref, ref, other_core(place)))
        for (axes, items), state in zip(streams, states):
            axis = axes[phase]
            up, down = at_step(place, axis, 1), at_step(place, axis, 3)
            state["onward"] = []
            for copy, way, region, half in state["first"]:
                copy.wait_recv()
                origin, target = (down, up) if way == 0 else (up, down)
                ref = region({**state["sel"], axis: origin[axis]}, half)
                state["onward"].append((net.put(ref, ref, target), region, half))
                if last and with_core:
                    state["core"].append(net.put(ref, ref, other_core(place)))
        for (axes, items), state in zip(streams, states):
            axis = axes[phase]
            up, down = at_step(place, axis, 1), at_step(place, axis, 3)
            for copy, way, region, half in state["second"]:
                copy.wait_recv()
                if last and with_core:
                    origin = down if way == 0 else up
                    ref = region({**state["sel"], axis: origin[axis]}, half)
                    state["core"].append(net.put(ref, ref, other_core(place)))
        for (axes, items), state in zip(streams, states):
            axis = axes[phase]
            across = at_step(place, axis, 2)
            for copy, region, half in state["onward"]:
                copy.wait_recv()
                if last and with_core:
                    ref = region({**state["sel"], axis: across[axis]}, half)
                    state["core"].append(net.put(ref, ref, other_core(place)))
            state["sel"] = {**state["sel"], axis: None}
    for state in states:
        for copy in state["core"]:
            copy.wait_recv()


def pick(index):
    return slice(None) if index is None else index


def lanes_of(sel):
    if sel["y"] is None:
        return pl.ds(pl.multiple_of(sel["c"] * 512, 512), 512)
    return pl.ds(pl.multiple_of((sel["c"] * 4 + sel["y"]) * 128, 128), 128)


def halved(low, high):
    cut = low + (high - low) // 32 * 16
    return ((low, cut - low), (cut, high - cut))


def neighbours(place, axes=("x", "y", "z"), core=True):
    found = [at_step(place, axis, step) for axis in axes for step in (1, 3)]
    return found + ([other_core(place)] if core else [])


def weights_kernel(gi, go, gg, gd, meta, wi, wo, wg, wd, info, send, recv, local):
    place = my_place()
    greet(neighbours(place))

    def in_wi(sel, rows):
        return wi.at[pick(sel["z"]), pick(sel["x"]), pl.ds(*rows), lanes_of(sel)]

    def in_wo(sel, rows):
        z, x = sel["z"], sel["x"]
        xh, xl = (None, None) if x is None else (lax.div(x, 2), lax.rem(x, 2))
        return wo.at[pick(xh), pick(z), pick(xl), pl.ds(*rows), lanes_of(sel)]

    def in_wg(half):
        def region(sel, rows):
            z, x = sel["z"], sel["x"]
            zh, zl = (None, None) if z is None else (lax.div(z, 2), lax.rem(z, 2))
            return wg.at[pick(zh), half, pick(zl), pick(x), pl.ds(*rows), lanes_of(sel)]

        return region

    def in_wd(sel, rows):
        z, x = sel["z"], sel["x"]
        xh, xl = (None, None) if x is None else (lax.div(x, 2), lax.rem(x, 2))
        return wd.at[pick(xl), pick(z), pick(xh), pl.ds(*rows), lanes_of(sel)]

    def in_info(sel, rows):
        return info.at[pick(sel["z"]), pick(sel["x"]), pick(sel["y"]), sel["c"], :, :]

    owns = [
        (gi, in_wi(place, (0, RI))),
        (go, in_wo(place, (0, RO))),
        (gg.at[pl.ds(0, 160)], in_wg(0)(place, (0, 160))),
        (gg.at[pl.ds(160, 160)], in_wg(1)(place, (0, 160))),
        (gd, in_wd(place, (0, RD))),
        (meta, in_info(place, None)),
    ]
    copies = [pltpu.make_async_copy(src, dst, local.at[k]) for k, (src, dst) in enumerate(owns)]
    for copy in copies:
        copy.start()
    for copy in copies:
        copy.wait()
    streams = [
        (("x", "z", "y"), [(in_wg(0), halved(0, 160)), (in_wo, halved(0, 64))]),
        (("z", "y", "x"), [(in_wg(1), halved(0, 160)), (in_wi, halved(0, 64))]),
        (
            ("y", "x", "z"),
            [(in_wd, halved(0, 160)), (in_wi, halved(64, 112)), (in_info, ((0, 8), None))],
        ),
    ]
    net = Net(send, recv)
    gather_streams(net, place, streams, True)
    net.finish()


def gather_weights(gi, go, gg, gd, meta):
    shapes = [
        jax.ShapeDtypeStruct((4, 4, RI, DP), BF16),
        jax.ShapeDtypeStruct((2, 4, 2, RO, DP), BF16),
        jax.ShapeDtypeStruct((2, 2, 2, 4, 160, DP), BF16),
        jax.ShapeDtypeStruct((2, 4, 2, 160, DP), BF16),
        jax.ShapeDtypeStruct((4, 4, 4, 2, 8, 128), jnp.int32),
    ]
    count = 176
    return pl.pallas_call(
        weights_kernel,
        out_shape=shapes,
        in_specs=[ANY] * 5,
        out_specs=[ANY] * 5,
        scratch_shapes=[
            pltpu.SemaphoreType.DMA((count,)),
            pltpu.SemaphoreType.DMA((count,)),
            pltpu.SemaphoreType.DMA((6,)),
        ],
        compiler_params=pltpu.CompilerParams(collective_id=0, has_side_effects=True),
        cost_estimate=pl.CostEstimate(flops=0, bytes_accessed=400_000_000, transcendentals=0),
        name="gather_weights",
    )(gi, go, gg, gd, meta)


LANE_PARTS = ((0, 384), (384, 384), (768, 256))
ORDERS = (("x", "z", "y"), ("z", "y", "x"), ("y", "x", "z"))


def rows_kernel(own, rows, send, recv, local):
    place = my_place()
    greet(neighbours(place))

    def in_rows(lanes):
        def region(sel, part):
            return rows.at[
                pick(sel["z"]), pick(sel["x"]), pick(sel["y"]), sel["c"], pl.ds(*part), pl.ds(*lanes)
            ]

        return region

    copy = pltpu.make_async_copy(
        own, rows.at[place["z"], place["x"], place["y"], place["c"]], local
    )
    copy.start()
    copy.wait()
    streams = [
        (axes, [(in_rows(lanes), ((0, 16), (16, 16)))]) for axes, lanes in zip(ORDERS, LANE_PARTS)
    ]
    net = Net(send, recv)
    gather_streams(net, place, streams, True)
    net.finish()


def gather_rows(own):
    count = 90
    return pl.pallas_call(
        rows_kernel,
        out_shape=jax.ShapeDtypeStruct((4, 4, 4, 2, 32, DP), BF16),
        in_specs=[ANY],
        out_specs=ANY,
        scratch_shapes=[
            pltpu.SemaphoreType.DMA((count,)),
            pltpu.SemaphoreType.DMA((count,)),
            pltpu.SemaphoreType.DMA,
        ],
        compiler_params=pltpu.CompilerParams(collective_id=1, has_side_effects=True),
        name="gather_rows",
    )(own)


HOPS = (("c", 2), ("x", 4), ("y", 4), ("z", 4))


def small_kernel(combine, last, own, out, held, slots, send, recv):
    place = my_place()
    peers = [other_core(place)] + [
        at_step(place, axis, step) for axis, _ in HOPS[1:] for step in (1, 2, 3)
    ]
    greet(peers)
    held[0] = own[...]
    net = Net(send, recv)
    for hop, (axis, size) in enumerate(HOPS):
        targets = (
            [other_core(place)]
            if axis == "c"
            else [at_step(place, axis, step) for step in (1, 2, 3)]
        )
        copies = [net.put(held.at[hop], slots.at[hop, place[axis]], target) for target in targets]
        slots[hop, place[axis]] = held[hop]
        for copy in copies:
            copy.wait_recv()
        total = slots[hop, 0]
        for index in range(1, size):
            total = combine(total, slots[hop, index])
        held[hop + 1] = total
    out[...] = last(held[len(HOPS)])
    net.finish()


def small_all(value, combine, last, out_shape, collective_id, name):
    shape = value.shape
    count = 10
    return pl.pallas_call(
        functools.partial(small_kernel, combine, last),
        out_shape=jax.ShapeDtypeStruct(out_shape, F32),
        in_specs=[VMEM],
        out_specs=VMEM,
        scratch_shapes=[
            pltpu.VMEM((len(HOPS) + 1,) + shape, F32),
            pltpu.VMEM((len(HOPS), 4) + shape, F32),
            pltpu.SemaphoreType.DMA((count,)),
            pltpu.SemaphoreType.DMA((count,)),
        ],
        compiler_params=pltpu.CompilerParams(collective_id=collective_id, has_side_effects=True),
        name=name,
    )(value)


def combine_stats(one, two):
    highest = jnp.maximum(one[0], two[0])
    total = one[1] * jnp.exp(one[0] - highest) + two[1] * jnp.exp(two[0] - highest)
    return jnp.stack([highest, total])


def log_of_stats(stats):
    return stats[0] + jnp.log(stats[1])


def add_up(dst, parts):
    if len(dst.shape) == 3:

        @pl.loop(0, dst.shape[0])
        def _(k):
            total = parts[0][k].astype(F32)
            for part in parts[1:]:
                total = total + part[k].astype(F32)
            dst[k] = total.astype(dst.dtype)

        return
    total = parts[0][...].astype(F32)
    for part in parts[1:]:
        total = total + part[...].astype(F32)
    dst[...] = total.astype(dst.dtype)


class Ring:
    def __init__(self, net, place, axis, source, got, mid, result):
        self.net, self.source, self.got, self.mid, self.result = net, source, got, mid, result
        steps = [at_step(place, axis, step) for step in range(4)]
        self.own, self.up, self.across, self.down = [step[axis] for step in steps]
        self.to_up, self.to_down = steps[1], steps[3]

    def send_across(self):
        self.far_up = self.net.put(self.source(self.across, 0), self.got(0), self.to_up)
        self.far_down = self.net.put(self.source(self.across, 1), self.got(1), self.to_down)

    def send_up(self):
        self.near_up = self.net.put(self.source(self.up, 1), self.got(2), self.to_up)

    def send_down(self):
        self.near_down = self.net.put(self.source(self.down, 0), self.got(3), self.to_down)

    def send_all(self):
        self.send_across()
        self.send_up()
        self.send_down()

    def pass_on(self):
        self.far_up.wait_recv()
        add_up(self.mid(0), [self.source(self.up, 0), self.got(0)])
        self.on_up = self.net.put(self.mid(0), self.got(4), self.to_up)
        self.far_down.wait_recv()
        add_up(self.mid(1), [self.source(self.down, 1), self.got(1)])
        self.on_down = self.net.put(self.mid(1), self.got(5), self.to_down)

    def close(self):
        for copy in (self.near_up, self.near_down, self.on_up, self.on_down):
            copy.wait_recv()
        add_up(self.result(0), [self.source(self.own, 0), self.got(4), self.got(3)])
        add_up(self.result(1), [self.source(self.own, 1), self.got(2), self.got(5)])


FAR_FIRST = (2, 1, 3, 0)


def start_scatter(net, place, orders, sources, works, outs):
    streams = []
    for order, source, work, out in zip(orders, sources, works, outs):
        rows = out.shape[0] // 2
        halves = (pl.ds(0, rows), pl.ds(rows, rows))
        deep = len(order) == 3
        stream = {"first": {}, "rest": []}

        def block(one, two, half, order=order, source=source, halves=halves, deep=deep):
            sel = {"z": None, "x": None, "y": None, order[0]: one, order[1]: two}
            lead = ("z", "x", "y") if deep else ("z", "x")
            return source.at[tuple(pick(sel[axis]) for axis in lead) + (halves[half],)]

        for sub, far in enumerate(FAR_FIRST):
            two = at_step(place, order[1], far)[order[1]]
            acc = work["acc1"]

            def result(half, two=two, acc=acc, halves=halves, deep=deep):
                return acc.at[(two,) + ((slice(None),) if deep else ()) + (halves[half],)]

            stream["first"][far] = Ring(
                net,
                place,
                order[0],
                lambda one, half, two=two, block=block: block(one, two, half),
                lambda k, sub=sub, work=work: work["got1"].at[sub, k],
                lambda k, sub=sub, work=work: work["mid1"].at[sub, k],
                result,
            )
        if deep:
            stream["rest"].append(
                Ring(
                    net,
                    place,
                    order[1],
                    lambda two, half, work=work, halves=halves: work["acc1"].at[
                        two, :, halves[half]
                    ],
                    lambda k, work=work: work["got2"].at[k],
                    lambda k, work=work: work["mid2"].at[k],
                    lambda half, work=work, halves=halves: work["acc2"].at[:, halves[half]],
                )
            )
        final, number = ("acc2", "3") if deep else ("acc1", "2")
        stream["rest"].append(
            Ring(
                net,
                place,
                order[-1],
                lambda k, half, work=work, halves=halves, final=final: work[final].at[
                    k, halves[half]
                ],
                lambda k, work=work, number=number: work["got" + number].at[k],
                lambda k, work=work, number=number: work["mid" + number].at[k],
                lambda half, out=out, halves=halves: out.at[halves[half]],
            )
        )
        streams.append(stream)
    return streams


def send_first(streams):
    for far in FAR_FIRST:
        for stream in streams:
            stream["first"][far].send_across()
    for far in FAR_FIRST:
        for stream in streams:
            stream["first"][far].send_up()
            stream["first"][far].send_down()


def finish_scatter(streams):
    for far in FAR_FIRST:
        for stream in streams:
            stream["first"][far].pass_on()
    for far in FAR_FIRST:
        for stream in streams:
            stream["first"][far].close()
            following = stream["rest"][0]
            if far == 2:
                following.send_across()
            if far == 1:
                following.send_up()
            if far == 3:
                following.send_down()
    for number in range(len(streams[0]["rest"])):
        for stream in streams:
            stream["rest"][number].pass_on()
        for stream in streams:
            stream["rest"][number].close()
            if number + 1 < len(stream["rest"]):
                stream["rest"][number + 1].send_all()


def scatter_sum(net, place, orders, sources, works, outs):
    streams = start_scatter(net, place, orders, sources, works, outs)
    send_first(streams)
    finish_scatter(streams)


WORK_NAMES = ("got1", "mid1", "acc1", "got2", "mid2", "acc2", "got3", "mid3")


def work_shapes(rows, lanes, first, later):
    half = rows // 2
    return [
        pltpu.VMEM((4, 6, 4, half, lanes), first),
        pltpu.VMEM((4, 2, 4, half, lanes), first),
        pltpu.VMEM((4, 4, rows, lanes), later),
        pltpu.VMEM((6, 4, half, lanes), later),
        pltpu.VMEM((2, 4, half, lanes), later),
        pltpu.VMEM((4, rows, lanes), later),
        pltpu.VMEM((6, half, lanes), later),
        pltpu.VMEM((2, half, lanes), later),
    ]


SHALLOW_NAMES = ("got1", "mid1", "acc1", "got2", "mid2")


def shallow_shapes(rows, lanes, first, later):
    half = rows // 2
    return [
        pltpu.VMEM((4, 6, half, lanes), first),
        pltpu.VMEM((4, 2, half, lanes), first),
        pltpu.VMEM((4, rows, lanes), later),
        pltpu.VMEM((6, half, lanes), later),
        pltpu.VMEM((2, half, lanes), later),
    ]


SUM_COPIES = 3 * (24 + 6 + 6)
SHALLOW_COPIES = 2 * (24 + 6)


def grads_kernel(di, do, dg, dd, out, *scratch):
    held = scratch[0:3]
    works = [dict(zip(WORK_NAMES, scratch[3 + 8 * k : 11 + 8 * k])) for k in range(3)]
    send, recv, local = scratch[27:]
    place = my_place()
    moves = []
    for y in range(4):
        lanes = pl.ds(y * 128, 128)
        for z in range(4):
            for half in range(2):
                moves.append(
                    (
                        dg.at[z // 2, half, z % 2, :, :, lanes],
                        held[half].at[z, :, y, pl.ds(0, 160)],
                    )
                )
        for x in range(4):
            moves.append((dd.at[x % 2, :, x // 2, :, lanes], held[2].at[:, x, y, pl.ds(0, 160)]))
            moves.append((do.at[x // 2, :, x % 2, :, lanes], held[0].at[:, x, y, pl.ds(160, 64)]))
        for z in range(4):
            moves.append(
                (di.at[z, :, pl.ds(0, 64), lanes], held[1].at[z, :, y, pl.ds(160, 64)])
            )
            moves.append(
                (di.at[z, :, pl.ds(64, 48), lanes], held[2].at[z, :, y, pl.ds(160, 48)])
            )
    copies = [pltpu.make_async_copy(src, dst, local.at[k]) for k, (src, dst) in enumerate(moves)]
    for copy in copies:
        copy.start()
    held[2][:, :, :, 208:224, :] = jnp.zeros((4, 4, 4, 16, 128), held[2].dtype)
    greet(neighbours(place, core=False))
    for copy in copies:
        copy.wait()
    net = Net(send, recv)
    scatter_sum(net, place, ORDERS, held, works, [out.at[k] for k in range(3)])
    net.finish()


def scatter_grads(di, do, dg, dd, first, later):
    rows, lanes = 224, 128
    scratch = [pltpu.VMEM((4, 4, 4, rows, lanes), first)] * 3
    for _ in range(3):
        scratch += work_shapes(rows, lanes, first, later)
    scratch += [
        pltpu.SemaphoreType.DMA((SUM_COPIES,)),
        pltpu.SemaphoreType.DMA((SUM_COPIES,)),
        pltpu.SemaphoreType.DMA((96,)),
    ]
    return pl.pallas_call(
        grads_kernel,
        out_shape=jax.ShapeDtypeStruct((3, rows, lanes), F32),
        in_specs=[ANY] * 4,
        out_specs=VMEM,
        scratch_shapes=scratch,
        compiler_params=pltpu.CompilerParams(
            collective_id=2, has_side_effects=True, vmem_limit_bytes=56 << 20
        ),
        name="scatter_grads",
    )(di, do, dg, dd)


def row_sums_kernel(part, out, *scratch):
    held = scratch[0:3]
    works = [dict(zip(WORK_NAMES, scratch[3 + 8 * k : 11 + 8 * k])) for k in range(3)]
    send, recv, local = scratch[27:]
    place = my_place()
    copies = [
        pltpu.make_async_copy(part.at[:, :, :, :, pl.ds(*lanes)], held[k], local.at[k])
        for k, lanes in enumerate(LANE_PARTS)
    ]
    for copy in copies:
        copy.start()
    greet(neighbours(place, core=False))
    for copy in copies:
        copy.wait()
    net = Net(send, recv)
    outs = [out.at[:, pl.ds(*lanes)] for lanes in LANE_PARTS]
    scatter_sum(net, place, ORDERS, held, works, outs)
    net.finish()


def scatter_rows(part, first, later):
    scratch = [pltpu.VMEM((4, 4, 4, 32, lanes), first) for _, lanes in LANE_PARTS]
    for _, lanes in LANE_PARTS:
        scratch += work_shapes(32, lanes, first, later)
    scratch += [
        pltpu.SemaphoreType.DMA((SUM_COPIES,)),
        pltpu.SemaphoreType.DMA((SUM_COPIES,)),
        pltpu.SemaphoreType.DMA((3,)),
    ]
    return pl.pallas_call(
        row_sums_kernel,
        out_shape=jax.ShapeDtypeStruct((32, DP), F32),
        in_specs=[ANY],
        out_specs=VMEM,
        scratch_shapes=scratch,
        compiler_params=pltpu.CompilerParams(
            collective_id=3, has_side_effects=True, vmem_limit_bytes=56 << 20
        ),
        name="scatter_rows",
    )(part)


def embed_grad_kernel(dx, ids, out, rows, table, chosen, *scratch):
    works = [dict(zip(SHALLOW_NAMES, scratch[5 * k : 5 * k + 5])) for k in range(2)]
    send, recv, local = scratch[10:]
    place = my_place()
    greet(neighbours(place))
    copy = pltpu.make_async_copy(dx, rows.at[place["y"], place["c"]], local)
    copy.start()
    copy.wait()

    def in_rows(sel, part):
        return rows.at[pick(sel["y"]), sel["c"], pl.ds(*part)]

    net = Net(send, recv)
    gather_streams(net, place, [(("y",), [(in_rows, ((0, 128), (128, 128)))])], True)
    base = (place["y"] * 2 + place["c"]) * 16

    def parts(count, place_of):
        @pl.loop(0, count)
        def _(k):
            z, x = place_of(k)
            start = (base + z * 4 + x) * 384

            @pl.loop(0, 24)
            def _(r):
                row = pl.multiple_of(r * 16, 16)
                number = lax.broadcasted_iota(jnp.int32, (16, 2048), 0) + (start + row)
                chosen[pl.ds(row, 16), :] = (number == ids[...]).astype(F32).astype(BF16)

            @pl.loop(0, 4)
            def _(l):
                lanes = pl.ds(pl.multiple_of(l * 256, 256), 256)
                total = jnp.zeros((384, 256), F32)
                for w in range(8):
                    total = total + jnp.dot(
                        chosen[:, pl.ds(w * 256, 256)],
                        rows[w // 2, w % 2, :, lanes],
                        preferred_element_type=F32,
                    )
                table[z, x, :, lanes] = total.astype(BF16)

    def further(axis, step):
        return lax.rem(place[axis] + step, 4)

    sources = [table.at[:, :, pl.ds(0, 192)], table.at[:, :, pl.ds(192, 192)]]
    outs = [out.at[pl.ds(0, 192)], out.at[pl.ds(192, 192)]]
    streams = start_scatter(net, place, (("x", "z"), ("z", "x")), sources, works, outs)
    by_x, by_z = streams[0]["first"], streams[1]["first"]
    parts(4, lambda k: (further("z", 2), further("x", k + 2)))
    for step in FAR_FIRST:
        by_z[step].send_across()
    by_x[2].send_across()
    parts(3, lambda k: (further("z", k + 3), further("x", 2)))
    for step in (1, 3, 0):
        by_x[step].send_across()
    by_x[2].send_up()
    by_x[2].send_down()
    by_z[2].send_up()
    by_z[2].send_down()
    parts(9, lambda k: (further("z", lax.div(k, 3) + 3), further("x", lax.rem(k, 3) + 3)))
    for step in (1, 3, 0):
        by_x[step].send_up()
        by_x[step].send_down()
        by_z[step].send_up()
        by_z[step].send_down()
    finish_scatter(streams)
    net.finish()


def embed_grad(dx, ids):
    count = SHALLOW_COPIES + 16
    scratch = [
        pltpu.VMEM((4, 2, 256, DP), BF16),
        pltpu.VMEM((4, 4, 384, DP), BF16),
        pltpu.VMEM((384, 2048), BF16),
    ]
    for _ in range(2):
        scratch += shallow_shapes(192, DP, BF16, BF16)
    scratch += [
        pltpu.SemaphoreType.DMA((count,)),
        pltpu.SemaphoreType.DMA((count,)),
        pltpu.SemaphoreType.DMA,
    ]
    return pl.pallas_call(
        embed_grad_kernel,
        out_shape=jax.ShapeDtypeStruct((384, DP), F32),
        in_specs=[ANY, VMEM],
        out_specs=VMEM,
        scratch_shapes=scratch,
        compiler_params=pltpu.CompilerParams(
            collective_id=6, has_side_effects=True, vmem_limit_bytes=56 << 20
        ),
        name="embed_grad",
    )(dx, ids)


def gram_kernel(pieces, turned, gram, part, *scratch):
    works = [dict(zip(SHALLOW_NAMES, scratch[5 * k : 5 * k + 5])) for k in range(2)]
    send, recv, local = scratch[10:]
    place = my_place()
    wides = [
        {**at_step(place, "y", step), "c": core}
        for step in (2, 1, 3, 0)
        for core in (place["c"], 1 - place["c"])
    ][:-2] + [other_core(place)]
    greet(wides + neighbours(place, ("x", "z"), False))
    net = Net(send, recv)

    def lanes_from(who):
        return pl.ds(pl.multiple_of((who["c"] * 4 + who["y"]) * 128, 128), 128)

    arrivals = [net.put(pieces.at[who["y"]], turned.at[:, lanes_from(place)], who) for who in wides]
    copy = pltpu.make_async_copy(pieces.at[place["y"]], turned.at[:, lanes_from(place)], local)
    copy.start()
    copy.wait()
    for arrival in arrivals:
        arrival.wait_recv()
    @pl.loop(0, 4)
    def _(k):
        rows = pl.ds(pl.multiple_of(place["c"] * 512 + k * 128, 128), 128)
        left = turned[:, rows].T
        for l in range(2):
            lanes = pl.ds(l * 512, 512)
            product = jnp.dot(left, turned[:, lanes], precision=HIGHEST, preferred_element_type=F32)
            for m in range(4):
                part[k, m, :, lanes] = product[m * 32 : m * 32 + 32]

    orders = (("x", "z"), ("z", "x"))
    lanes = (pl.ds(0, 512), pl.ds(512, 512))
    sources = [part.at[:, :, :, lane] for lane in lanes]
    mine = gram.at[place["c"], place["z"], place["x"]]
    outs = [mine.at[:, lane] for lane in lanes]
    scatter_sum(net, place, orders, sources, works, outs)

    def in_gram(lane):
        def region(sel, rows):
            return gram.at[sel["c"], pick(sel["z"]), pick(sel["x"]), pl.ds(*rows), lane]

        return region

    streams = [
        (order[::-1], [(in_gram(lane), ((0, 16), (16, 16)))]) for order, lane in zip(orders, lanes)
    ]
    gather_streams(net, place, streams, True)
    net.finish()


def gram_of(pieces):
    count = 7 + SHALLOW_COPIES + 44
    scratch = [pltpu.VMEM((4, 4, 32, DP), F32)]
    for _ in range(2):
        scratch += shallow_shapes(32, 512, F32, F32)
    scratch += [
        pltpu.SemaphoreType.DMA((count,)),
        pltpu.SemaphoreType.DMA((count,)),
        pltpu.SemaphoreType.DMA,
    ]
    return pl.pallas_call(
        gram_kernel,
        out_shape=[
            jax.ShapeDtypeStruct((320, DP), F32),
            jax.ShapeDtypeStruct((2, 4, 4, 32, DP), F32),
        ],
        in_specs=[VMEM],
        out_specs=[VMEM, VMEM],
        scratch_shapes=scratch,
        compiler_params=pltpu.CompilerParams(
            collective_id=7, has_side_effects=True, vmem_limit_bytes=40 << 20
        ),
        name="gram_sums",
    )(pieces)


def pad_features(values):
    lead = values.shape[:-1]
    blocks = values.reshape(lead + (4, 2, 2, 60))
    blocks = jnp.moveaxis(blocks, -3, -4)
    blocks = jnp.pad(blocks, [(0, 0)] * (len(lead) + 3) + [(0, 4)])
    return blocks.reshape(lead + (DP,))


def feature_table():
    feature = lax.broadcasted_iota(jnp.int32, (D, DP), 0)
    place = lax.broadcasted_iota(jnp.int32, (D, DP), 1)
    wide, rest = feature // 120, feature % 120
    where = ((wide % 2) * 4 + wide // 2) * 128 + (rest // 60) * 64 + rest % 60
    return (where == place).astype(BF16)


def column_table():
    column = lax.broadcasted_iota(jnp.int32, (QKV, 16 * RI), 0)
    place = lax.broadcasted_iota(jnp.int32, (QKV, 16 * RI), 1)
    return ((column // 100) * RI + column % 100 == place).astype(BF16)


def to_shard(matrix, rows):
    columns = matrix.shape[1]
    turned = matrix.T.reshape(columns, 2, 60)
    turned = jnp.pad(turned, ((0, rows - columns), (0, 0), (0, 4)))
    return turned.reshape(rows, 128)


def from_shard(shard, columns):
    return shard[:columns].reshape(columns, 2, 64)[:, :, :60].reshape(columns, 120).T


def dot(left, right, left_axis, right_axis, precision=None):
    return lax.dot_general(
        left,
        right,
        (((left_axis,), (right_axis,)), ((), ())),
        preferred_element_type=F32,
        precision=precision,
    )


def rms_norm(values, gain_row):
    mean = jnp.sum(values * values, axis=-1, keepdims=True) * (1.0 / D)
    return values * lax.rsqrt(mean + NORM_EPS) * gain_row


def rotate(values, places):
    half_width = HD // 2
    frequency = ROPE_THETA ** (-2.0 * jnp.arange(half_width).astype(F32) / HD)
    angles = places.astype(F32)[:, None] * frequency[None, :]
    cosine = jnp.concatenate([jnp.cos(angles), jnp.cos(angles)], axis=-1)[:, None, :]
    sine_part = jnp.concatenate([jnp.sin(angles), jnp.sin(angles)], axis=-1)[:, None, :]
    turned = jnp.concatenate([-values[..., half_width:], values[..., :half_width]], axis=-1)
    return values * cosine + turned * sine_part


def gated(gate_up):
    return gate_up[:, :FF] * jax.nn.sigmoid(gate_up[:, :FF]) * gate_up[:, FF:]


def adam_update(weight, first_moment, second_moment, gradient, step_rate, decay_rate):
    first_new = BETA_ONE * first_moment + (1.0 - BETA_ONE) * gradient
    second_new = BETA_TWO * second_moment + (1.0 - BETA_TWO) * gradient * gradient
    update = (
        first_new
        / (1.0 - BETA_ONE**STEP)
        / (jnp.sqrt(second_new / (1.0 - BETA_TWO**STEP)) + ADAM_EPS)
    )
    return (first_new, second_new, weight * (1.0 - step_rate * decay_rate) - step_rate * update)


def partner(value):
    return lax.ppermute(value, "wide", [(k, k ^ 1) for k in range(8)])


def body(
    token_ids,
    target_ids,
    prefix_lengths,
    loss_positions,
    w_input,
    w_output,
    w_gate_up,
    w_down,
    norm_gains,
    embed_table,
    moment_input,
    moment_output,
    moment_gate_up,
    moment_down,
    table_first,
    table_second,
    gains_first,
    gains_second,
):
    wide = lax.axis_index("wide")
    narrow = lax.axis_index("narrow")
    core = wide % 2
    masters = (w_input[0], w_output[0], w_gate_up[0], w_down[0])
    moments = (moment_input[0], moment_output[0], moment_gate_up[0], moment_down[0])
    group_size = H // KVH
    kv_width = KVH * HD
    scale_factor = HD ** (-0.5)
    features = feature_table()
    columns = column_table()
    gains = pad_features(norm_gains)
    own_places = wide * ROWS + jnp.arange(ROWS)
    key_places = jnp.arange(SEQ)
    tokens = token_ids[:, 0]
    targets = target_ids[:, 0]
    prefixes = prefix_lengths[:, 0]
    positions = loss_positions[:, 0]

    own_positions = lax.dynamic_slice_in_dim(positions, wide * PICK, PICK, axis=1)
    own_targets = jnp.take_along_axis(targets, own_positions, axis=1).reshape(MB * PICK)
    own_counted = (own_positions >= prefixes[:, None]).astype(jnp.int32).reshape(MB * PICK)
    meta = jnp.pad(jnp.stack([own_targets, own_counted]), ((0, 6), (0, 128 - MB * PICK)))

    table_low = dot(embed_table.astype(BF16), features, 1, 0).astype(BF16)
    slab = lax.all_gather(table_low, "narrow", axis=0, tiled=True)
    table_other = partner(table_low)

    shards = [
        to_shard(master.astype(BF16), rows) for master, rows in zip(masters, (RI, RO, RG, RD))
    ]
    wi, wo, wg, wd, info = gather_weights(*shards, meta)
    slab, wi = lax.optimization_barrier((slab, wi))
    wi = wi.reshape(16, RI, DP)[:, :100].reshape(QKV, DP)
    wo = wo.reshape(DP, DP)
    wg = wg.reshape(2 * FF, DP)
    wd = wd.reshape(FF, DP)
    info = info.reshape(128, 8, 128)
    all_targets = info[:, 0, : MB * PICK].reshape(4096)
    all_counted = info[:, 1, : MB * PICK].reshape(4096).astype(F32)

    slab_rows = slab.shape[0]
    ordered = tokens.reshape(MB, 8, ROWS).swapaxes(0, 1).reshape(2048)
    local_ids = ordered - wide * slab_rows
    inside = (local_ids >= 0) & (local_ids < slab_rows)
    safe_ids = jnp.clip(local_ids, 0, slab_rows - 1)
    looked_up = jnp.where(inside[:, None], slab[safe_ids], jnp.zeros((), BF16))
    x0 = lax.psum_scatter(looked_up, "wide", scatter_dimension=0, tiled=True).astype(F32)

    a = rms_norm(x0, gains[0]).astype(BF16)
    projected = dot(a, wi, 1, 1)
    places_all = jnp.concatenate([own_places, own_places])
    rows_count = MB * ROWS
    query = rotate(projected[:, : H * HD].reshape(rows_count, H, HD), places_all).astype(BF16)
    key_own = rotate(
        projected[:, H * HD : H * HD + kv_width].reshape(rows_count, KVH, HD), places_all
    ).astype(BF16)
    value_own = projected[:, H * HD + kv_width :].astype(BF16)
    kv_own = jnp.concatenate([key_own.reshape(rows_count, kv_width), value_own], axis=1)
    kv_all = lax.all_gather(kv_own, "wide", axis=0, tiled=False)
    kv_all = kv_all.reshape(8, MB, ROWS, 2 * kv_width)

    def allowed_of(batch):
        return (key_places[None, :] <= own_places[:, None]) | (
            key_places[None, :] < prefixes[batch]
        )

    kept = []
    mixed_parts = []
    for batch in range(MB):
        q = query.reshape(MB, ROWS, KVH, group_size, HD)[batch]
        k = kv_all[:, batch, :, :kv_width].reshape(SEQ, KVH, HD)
        v = kv_all[:, batch, :, kv_width:].reshape(SEQ, KVH, HD)
        scores = jnp.einsum("qkgd,tkd->kgqt", q, k, preferred_element_type=F32) * scale_factor
        scores = jnp.where(allowed_of(batch), scores, NEGATIVE)
        highest = jnp.max(scores, axis=-1, keepdims=True)
        exp_part = jnp.exp(scores - highest)
        exp_total = jnp.sum(exp_part, axis=-1, keepdims=True)
        log_total = highest + jnp.log(exp_total)
        probs = (exp_part / exp_total).astype(BF16)
        mixed = jnp.einsum("kgqt,tkd->qkgd", probs, v, preferred_element_type=F32)
        mixed_parts.append(mixed.reshape(ROWS, H * HD).astype(BF16))
        kept.append((q, k, v, log_total))
    o_pad = dot(jnp.concatenate(mixed_parts), features, 1, 0).astype(BF16)
    x1 = x0 + dot(o_pad, wo, 1, 1)

    b = rms_norm(x1, gains[1]).astype(BF16)
    gate_up = dot(b, wg, 1, 1)
    activated = gated(gate_up).astype(BF16)
    x2 = x1 + dot(activated, wd, 1, 0)

    final = rms_norm(x2, gains[2]).astype(BF16)
    own_offsets = (own_positions - wide * ROWS + jnp.arange(MB)[:, None] * ROWS).reshape(-1)
    all_rows = gather_rows(final[own_offsets]).reshape(4096, DP)
    logits = dot(all_rows, table_low, 1, 1)
    vocab_start = (wide * 16 + narrow) * 384
    hit = jnp.arange(384)[None, :] == (all_targets - vocab_start)[:, None]
    highest = jnp.max(logits, axis=-1)
    exp_total = jnp.sum(jnp.exp(logits - highest[:, None]), axis=-1)
    stats = jnp.stack([highest.reshape(32, 128), exp_total.reshape(32, 128)])
    log_total = small_all(stats, combine_stats, log_of_stats, (32, 128), 4, "row_totals")
    log_total = log_total.reshape(4096)
    hit_sum = jnp.sum(jnp.where(hit, logits, 0.0) * all_counted[:, None])
    logit_sum = jnp.sum(logits * all_counted[:, None])
    token_count = jnp.sum(all_counted)
    loss_known = jnp.sum(all_counted * (log_total + ZLOSS_WEIGHT * log_total * log_total))
    d_logits = (
        all_counted[:, None]
        * (
            (1.0 + 2.0 * ZLOSS_WEIGHT * log_total)[:, None] * jnp.exp(logits - log_total[:, None])
            - (1.0 - SMOOTH) * hit.astype(F32)
            - SMOOTH / V
        )
    ).astype(BF16)
    table_grad_rows = dot(d_logits, all_rows, 0, 0)
    d_by_core = d_logits.reshape(64, 2, 32, 384)
    d_mine = lax.dynamic_index_in_dim(d_by_core, core, 1, keepdims=False).reshape(2048, 384)
    d_theirs = lax.dynamic_index_in_dim(d_by_core, 1 - core, 1, keepdims=False).reshape(2048, 384)
    d_theirs = partner(d_theirs)
    row_part = dot(d_mine, table_low, 1, 0) + dot(d_theirs, table_other, 1, 0)
    d_rows = scatter_rows(row_part.astype(BF16).reshape(4, 4, 4, 32, DP), BF16, F32)

    d_final = jnp.zeros((rows_count, DP), F32).at[own_offsets].add(d_rows)
    d_x2, d_gain_final = jax.vjp(rms_norm, x2, gains[2])[1](d_final)
    d_branch = d_x2.astype(BF16)
    d_activated = dot(d_branch, wd, 1, 1)
    d_gate_up = jax.vjp(gated, gate_up)[1](d_activated)[0].astype(BF16)
    d_b = dot(d_gate_up, wg, 1, 0)
    d_x1_part, d_gain_mlp = jax.vjp(rms_norm, x1, gains[1])[1](d_b)
    d_x1 = d_x2 + d_x1_part
    d_out = d_x1.astype(BF16)
    d_mixed_pad = dot(d_out, wo, 1, 0).astype(BF16)
    d_mixed = dot(d_mixed_pad, features, 1, 1).astype(BF16)
    d_queries, d_kv = [], []
    for batch in range(MB):
        q, k, v, log_sum = kept[batch]
        d_m = d_mixed.reshape(MB, ROWS, KVH, group_size, HD)[batch]
        scores = jnp.einsum("qkgd,tkd->kgqt", q, k, preferred_element_type=F32) * scale_factor
        scores = jnp.where(allowed_of(batch), scores, NEGATIVE)
        probs = jnp.exp(scores - log_sum)
        d_probs = jnp.einsum("qkgd,tkd->kgqt", d_m, v, preferred_element_type=F32)
        d_scores = (
            probs * (d_probs - jnp.sum(probs * d_probs, axis=-1, keepdims=True))
        ).astype(BF16)
        d_q = jnp.einsum("kgqt,tkd->qkgd", d_scores, k, preferred_element_type=F32) * scale_factor
        d_k = jnp.einsum("kgqt,qkgd->tkd", d_scores, q, preferred_element_type=F32) * scale_factor
        d_v = jnp.einsum(
            "kgqt,qkgd->tkd", probs.astype(BF16), d_m, preferred_element_type=F32
        )
        d_queries.append(d_q.reshape(ROWS, H, HD))
        d_kv.append(
            jnp.concatenate(
                [d_k.reshape(8, ROWS, kv_width), d_v.reshape(8, ROWS, kv_width)], axis=2
            )
        )
    d_kv_all = jnp.stack(d_kv, axis=1).reshape(8 * rows_count, 2 * kv_width)
    d_kv_own = lax.psum_scatter(d_kv_all, "wide", scatter_dimension=0, tiled=True)

    def unrotate(gradient, heads):
        primal = jnp.zeros((rows_count, heads, HD), F32)
        return jax.vjp(lambda values: rotate(values, places_all), primal)[1](gradient)[0]

    d_projected = jnp.concatenate(
        [
            unrotate(jnp.concatenate(d_queries), H).reshape(rows_count, H * HD),
            unrotate(d_kv_own[:, :kv_width].reshape(rows_count, KVH, HD), KVH).reshape(
                rows_count, kv_width
            ),
            d_kv_own[:, kv_width:],
        ],
        axis=1,
    ).astype(BF16)
    d_a = dot(d_projected, wi, 1, 0)
    d_x0_part, d_gain_attn = jax.vjp(rms_norm, x0, gains[0])[1](d_a)
    d_x0 = (d_x1 + d_x0_part).astype(BF16)

    def half_pair(value):
        mine = lax.dynamic_slice_in_dim(value, core * 512, 512, axis=1)
        theirs = lax.dynamic_slice_in_dim(value, (1 - core) * 512, 512, axis=1)
        return jnp.concatenate([mine, partner(theirs)])

    def both(value):
        return jnp.concatenate([value, partner(value)])

    d_projected_pad = dot(d_projected, columns, 1, 0).astype(BF16)
    grad_wd = dot(both(activated), half_pair(d_branch), 0, 0).astype(BF16)
    grad_wg = dot(both(d_gate_up), half_pair(b), 0, 0).astype(BF16)
    grad_wo = dot(both(d_out), half_pair(o_pad), 0, 0).astype(BF16)
    grad_wi = dot(both(d_projected_pad), half_pair(a), 0, 0).astype(BF16)
    summed_grads = scatter_grads(
        grad_wi.reshape(4, 4, RI, 512),
        grad_wo.reshape(2, 4, 2, RO, 512),
        grad_wg.reshape(2, 2, 2, 4, 160, 512),
        grad_wd.reshape(2, 4, 2, 160, 512),
        BF16,
        F32,
    )
    grad_shards = (
        jnp.concatenate([summed_grads[1, 160:224], summed_grads[2, 160:208]]),
        summed_grads[0, 160:224],
        jnp.concatenate([summed_grads[0, :160], summed_grads[1, :160]]),
        summed_grads[2, :160],
    )

    table_grad = embed_grad(d_x0, ordered[None, :])
    table_grad = dot(table_grad + table_grad_rows, features, 1, 1, HIGHEST)

    squares = sum(jnp.sum(shard * shard) for shard in grad_shards) + jnp.sum(
        table_grad * table_grad
    )
    gain_grads = jnp.stack([d_gain_attn, d_gain_mlp, d_gain_final]).reshape(24, 128)
    scalars = jnp.pad(jnp.stack([squares, hit_sum, logit_sum]), (0, 125))
    packed = jnp.pad(jnp.concatenate([gain_grads, scalars[None]]), ((0, 7), (0, 0)))
    summed = small_all(packed, jnp.add, lambda v: v, (32, 128), 5, "global_sums")
    gain_grad = dot(summed[:24].reshape(3, DP), features, 1, 1, HIGHEST)
    loss_total = loss_known - (1.0 - SMOOTH) * summed[24, 1] - SMOOTH / V * summed[24, 2]
    grad_norm = jnp.sqrt(summed[24, 0] + jnp.sum(gain_grad * gain_grad)) / token_count
    factor = jnp.minimum(1.0, CLIP_NORM / grad_norm) / token_count

    new_shards = [
        MOMENTUM * to_shard(moment, rows) + factor * grad
        for moment, rows, grad in zip(moments, (RI, RO, RG, RD), grad_shards)
    ]
    pieces = jnp.stack([jnp.pad(s, ((0, 320 - s.shape[0]), (0, 0))) for s in new_shards])
    turned, gram = gram_of(pieces)
    gram = gram.reshape(DP, DP)
    turned = lax.dynamic_slice_in_dim(turned, core * 160, 160)
    norm = jnp.sqrt(jnp.trace(gram)) + 1e-07
    current = turned / norm
    gram = gram / norm / norm
    identity = jnp.eye(DP, dtype=F32)
    for ns_step in range(ITERS):
        if ns_step < ITERS - 1:
            square = dot(gram, gram, 1, 0, HIGH)
            step_matrix = NS_A * identity + NS_B * gram + NS_C * square
            current = dot(current, step_matrix, 1, 0, HIGH)
            gram = dot(dot(step_matrix, gram, 1, 0, HIGH), step_matrix, 1, 0, HIGH)
        else:
            applied = dot(current, gram, 1, 0, HIGH)
            current = NS_A * current + NS_B * applied + NS_C * dot(applied, gram, 1, 0, HIGH)
    pieces = current.reshape(160, 2, 4, 128).transpose(2, 1, 0, 3).reshape(8, 160, 128)
    pieces = lax.all_to_all(pieces, "wide", split_axis=0, concat_axis=0)
    pieces = pieces.reshape(4, 320, 128)
    new_moments, new_weights = [], []
    for kind, rows in enumerate((RI, RO, RG, RD)):
        count = masters[kind].shape[1]
        ortho = pieces[kind, :rows]
        new_moments.append(from_shard(new_shards[kind], count)[None])
        new_weights.append(
            (
                masters[kind] * (1.0 - MUON_RATE * WEIGHT_DECAY)
                - MUON_RATE * 0.2 * math.sqrt(count * 16) * from_shard(ortho, count)
            )[None]
        )
    table_m, table_v, table_new = adam_update(
        embed_table, table_first, table_second, factor * table_grad, TABLE_RATE, WEIGHT_DECAY
    )
    gains_m, gains_v, gains_new = adam_update(
        norm_gains, gains_first, gains_second, factor * gain_grad, GAIN_RATE, 0.0
    )
    return (
        loss_total,
        token_count,
        grad_norm,
        *new_moments,
        *new_weights,
        *[weight.astype(BF16) for weight in new_weights],
        table_m,
        table_v,
        table_new,
        table_new.astype(BF16),
        gains_m,
        gains_v,
        gains_new,
    )


def solution(mesh):
    whole = P()
    by_sequence = P(None, "narrow", None)
    matrix = P(None, "wide", "narrow")
    table = P(("wide", "narrow"), None)
    return jax.shard_map(
        body,
        mesh=mesh,
        in_specs=(
            (by_sequence, by_sequence, P(None, "narrow"), by_sequence)
            + (matrix,) * 4
            + (whole, table)
            + (matrix,) * 4
            + (table, table, whole, whole)
        ),
        out_specs=(whole,) * 3 + (matrix,) * 12 + (table,) * 4 + (whole,) * 3,
        check_vma=False,
    )
```

```python
import functools
import math

import jax
import jax.numpy as jnp
from jax import lax
from jax.experimental import pallas as pl
from jax.experimental.pallas import tpu as pltpu
from jax.sharding import PartitionSpec as P

D = 960
H = 15
KVH = 5
HD = 64
FF = 2560
V = 49152
QKV = 1600
ITERS = 5
STEP = 10
MB = 2
SEQ = 1024
ROWS = 128
PICK = 16
DP = 1024

NORM_EPS = 1e-05
ROPE_THETA = 100000.0
SMOOTH = 0.1
ZLOSS_WEIGHT = 0.0001
CLIP_NORM = 0.02
MOMENTUM = 0.95
NS_A = 3.4445
NS_B = -4.775
NS_C = 2.0315
MUON_RATE = 0.1
WEIGHT_DECAY = 0.1
BETA_ONE = 0.9
BETA_TWO = 0.95
TABLE_RATE = 0.03
GAIN_RATE = 0.4
ADAM_EPS = 1e-08
NEGATIVE = -1e30

HIGHEST = lax.Precision.HIGHEST
HIGH = lax.Precision.HIGH
F32 = jnp.float32
BF16 = jnp.bfloat16
MESH = pl.DeviceIdType.MESH
ANY = pl.BlockSpec(memory_space=pl.ANY)
VMEM = pl.BlockSpec(memory_space=pltpu.VMEM)

RI, RO, RG, RD = 112, 64, 320, 160


def my_place():
    wide = lax.axis_index("wide")
    narrow = lax.axis_index("narrow")
    return {
        "y": lax.div(wide, 2),
        "c": lax.rem(wide, 2),
        "z": lax.div(narrow, 4),
        "x": lax.rem(narrow, 4),
    }


def device(place):
    return (place["y"] * 2 + place["c"], place["z"] * 4 + place["x"])


def at_step(place, axis, step):
    return {**place, axis: lax.rem(place[axis] + step, 4)}


def other_core(place):
    return {**place, "c": 1 - place["c"]}


def greet(targets):
    barrier = pltpu.get_barrier_semaphore()
    for target in targets:
        pl.semaphore_signal(barrier, inc=1, device_id=device(target), device_id_type=MESH)
    pl.semaphore_wait(barrier, len(targets))


class Net:
    def __init__(self, send, recv):
        self.send = send
        self.recv = recv
        self.copies = []

    def put(self, src, dst, target):
        k = len(self.copies)
        copy = pltpu.make_async_remote_copy(
            src_ref=src,
            dst_ref=dst,
            send_sem=self.send.at[k],
            recv_sem=self.recv.at[k],
            device_id=device(target),
            device_id_type=MESH,
        )
        copy.start()
        self.copies.append(copy)
        return copy

    def finish(self):
        for copy in self.copies:
            copy.wait_send()


class Spread:
    def __init__(self, net, place, axes, items, with_core):
        self.net, self.place, self.axes, self.items = net, place, axes, items
        self.with_core = with_core
        self.sel = dict(place)
        self.phase = 0
        self.core = []

    def to_core(self, region, sel, half):
        if self.with_core and self.phase == len(self.axes) - 1:
            ref = region(sel, half)
            self.core.append(self.net.put(ref, ref, other_core(self.place)))

    def begin(self):
        self.axis = self.axes[self.phase]
        self.up, self.across, self.down = [at_step(self.place, self.axis, k) for k in (1, 2, 3)]
        self.first, self.second, self.onward = [], [], []
        for group, first_half in ((self.first, 0), (self.second, 1)):
            for region, halves in self.items:
                for target, origin, half in (
                    (self.up, self.down, first_half),
                    (self.down, self.up, 1 - first_half),
                ):
                    if halves[half] is not None:
                        ref = region(self.sel, halves[half])
                        copy = self.net.put(ref, ref, target)
                        group.append((copy, origin, target, region, halves[half]))
        for region, halves in self.items:
            for half in halves:
                if half is not None:
                    self.to_core(region, self.sel, half)

    def relay(self):
        for copy, origin, target, region, half in self.first:
            copy.wait_recv()
            sel = {**self.sel, self.axis: origin[self.axis]}
            ref = region(sel, half)
            self.onward.append((self.net.put(ref, ref, target), region, half))
            self.to_core(region, sel, half)

    def near(self):
        for copy, origin, _, region, half in self.second:
            copy.wait_recv()
            self.to_core(region, {**self.sel, self.axis: origin[self.axis]}, half)

    def far(self):
        for copy, region, half in self.onward:
            copy.wait_recv()
            self.to_core(region, {**self.sel, self.axis: self.across[self.axis]}, half)
        self.sel[self.axis] = None
        self.phase += 1

    def end(self):
        for copy in self.core:
            copy.wait_recv()


def gather_streams(net, place, streams, with_core):
    spreads = [Spread(net, place, axes, items, with_core) for axes, items in streams]
    for _ in range(len(streams[0][0])):
        for step in ("begin", "relay", "near", "far"):
            for spread in spreads:
                getattr(spread, step)()
    for spread in spreads:
        spread.end()


def pick(index):
    return slice(None) if index is None else index


def lanes_of(sel):
    if sel["y"] is None:
        return pl.ds(pl.multiple_of(sel["c"] * 512, 512), 512)
    return pl.ds(pl.multiple_of((sel["c"] * 4 + sel["y"]) * 128, 128), 128)


def halved(low, high):
    cut = low + (high - low) // 32 * 16
    return ((low, cut - low), (cut, high - cut))


def neighbours(place, axes=("x", "y", "z"), core=True):
    found = [at_step(place, axis, step) for axis in axes for step in (1, 3)]
    return found + ([other_core(place)] if core else [])


def fetch_kernel(
    gi, go, gg, gd, meta, table, ids, marks, wi, wo, wg, wd, info, x0, *scratch
):
    slab_x, slab_z, total, chosen, packed, theirs, got, send, recv, local = scratch
    place = my_place()

    def in_wi(sel, rows):
        return wi.at[pick(sel["z"]), pick(sel["x"]), pl.ds(*rows), lanes_of(sel)]

    def in_wo(sel, rows):
        z, x = sel["z"], sel["x"]
        xh, xl = (None, None) if x is None else (lax.div(x, 2), lax.rem(x, 2))
        return wo.at[pick(xh), pick(z), pick(xl), pl.ds(*rows), lanes_of(sel)]

    def in_wg(half):
        def region(sel, rows):
            z, x = sel["z"], sel["x"]
            zh, zl = (None, None) if z is None else (lax.div(z, 2), lax.rem(z, 2))
            return wg.at[pick(zh), half, pick(zl), pick(x), pl.ds(*rows), lanes_of(sel)]

        return region

    def in_wd(sel, rows):
        z, x = sel["z"], sel["x"]
        xh, xl = (None, None) if x is None else (lax.div(x, 2), lax.rem(x, 2))
        return wd.at[pick(xl), pick(z), pick(xh), pl.ds(*rows), lanes_of(sel)]

    def in_info(sel, rows):
        return info.at[pick(sel["z"]), pick(sel["x"]), pick(sel["y"]), sel["c"], :, :]

    owns = [
        (gi, in_wi(place, (0, RI))),
        (go, in_wo(place, (0, RO))),
        (gg.at[pl.ds(0, 160)], in_wg(0)(place, (0, 160))),
        (gg.at[pl.ds(160, 160)], in_wg(1)(place, (0, 160))),
        (gd, in_wd(place, (0, RD))),
        (meta, in_info(place, None)),
        (table.at[pl.ds(0, 192)], slab_x.at[place["z"], place["x"]]),
        (table.at[pl.ds(192, 192)], slab_z.at[place["x"], place["z"]]),
    ]
    copies = [pltpu.make_async_copy(src, dst, local.at[k]) for k, (src, dst) in enumerate(owns)]
    for copy in copies:
        copy.start()
    for copy in copies:
        copy.wait()
    greet(neighbours(place))
    net = Net(send, recv)
    rows = ((0, 96), (96, 96))
    tables = [
        Spread(
            net,
            place,
            ("x", "z"),
            [(lambda sel, part: slab_x.at[pick(sel["z"]), pick(sel["x"]), pl.ds(*part)], rows)],
            False,
        ),
        Spread(
            net,
            place,
            ("z", "x"),
            [(lambda sel, part: slab_z.at[pick(sel["x"]), pick(sel["z"]), pl.ds(*part)], rows)],
            False,
        ),
    ]
    weights = [
        Spread(net, place, axes, items, True)
        for axes, items in (
            (("x", "z", "y"), [(in_wg(0), halved(0, 160)), (in_wo, halved(0, 64))]),
            (("z", "x", "y"), [(in_wg(1), halved(0, 160)), (in_wi, halved(0, 64))]),
            (
                ("y", "z", "x"),
                [(in_wd, halved(0, 160)), (in_wi, halved(64, 112)), (in_info, ((0, 8), None))],
            ),
        )
    ]

    def each(spreads, *steps):
        for step in steps:
            for spread in spreads:
                getattr(spread, step)()

    base = (place["y"] * 2 + place["c"]) * (16 * 384)

    def look_up(slab, index, kind, start, initial):
        @pl.loop(0, 16)
        def _(r):
            part = pl.ds(pl.multiple_of(r * 128, 128), 128)
            wanted = ids[part, :] - start
            chosen[part, :] = (marks[kind : kind + 1, :] == wanted).astype(F32).astype(BF16)

        @pl.loop(0, 8)
        def _(k):
            part = pl.ds(pl.multiple_of(lax.div(k, 4) * 1024, 1024), 1024)
            lanes = pl.ds(pl.multiple_of(lax.rem(k, 4) * 256, 256), 256)
            block = slab[index, :, :, lanes].reshape(768, 256)
            found = jnp.dot(chosen[part, :], block, preferred_element_type=F32)
            total[part, lanes] = found if initial else total[part, lanes] + found

    def by_x(step, initial=False):
        z = lax.rem(place["z"] + step, 4)
        look_up(slab_x, z, 0, base + z * (4 * 384), initial)

    def by_z(step):
        x = lax.rem(place["x"] + step, 4)
        look_up(slab_z, x, 1, base + x * 384 + 192, False)

    each(tables, "begin")
    each(weights, "begin")
    each(tables, "relay")
    each(weights, "relay")
    each(tables, "near", "far", "begin")
    each(weights, "near", "far", "begin")
    by_x(0, True)
    by_z(0)
    each(tables, "relay")
    each(weights, "relay", "near", "far", "begin")
    each(tables, "near")
    by_x(1)
    by_x(3)
    each(weights, "relay")
    by_z(1)
    by_z(3)
    each(tables, "far")
    by_x(2)
    each(weights, "near")
    by_z(2)
    for y in range(4):
        for c in range(2):
            packed[c, y] = total[(y * 2 + c) * 256 : (y * 2 + c + 1) * 256, :].astype(BF16)
    swap = net.put(packed.at[1 - place["c"]], theirs, other_core(place))
    swap.wait_recv()
    mine = packed.at[place["c"]]
    for y in range(4):
        add_up(theirs.at[y], [mine.at[y], theirs.at[y]])
    halves = (pl.ds(0, 128), pl.ds(128, 128))
    ring = Ring(
        net,
        place,
        "y",
        lambda k, half: theirs.at[k, halves[half]],
        lambda k: got.at[k],
        lambda half: x0.at[halves[half]],
    )
    ring.send_all()
    each(weights, "far")
    ring.pass_on()
    ring.close()
    each(weights, "end")
    net.finish()


def fetch(gi, go, gg, gd, meta, table, ids, marks):
    shapes = [
        jax.ShapeDtypeStruct((4, 4, RI, DP), BF16),
        jax.ShapeDtypeStruct((2, 4, 2, RO, DP), BF16),
        jax.ShapeDtypeStruct((2, 2, 2, 4, 160, DP), BF16),
        jax.ShapeDtypeStruct((2, 4, 2, 160, DP), BF16),
        jax.ShapeDtypeStruct((4, 4, 4, 2, 8, 128), jnp.int32),
        jax.ShapeDtypeStruct((256, DP), BF16),
    ]
    count = 210
    return pl.pallas_call(
        fetch_kernel,
        out_shape=shapes,
        in_specs=[ANY] * 6 + [VMEM] * 2,
        out_specs=[ANY] * 5 + [VMEM],
        scratch_shapes=[
            pltpu.VMEM((4, 4, 192, DP), BF16),
            pltpu.VMEM((4, 4, 192, DP), BF16),
            pltpu.VMEM((2048, DP), F32),
            pltpu.VMEM((2048, 768), BF16),
            pltpu.VMEM((2, 4, 256, DP), BF16),
            pltpu.VMEM((4, 256, DP), BF16),
            pltpu.VMEM((6, 128, DP), BF16),
            pltpu.SemaphoreType.DMA((count,)),
            pltpu.SemaphoreType.DMA((count,)),
            pltpu.SemaphoreType.DMA((8,)),
        ],
        compiler_params=pltpu.CompilerParams(
            collective_id=0, has_side_effects=True, vmem_limit_bytes=56 << 20
        ),
        name="fetch",
    )(gi, go, gg, gd, meta, table, ids, marks)


LANE_PARTS = ((0, 384), (384, 384), (768, 256))
ORDERS = (("x", "z", "y"), ("z", "y", "x"), ("y", "x", "z"))


def rows_kernel(own, rows, send, recv, local):
    place = my_place()
    greet(neighbours(place))

    def in_rows(lanes):
        def region(sel, part):
            return rows.at[
                pick(sel["z"]), pick(sel["x"]), pick(sel["y"]), sel["c"], pl.ds(*part), pl.ds(*lanes)
            ]

        return region

    copy = pltpu.make_async_copy(
        own, rows.at[place["z"], place["x"], place["y"], place["c"]], local
    )
    copy.start()
    copy.wait()
    streams = [
        (axes, [(in_rows(lanes), ((0, 16), (16, 16)))]) for axes, lanes in zip(ORDERS, LANE_PARTS)
    ]
    net = Net(send, recv)
    gather_streams(net, place, streams, True)
    net.finish()


def gather_rows(own):
    count = 90
    return pl.pallas_call(
        rows_kernel,
        out_shape=jax.ShapeDtypeStruct((4, 4, 4, 2, 32, DP), BF16),
        in_specs=[VMEM],
        out_specs=VMEM,
        scratch_shapes=[
            pltpu.SemaphoreType.DMA((count,)),
            pltpu.SemaphoreType.DMA((count,)),
            pltpu.SemaphoreType.DMA,
        ],
        compiler_params=pltpu.CompilerParams(
            collective_id=1, has_side_effects=True, vmem_limit_bytes=24 << 20
        ),
        name="gather_rows",
    )(own)


HOPS = (("c", 2), ("x", 4), ("y", 4), ("z", 4))


def small_kernel(combine, last, own, out, held, slots, send, recv):
    place = my_place()
    peers = [other_core(place)] + [
        at_step(place, axis, step) for axis, _ in HOPS[1:] for step in (1, 2, 3)
    ]
    greet(peers)
    held[0] = own[...]
    net = Net(send, recv)
    for hop, (axis, size) in enumerate(HOPS):
        targets = (
            [other_core(place)]
            if axis == "c"
            else [at_step(place, axis, step) for step in (1, 2, 3)]
        )
        copies = [net.put(held.at[hop], slots.at[hop, place[axis]], target) for target in targets]
        slots[hop, place[axis]] = held[hop]
        for copy in copies:
            copy.wait_recv()
        total = slots[hop, 0]
        for index in range(1, size):
            total = combine(total, slots[hop, index])
        held[hop + 1] = total
    out[...] = last(held[len(HOPS)])
    net.finish()


def small_all(value, combine, last, out_shape, collective_id, name):
    shape = value.shape
    count = 10
    return pl.pallas_call(
        functools.partial(small_kernel, combine, last),
        out_shape=jax.ShapeDtypeStruct(out_shape, F32),
        in_specs=[VMEM],
        out_specs=VMEM,
        scratch_shapes=[
            pltpu.VMEM((len(HOPS) + 1,) + shape, F32),
            pltpu.VMEM((len(HOPS), 4) + shape, F32),
            pltpu.SemaphoreType.DMA((count,)),
            pltpu.SemaphoreType.DMA((count,)),
        ],
        compiler_params=pltpu.CompilerParams(collective_id=collective_id, has_side_effects=True),
        name=name,
    )(value)


def combine_stats(one, two):
    highest = jnp.maximum(one[0], two[0])
    total = one[1] * jnp.exp(one[0] - highest) + two[1] * jnp.exp(two[0] - highest)
    return jnp.stack([highest, total])


def log_of_stats(stats):
    return stats[0] + jnp.log(stats[1])


def add_up(dst, parts):
    if len(dst.shape) == 3:

        @pl.loop(0, dst.shape[0])
        def _(k):
            total = parts[0][k].astype(F32)
            for part in parts[1:]:
                total = total + part[k].astype(F32)
            dst[k] = total.astype(dst.dtype)

        return
    total = parts[0][...].astype(F32)
    for part in parts[1:]:
        total = total + part[...].astype(F32)
    dst[...] = total.astype(dst.dtype)


class Ring:
    def __init__(self, net, place, axis, source, got, result):
        self.net, self.source, self.got, self.result = net, source, got, result
        steps = [at_step(place, axis, step) for step in range(4)]
        self.own, self.up, self.across, self.down = [step[axis] for step in steps]
        self.to_up, self.to_down = steps[1], steps[3]

    def send_across(self):
        self.far_up = self.net.put(self.source(self.across, 0), self.got(0), self.to_up)
        self.far_down = self.net.put(self.source(self.across, 1), self.got(1), self.to_down)

    def send_up(self):
        self.near_up = self.net.put(self.source(self.up, 1), self.got(2), self.to_up)

    def send_down(self):
        self.near_down = self.net.put(self.source(self.down, 0), self.got(3), self.to_down)

    def send_all(self):
        self.send_across()
        self.send_up()
        self.send_down()

    def pass_on(self):
        self.far_up.wait_recv()
        add_up(self.got(0), [self.source(self.up, 0), self.got(0)])
        self.on_up = self.net.put(self.got(0), self.got(4), self.to_up)
        self.far_down.wait_recv()
        add_up(self.got(1), [self.source(self.down, 1), self.got(1)])
        self.on_down = self.net.put(self.got(1), self.got(5), self.to_down)

    def close(self):
        for copy in (self.near_up, self.near_down, self.on_up, self.on_down):
            copy.wait_recv()
        add_up(self.result(0), [self.source(self.own, 0), self.got(4), self.got(3)])
        add_up(self.result(1), [self.source(self.own, 1), self.got(2), self.got(5)])


FAR_FIRST = (2, 1, 3, 0)


def start_scatter(net, place, order, source, gots, out, acc=None):
    rows = out.shape[0] // 2
    halves = (pl.ds(0, rows), pl.ds(rows, rows))
    lead = ("z", "x", "y")[: len(order)]

    def block(sel, half):
        return source.at[tuple(pick(sel.get(axis)) for axis in lead) + (halves[half],)]

    def summed(sel, half):
        if acc is None:
            return block({order[0]: place[order[0]], **sel}, half)
        return acc.at[tuple(pick(sel.get(axis)) for axis in order[1:]) + (halves[half],)]

    stream = {"first": {}, "rest": []}
    one, two = order[:2]
    for sub, far in enumerate(FAR_FIRST):
        at_two = at_step(place, two, far)[two]
        stream["first"][far] = Ring(
            net,
            place,
            one,
            lambda k, half, at_two=at_two: block({one: k, two: at_two}, half),
            lambda k, sub=sub: gots[0].at[sub, k],
            lambda half, at_two=at_two: summed({two: at_two}, half),
        )
    for number in range(1, len(order)):
        done = {axis: place[axis] for axis in order[1:number]}

        def part(k, half, done=done, axis=order[number]):
            return summed({**done, axis: k}, half)

        if number + 1 < len(order):
            result = lambda half, part=part, axis=order[number]: part(place[axis], half)
        else:
            result = lambda half: out.at[halves[half]]
        stream["rest"].append(
            Ring(net, place, order[number], part, lambda k, n=number: gots[n].at[k], result)
        )
    return stream


def send_first(streams):
    for far in FAR_FIRST:
        for stream in streams:
            stream["first"][far].send_across()
    for far in FAR_FIRST:
        for stream in streams:
            stream["first"][far].send_up()
            stream["first"][far].send_down()


def finish_scatter(streams, passed=False):
    if not passed:
        for far in FAR_FIRST:
            for stream in streams:
                stream["first"][far].pass_on()
    for far in FAR_FIRST:
        for stream in streams:
            stream["first"][far].close()
            following = stream["rest"][0]
            if far == 2:
                following.send_across()
            if far == 1:
                following.send_up()
            if far == 3:
                following.send_down()
    for number in range(max(len(stream["rest"]) for stream in streams)):
        active = [stream["rest"] for stream in streams if number < len(stream["rest"])]
        for rest in active:
            rest[number].pass_on()
        for rest in active:
            rest[number].close()
            if number + 1 < len(rest):
                rest[number + 1].send_all()


def got_shapes(depth, rows, lanes, first, later):
    half = rows // 2
    return [
        pltpu.VMEM(
            ((4, 6) if number == 0 else (6,)) + (4,) * (depth - max(number, 1) - 1) + (half, lanes),
            later if number else first,
        )
        for number in range(depth)
    ]


def row_sums_kernel(part, out, *scratch):
    held = scratch[0:3]
    accs = scratch[12:15]
    send, recv, local = scratch[15:]
    place = my_place()
    copies = [
        pltpu.make_async_copy(part.at[:, :, :, :, pl.ds(*lanes)], held[k], local.at[k])
        for k, lanes in enumerate(LANE_PARTS)
    ]
    for copy in copies:
        copy.start()
    greet(neighbours(place, core=False))
    for copy in copies:
        copy.wait()
    net = Net(send, recv)
    streams = [
        start_scatter(
            net,
            place,
            order,
            held[k],
            scratch[3 + 3 * k : 6 + 3 * k],
            out.at[:, pl.ds(*lanes)],
            accs[k],
        )
        for k, (order, lanes) in enumerate(zip(ORDERS, LANE_PARTS))
    ]
    send_first(streams)
    finish_scatter(streams)
    net.finish()


def scatter_rows(part):
    scratch = [pltpu.VMEM((4, 4, 4, 32, lanes), part.dtype) for _, lanes in LANE_PARTS]
    for _, lanes in LANE_PARTS:
        scratch += got_shapes(3, 32, lanes, part.dtype, F32)
    scratch += [pltpu.VMEM((4, 4, 32, lanes), F32) for _, lanes in LANE_PARTS]
    scratch += [
        pltpu.SemaphoreType.DMA((108,)),
        pltpu.SemaphoreType.DMA((108,)),
        pltpu.SemaphoreType.DMA((3,)),
    ]
    return pl.pallas_call(
        row_sums_kernel,
        out_shape=jax.ShapeDtypeStruct((32, DP), F32),
        in_specs=[ANY],
        out_specs=VMEM,
        scratch_shapes=scratch,
        compiler_params=pltpu.CompilerParams(
            collective_id=3, has_side_effects=True, vmem_limit_bytes=40 << 20
        ),
        name="scatter_rows",
    )(part)


GRAD_ORDERS = (("y", "x", "z"), ("y", "z", "x"), ("x", "z", "y"))


def grads_kernel(dx, ids, di, do, dg, dd, out, weights_out, *scratch):
    rows, table, chosen = scratch[:3]
    held = scratch[3:6]
    gots = scratch[6:10]
    weight_gots = scratch[10:19]
    accs = scratch[19:22]
    send, recv, local = scratch[22:]
    place = my_place()
    moves = [(dx, rows.at[place["y"], place["c"]])]
    for y in range(4):
        lanes = pl.ds(y * 128, 128)
        for z in range(4):
            for half in range(2):
                moves.append(
                    (
                        dg.at[z // 2, half, z % 2, :, :, lanes],
                        held[half].at[z, :, y, pl.ds(0, 160)],
                    )
                )
        for x in range(4):
            moves.append((dd.at[x % 2, :, x // 2, :, lanes], held[2].at[:, x, y, pl.ds(0, 160)]))
            moves.append((do.at[x // 2, :, x % 2, :, lanes], held[0].at[:, x, y, pl.ds(160, 64)]))
        for z in range(4):
            moves.append((di.at[z, :, pl.ds(0, 64), lanes], held[1].at[z, :, y, pl.ds(160, 64)]))
            moves.append((di.at[z, :, pl.ds(64, 48), lanes], held[2].at[z, :, y, pl.ds(160, 48)]))
    copies = [pltpu.make_async_copy(src, dst, local.at[k]) for k, (src, dst) in enumerate(moves)]
    for copy in copies:
        copy.start()
    held[2][:, :, :, 208:224, :] = jnp.zeros((4, 4, 4, 16, 128), BF16)
    greet(neighbours(place))
    copies[0].wait()

    def in_rows(sel, part):
        return rows.at[pick(sel["y"]), sel["c"], pl.ds(*part)]

    net = Net(send, recv)
    spread = Spread(net, place, ("y",), [(in_rows, ((0, 128), (128, 128)))], True)
    spread.begin()
    for copy in copies[1:]:
        copy.wait()
    weight_streams = [
        start_scatter(
            net, place, order, held[k], weight_gots[3 * k : 3 * k + 3], weights_out.at[k], accs[k]
        )
        for k, order in enumerate(GRAD_ORDERS)
    ]
    send_first(weight_streams[2:])
    spread.relay()
    spread.near()
    spread.far()
    send_first(weight_streams[:2])
    spread.end()
    base = (place["y"] * 2 + place["c"]) * 16

    def parts(count, place_of):
        @pl.loop(0, count)
        def _(k):
            z, x = place_of(k)
            start = (base + z * 4 + x) * 384

            @pl.loop(0, 24)
            def _(r):
                row = pl.multiple_of(r * 16, 16)
                number = lax.broadcasted_iota(jnp.int32, (16, 2048), 0) + (start + row)
                chosen[pl.ds(row, 16), :] = (number == ids[...]).astype(F32).astype(BF16)

            @pl.loop(0, 4)
            def _(l):
                lanes = pl.ds(pl.multiple_of(l * 256, 256), 256)
                total = jnp.zeros((384, 256), F32)
                for w in range(8):
                    total = total + jnp.dot(
                        chosen[:, pl.ds(w * 256, 256)],
                        rows[w // 2, w % 2, :, lanes],
                        preferred_element_type=F32,
                    )
                table[z, x, :, lanes] = total.astype(BF16)

    def further(axis, step):
        return lax.rem(place[axis] + step, 4)

    streams = [
        start_scatter(
            net,
            place,
            order,
            table.at[:, :, pl.ds(192 * k, 192)],
            gots[2 * k : 2 * k + 2],
            out.at[pl.ds(192 * k, 192)],
        )
        for k, order in enumerate((("x", "z"), ("z", "x")))
    ]
    by_x, by_z = streams[0]["first"], streams[1]["first"]
    parts(4, lambda k: (further("z", 2), further("x", k + 2)))
    for step in FAR_FIRST:
        by_z[step].send_across()
    by_x[2].send_across()
    parts(3, lambda k: (further("z", k + 3), further("x", 2)))
    for step in (1, 3, 0):
        by_x[step].send_across()
    by_x[2].send_up()
    by_x[2].send_down()
    by_z[2].send_up()
    by_z[2].send_down()
    for step in FAR_FIRST:
        weight_streams[2]["first"][step].pass_on()
    parts(9, lambda k: (further("z", lax.div(k, 3) + 3), further("x", lax.rem(k, 3) + 3)))
    for step in (1, 3, 0):
        by_x[step].send_up()
        by_x[step].send_down()
        by_z[step].send_up()
        by_z[step].send_down()
    for step in FAR_FIRST:
        for stream in streams + weight_streams[:2]:
            stream["first"][step].pass_on()
    finish_scatter(streams + weight_streams, passed=True)
    net.finish()


def scatter_grads(dx, ids, di, do, dg, dd):
    count = 3 * 36 + 2 * 30 + 16
    scratch = [
        pltpu.VMEM((4, 2, 256, DP), BF16),
        pltpu.VMEM((4, 4, 384, DP), BF16),
        pltpu.VMEM((384, 2048), BF16),
    ]
    scratch += [pltpu.VMEM((4, 4, 4, 224, 128), BF16)] * 3
    scratch += got_shapes(2, 192, DP, BF16, BF16) * 2
    scratch += got_shapes(3, 224, 128, BF16, F32) * 3
    scratch += [pltpu.VMEM((4, 4, 224, 128), F32)] * 3
    scratch += [
        pltpu.SemaphoreType.DMA((count,)),
        pltpu.SemaphoreType.DMA((count,)),
        pltpu.SemaphoreType.DMA((97,)),
    ]
    return pl.pallas_call(
        grads_kernel,
        out_shape=[
            jax.ShapeDtypeStruct((384, DP), F32),
            jax.ShapeDtypeStruct((3, 224, 128), F32),
        ],
        in_specs=[ANY, VMEM] + [ANY] * 4,
        out_specs=[VMEM, VMEM],
        scratch_shapes=scratch,
        compiler_params=pltpu.CompilerParams(
            collective_id=2, has_side_effects=True, vmem_limit_bytes=60 << 20
        ),
        name="scatter_grads",
    )(dx, ids, di, do, dg, dd)


def lanes_of_wide(y, c):
    return pl.ds(pl.multiple_of((y * 2 + c) * 128, 128), 128)


def keys_kernel(own, out, send, recv, local):
    place = my_place()
    copy = pltpu.make_async_copy(own, out.at[:, :, lanes_of_wide(place["y"], place["c"])], local)
    copy.start()
    greet(neighbours(place, ("y",)))
    copy.wait()

    def region(sel, rows):
        return out.at[:, pl.ds(*rows), lanes_of_wide(sel["y"], sel["c"])]

    net = Net(send, recv)
    gather_streams(net, place, [(("y",), [(region, ((0, 160), (160, 160)))])], True)
    net.finish()


def gather_keys(own):
    return pl.pallas_call(
        keys_kernel,
        out_shape=jax.ShapeDtypeStruct((4, 320, SEQ), BF16),
        in_specs=[VMEM],
        out_specs=VMEM,
        scratch_shapes=[
            pltpu.SemaphoreType.DMA((14,)),
            pltpu.SemaphoreType.DMA((14,)),
            pltpu.SemaphoreType.DMA,
        ],
        compiler_params=pltpu.CompilerParams(
            collective_id=6, has_side_effects=True, vmem_limit_bytes=16 << 20
        ),
        name="gather_keys",
    )(own)


def key_sums_kernel(*refs):
    parts, out = refs[:4], refs[4]
    theirs, held, got, send, recv = refs[5:]
    place = my_place()
    greet(neighbours(place, ("y",)))
    net = Net(send, recv)
    swaps = [
        [
            net.put(
                part.at[:, lanes_of_wide(at_step(place, "y", step)["y"], 1 - place["c"])],
                theirs.at[at_step(place, "y", step)["y"], k],
                other_core(place),
            )
            for k, part in enumerate(parts)
        ]
        for step in FAR_FIRST
    ]
    ring = Ring(
        net,
        place,
        "y",
        lambda k, half: held.at[k, pl.ds(2 * half, 2)],
        lambda k: got.at[k],
        lambda half: out.at[pl.ds(2 * half, 2)],
    )
    for step, swap in zip(FAR_FIRST, swaps):
        y = at_step(place, "y", step)["y"]
        for k, part in enumerate(parts):
            swap[k].wait_recv()
            own = part[:, lanes_of_wide(y, place["c"])]
            held[y, k] = (own + theirs[y, k]).astype(BF16)
        if step == 2:
            ring.send_across()
        if step == 1:
            ring.send_up()
        if step == 3:
            ring.send_down()
    ring.pass_on()
    ring.close()
    net.finish()


def sum_keys(parts):
    return pl.pallas_call(
        key_sums_kernel,
        out_shape=jax.ShapeDtypeStruct((4, 320, 128), F32),
        in_specs=[VMEM] * 4,
        out_specs=VMEM,
        scratch_shapes=[
            pltpu.VMEM((4, 4, 320, 128), F32),
            pltpu.VMEM((4, 4, 320, 128), BF16),
            pltpu.VMEM((6, 2, 320, 128), BF16),
            pltpu.SemaphoreType.DMA((22,)),
            pltpu.SemaphoreType.DMA((22,)),
        ],
        compiler_params=pltpu.CompilerParams(
            collective_id=8, has_side_effects=True, vmem_limit_bytes=32 << 20
        ),
        name="sum_keys",
    )(*parts)


def gram_kernel(pieces, turned, gram, part, *scratch):
    gots = scratch[:4]
    send, recv, local = scratch[4:]
    place = my_place()
    wides = [
        {**at_step(place, "y", step), "c": core}
        for step in (2, 1, 3, 0)
        for core in (place["c"], 1 - place["c"])
    ][:-2] + [other_core(place)]
    greet(wides + neighbours(place, ("x", "z"), False))
    net = Net(send, recv)

    def lanes_from(who):
        return pl.ds(pl.multiple_of((who["c"] * 4 + who["y"]) * 128, 128), 128)

    arrivals = [net.put(pieces.at[who["y"]], turned.at[:, lanes_from(place)], who) for who in wides]
    copy = pltpu.make_async_copy(pieces.at[place["y"]], turned.at[:, lanes_from(place)], local)
    copy.start()
    copy.wait()
    for arrival in arrivals:
        arrival.wait_recv()
    @pl.loop(0, 4)
    def _(k):
        rows = pl.ds(pl.multiple_of(place["c"] * 512 + k * 128, 128), 128)
        left = turned[:, rows].T
        for l in range(2):
            lanes = pl.ds(l * 512, 512)
            product = jnp.dot(left, turned[:, lanes], precision=HIGHEST, preferred_element_type=F32)
            for m in range(4):
                part[k, m, :, lanes] = product[m * 32 : m * 32 + 32]

    orders = (("x", "z"), ("z", "x"))
    lanes = (pl.ds(0, 512), pl.ds(512, 512))
    mine = gram.at[place["c"], place["z"], place["x"]]
    streams = [
        start_scatter(
            net, place, order, part.at[:, :, :, lane], gots[2 * k : 2 * k + 2], mine.at[:, lane]
        )
        for k, (order, lane) in enumerate(zip(orders, lanes))
    ]
    send_first(streams)
    finish_scatter(streams)

    def in_gram(lane):
        def region(sel, rows):
            return gram.at[sel["c"], pick(sel["z"]), pick(sel["x"]), pl.ds(*rows), lane]

        return region

    streams = [
        (order[::-1], [(in_gram(lane), ((0, 16), (16, 16)))]) for order, lane in zip(orders, lanes)
    ]
    gather_streams(net, place, streams, True)
    net.finish()


def gram_of(pieces):
    count = 7 + 2 * 30 + 44
    scratch = [pltpu.VMEM((4, 4, 32, DP), F32)]
    scratch += got_shapes(2, 32, 512, F32, F32) * 2
    scratch += [
        pltpu.SemaphoreType.DMA((count,)),
        pltpu.SemaphoreType.DMA((count,)),
        pltpu.SemaphoreType.DMA,
    ]
    return pl.pallas_call(
        gram_kernel,
        out_shape=[
            jax.ShapeDtypeStruct((320, DP), F32),
            jax.ShapeDtypeStruct((2, 4, 4, 32, DP), F32),
        ],
        in_specs=[VMEM],
        out_specs=[VMEM, VMEM],
        scratch_shapes=scratch,
        compiler_params=pltpu.CompilerParams(
            collective_id=7, has_side_effects=True, vmem_limit_bytes=40 << 20
        ),
        name="gram_sums",
    )(pieces)


def pad_features(values):
    lead = values.shape[:-1]
    blocks = values.reshape(lead + (4, 2, 2, 60))
    blocks = jnp.moveaxis(blocks, -3, -4)
    blocks = jnp.pad(blocks, [(0, 0)] * (len(lead) + 3) + [(0, 4)])
    return blocks.reshape(lead + (DP,))


def feature_table():
    feature = lax.broadcasted_iota(jnp.int32, (D, DP), 0)
    place = lax.broadcasted_iota(jnp.int32, (D, DP), 1)
    wide, rest = feature // 120, feature % 120
    where = ((wide % 2) * 4 + wide // 2) * 128 + (rest // 60) * 64 + rest % 60
    return (where == place).astype(BF16)


def column_table():
    column = lax.broadcasted_iota(jnp.int32, (QKV, 16 * RI), 0)
    place = lax.broadcasted_iota(jnp.int32, (QKV, 16 * RI), 1)
    return ((column // 100) * RI + column % 100 == place).astype(BF16)


def to_shard(matrix, rows):
    columns = matrix.shape[1]
    turned = matrix.T.reshape(columns, 2, 60)
    turned = jnp.pad(turned, ((0, rows - columns), (0, 0), (0, 4)))
    return turned.reshape(rows, 128)


def from_shard(shard, columns):
    return shard[:columns].reshape(columns, 2, 64)[:, :, :60].reshape(columns, 120).T


def dot(left, right, left_axis, right_axis, precision=None):
    return lax.dot_general(
        left,
        right,
        (((left_axis,), (right_axis,)), ((), ())),
        preferred_element_type=F32,
        precision=precision,
    )


def rms_norm(values, gain_row):
    mean = jnp.sum(values * values, axis=-1, keepdims=True) * (1.0 / D)
    return values * lax.rsqrt(mean + NORM_EPS) * gain_row


def rotate(values, places):
    half_width = HD // 2
    frequency = ROPE_THETA ** (-2.0 * jnp.arange(half_width).astype(F32) / HD)
    angles = places.astype(F32)[:, None] * frequency[None, :]
    cosine = jnp.concatenate([jnp.cos(angles), jnp.cos(angles)], axis=-1)[:, None, :]
    sine_part = jnp.concatenate([jnp.sin(angles), jnp.sin(angles)], axis=-1)[:, None, :]
    turned = jnp.concatenate([-values[..., half_width:], values[..., :half_width]], axis=-1)
    return values * cosine + turned * sine_part


def gated(gate_up):
    return gate_up[:, :FF] * jax.nn.sigmoid(gate_up[:, :FF]) * gate_up[:, FF:]


def adam_update(weight, first_moment, second_moment, gradient, step_rate, decay_rate):
    first_new = BETA_ONE * first_moment + (1.0 - BETA_ONE) * gradient
    second_new = BETA_TWO * second_moment + (1.0 - BETA_TWO) * gradient * gradient
    update = (
        first_new
        / (1.0 - BETA_ONE**STEP)
        / (jnp.sqrt(second_new / (1.0 - BETA_TWO**STEP)) + ADAM_EPS)
    )
    return (first_new, second_new, weight * (1.0 - step_rate * decay_rate) - step_rate * update)


def partner(value):
    return lax.ppermute(value, "wide", [(k, k ^ 1) for k in range(8)])


def body(
    token_ids,
    target_ids,
    prefix_lengths,
    loss_positions,
    w_input,
    w_output,
    w_gate_up,
    w_down,
    norm_gains,
    embed_table,
    moment_input,
    moment_output,
    moment_gate_up,
    moment_down,
    table_first,
    table_second,
    gains_first,
    gains_second,
):
    wide = lax.axis_index("wide")
    narrow = lax.axis_index("narrow")
    core = wide % 2
    masters = (w_input[0], w_output[0], w_gate_up[0], w_down[0])
    moments = (moment_input[0], moment_output[0], moment_gate_up[0], moment_down[0])
    group_size = H // KVH
    kv_width = KVH * HD
    scale_factor = HD ** (-0.5)
    features = feature_table()
    columns = column_table()
    gains = pad_features(norm_gains)
    own_places = wide * ROWS + jnp.arange(ROWS)
    key_places = jnp.arange(SEQ)
    tokens = token_ids[:, 0]
    targets = target_ids[:, 0]
    prefixes = prefix_lengths[:, 0]
    positions = loss_positions[:, 0]

    own_positions = lax.dynamic_slice_in_dim(positions, wide * PICK, PICK, axis=1)
    own_targets = jnp.take_along_axis(targets, own_positions, axis=1).reshape(MB * PICK)
    own_counted = (own_positions >= prefixes[:, None]).astype(jnp.int32).reshape(MB * PICK)
    meta = jnp.pad(jnp.stack([own_targets, own_counted]), ((0, 6), (0, 128 - MB * PICK)))

    table_low = dot(embed_table.astype(BF16), features, 1, 0).astype(BF16)
    table_other = partner(table_low)

    shards = [
        to_shard(master.astype(BF16), rows) for master, rows in zip(masters, (RI, RO, RG, RD))
    ]
    ordered = tokens.reshape(MB, 8, ROWS).swapaxes(0, 1).reshape(2048)
    mark = jnp.arange(768)
    marks = jnp.stack([mark // 192 * 384, mark // 192 * 1536]) + mark % 192
    wi, wo, wg, wd, info, x0 = fetch(
        *shards, meta, table_low, ordered[:, None], marks.astype(jnp.int32)
    )
    x0 = x0.astype(F32)
    wi = wi.reshape(16, RI, DP)[:, :100].reshape(QKV, DP)
    wo = wo.reshape(DP, DP)
    wg = wg.reshape(2 * FF, DP)
    wd = wd.reshape(FF, DP)
    info = info.reshape(128, 8, 128)
    all_targets = info[:, 0, : MB * PICK].reshape(4096)
    all_counted = info[:, 1, : MB * PICK].reshape(4096).astype(F32)

    a = rms_norm(x0, gains[0]).astype(BF16)
    projected = dot(a, wi, 1, 1)
    places_all = jnp.concatenate([own_places, own_places])
    rows_count = MB * ROWS
    query = rotate(projected[:, : H * HD].reshape(rows_count, H, HD), places_all).astype(BF16)
    key_own = rotate(
        projected[:, H * HD : H * HD + kv_width].reshape(rows_count, KVH, HD), places_all
    ).astype(BF16)
    value_own = projected[:, H * HD + kv_width :].astype(BF16)
    kv_own = [
        part.reshape(MB, ROWS, kv_width).swapaxes(1, 2)
        for part in (key_own.reshape(rows_count, kv_width), value_own)
    ]
    kv_all = gather_keys(jnp.concatenate(kv_own)).reshape(4, KVH, HD, SEQ)

    def allowed_of(batch):
        return (key_places[None, :] <= own_places[:, None]) | (
            key_places[None, :] < prefixes[batch]
        )

    kept = []
    mixed_parts = []
    for batch in range(MB):
        q = query.reshape(MB, ROWS, KVH, group_size, HD)[batch]
        k, v = kv_all[batch], kv_all[MB + batch]
        scores = jnp.einsum("qkgd,kdt->kgqt", q, k, preferred_element_type=F32) * scale_factor
        scores = jnp.where(allowed_of(batch), scores, NEGATIVE)
        highest = jnp.max(scores, axis=-1, keepdims=True)
        exp_part = jnp.exp(scores - highest)
        exp_total = jnp.sum(exp_part, axis=-1, keepdims=True)
        log_total = highest + jnp.log(exp_total)
        probs = (exp_part / exp_total).astype(BF16)
        mixed = jnp.einsum("kgqt,kdt->qkgd", probs, v, preferred_element_type=F32)
        mixed_parts.append(mixed.reshape(ROWS, H * HD).astype(BF16))
        kept.append((q, k, v, log_total))
    o_pad = dot(jnp.concatenate(mixed_parts), features, 1, 0).astype(BF16)
    x1 = x0 + dot(o_pad, wo, 1, 1)

    b = rms_norm(x1, gains[1]).astype(BF16)
    gate_up = dot(b, wg, 1, 1)
    activated = gated(gate_up).astype(BF16)
    x2 = x1 + dot(activated, wd, 1, 0)

    final = rms_norm(x2, gains[2]).astype(BF16)
    own_offsets = (own_positions - wide * ROWS + jnp.arange(MB)[:, None] * ROWS).reshape(-1)
    all_rows = gather_rows(final[own_offsets]).reshape(4096, DP)
    logits = dot(all_rows, table_low, 1, 1)
    vocab_start = (wide * 16 + narrow) * 384
    hit = jnp.arange(384)[None, :] == (all_targets - vocab_start)[:, None]
    highest = jnp.max(logits, axis=-1)
    exp_total = jnp.sum(jnp.exp(logits - highest[:, None]), axis=-1)
    stats = jnp.stack([highest.reshape(32, 128), exp_total.reshape(32, 128)])
    log_total = small_all(stats, combine_stats, log_of_stats, (32, 128), 4, "row_totals")
    log_total = log_total.reshape(4096)
    hit_sum = jnp.sum(jnp.where(hit, logits, 0.0) * all_counted[:, None])
    logit_sum = jnp.sum(logits * all_counted[:, None])
    token_count = jnp.sum(all_counted)
    loss_known = jnp.sum(all_counted * (log_total + ZLOSS_WEIGHT * log_total * log_total))
    d_logits = (
        all_counted[:, None]
        * (
            (1.0 + 2.0 * ZLOSS_WEIGHT * log_total)[:, None] * jnp.exp(logits - log_total[:, None])
            - (1.0 - SMOOTH) * hit.astype(F32)
            - SMOOTH / V
        )
    ).astype(BF16)
    table_grad_rows = dot(d_logits, all_rows, 0, 0)
    d_by_core = d_logits.reshape(64, 2, 32, 384)
    d_mine = lax.dynamic_index_in_dim(d_by_core, core, 1, keepdims=False).reshape(2048, 384)
    d_theirs = lax.dynamic_index_in_dim(d_by_core, 1 - core, 1, keepdims=False).reshape(2048, 384)
    d_theirs = partner(d_theirs)
    row_part = dot(d_mine, table_low, 1, 0) + dot(d_theirs, table_other, 1, 0)
    d_rows = scatter_rows(row_part.astype(BF16).reshape(4, 4, 4, 32, DP))

    d_final = jnp.zeros((rows_count, DP), F32).at[own_offsets].add(d_rows)
    d_x2, d_gain_final = jax.vjp(rms_norm, x2, gains[2])[1](d_final)
    d_branch = d_x2.astype(BF16)
    d_activated = dot(d_branch, wd, 1, 1)
    d_gate_up = jax.vjp(gated, gate_up)[1](d_activated)[0].astype(BF16)
    d_b = dot(d_gate_up, wg, 1, 0)
    d_x1_part, d_gain_mlp = jax.vjp(rms_norm, x1, gains[1])[1](d_b)
    d_x1 = d_x2 + d_x1_part
    d_out = d_x1.astype(BF16)
    d_mixed_pad = dot(d_out, wo, 1, 0).astype(BF16)
    d_mixed = dot(d_mixed_pad, features, 1, 1).astype(BF16)
    d_queries, d_kv = [], []
    for batch in range(MB):
        q, k, v, log_sum = kept[batch]
        d_m = d_mixed.reshape(MB, ROWS, KVH, group_size, HD)[batch]
        scores = jnp.einsum("qkgd,kdt->kgqt", q, k, preferred_element_type=F32) * scale_factor
        scores = jnp.where(allowed_of(batch), scores, NEGATIVE)
        probs = jnp.exp(scores - log_sum)
        d_probs = jnp.einsum("qkgd,kdt->kgqt", d_m, v, preferred_element_type=F32)
        d_scores = (
            probs * (d_probs - jnp.sum(probs * d_probs, axis=-1, keepdims=True))
        ).astype(BF16)
        d_q = jnp.einsum("kgqt,kdt->qkgd", d_scores, k, preferred_element_type=F32) * scale_factor
        d_k = jnp.einsum("kgqt,qkgd->kdt", d_scores, q, preferred_element_type=F32) * scale_factor
        d_v = jnp.einsum(
            "kgqt,qkgd->kdt", probs.astype(BF16), d_m, preferred_element_type=F32
        )
        d_queries.append(d_q.reshape(ROWS, H, HD))
        d_kv.append((d_k.reshape(kv_width, SEQ), d_v.reshape(kv_width, SEQ)))
    d_kv_own = sum_keys([d_kv[0][0], d_kv[1][0], d_kv[0][1], d_kv[1][1]])
    d_kv_own = d_kv_own.swapaxes(1, 2).reshape(2, rows_count, kv_width)

    def unrotate(gradient, heads):
        primal = jnp.zeros((rows_count, heads, HD), F32)
        return jax.vjp(lambda values: rotate(values, places_all), primal)[1](gradient)[0]

    d_projected = jnp.concatenate(
        [
            unrotate(jnp.concatenate(d_queries), H).reshape(rows_count, H * HD),
            unrotate(d_kv_own[0].reshape(rows_count, KVH, HD), KVH).reshape(
                rows_count, kv_width
            ),
            d_kv_own[1],
        ],
        axis=1,
    ).astype(BF16)
    d_a = dot(d_projected, wi, 1, 0)
    d_x0_part, d_gain_attn = jax.vjp(rms_norm, x0, gains[0])[1](d_a)
    d_x0 = (d_x1 + d_x0_part).astype(BF16)

    def half_pair(value):
        mine = lax.dynamic_slice_in_dim(value, core * 512, 512, axis=1)
        theirs = lax.dynamic_slice_in_dim(value, (1 - core) * 512, 512, axis=1)
        return jnp.concatenate([mine, partner(theirs)])

    def both(value):
        return jnp.concatenate([value, partner(value)])

    d_projected_pad = dot(d_projected, columns, 1, 0).astype(BF16)
    grad_wd = dot(both(activated), half_pair(d_branch), 0, 0).astype(BF16)
    grad_wg = dot(both(d_gate_up), half_pair(b), 0, 0).astype(BF16)
    grad_wo = dot(both(d_out), half_pair(o_pad), 0, 0).astype(BF16)
    grad_wi = dot(both(d_projected_pad), half_pair(a), 0, 0).astype(BF16)
    table_grad, summed_grads = scatter_grads(
        d_x0,
        ordered[None, :],
        grad_wi.reshape(4, 4, RI, 512),
        grad_wo.reshape(2, 4, 2, RO, 512),
        grad_wg.reshape(2, 2, 2, 4, 160, 512),
        grad_wd.reshape(2, 4, 2, 160, 512),
    )
    grad_shards = (
        jnp.concatenate([summed_grads[1, 160:224], summed_grads[2, 160:208]]),
        summed_grads[0, 160:224],
        jnp.concatenate([summed_grads[0, :160], summed_grads[1, :160]]),
        summed_grads[2, :160],
    )

    table_grad = dot(table_grad + table_grad_rows, features, 1, 1, HIGHEST)

    squares = sum(jnp.sum(shard * shard) for shard in grad_shards) + jnp.sum(
        table_grad * table_grad
    )
    gain_grads = jnp.stack([d_gain_attn, d_gain_mlp, d_gain_final]).reshape(24, 128)
    scalars = jnp.pad(jnp.stack([squares, hit_sum, logit_sum]), (0, 125))
    packed = jnp.pad(jnp.concatenate([gain_grads, scalars[None]]), ((0, 7), (0, 0)))
    summed = small_all(packed, jnp.add, lambda v: v, (32, 128), 5, "global_sums")
    gain_grad = dot(summed[:24].reshape(3, DP), features, 1, 1, HIGHEST)
    loss_total = loss_known - (1.0 - SMOOTH) * summed[24, 1] - SMOOTH / V * summed[24, 2]
    grad_norm = jnp.sqrt(summed[24, 0] + jnp.sum(gain_grad * gain_grad)) / token_count
    factor = jnp.minimum(1.0, CLIP_NORM / grad_norm) / token_count

    new_shards = [
        MOMENTUM * to_shard(moment, rows) + factor * grad
        for moment, rows, grad in zip(moments, (RI, RO, RG, RD), grad_shards)
    ]
    pieces = jnp.stack([jnp.pad(s, ((0, 320 - s.shape[0]), (0, 0))) for s in new_shards])
    turned, gram = gram_of(pieces)
    gram = gram.reshape(DP, DP)
    turned = lax.dynamic_slice_in_dim(turned, core * 160, 160)
    norm = jnp.sqrt(jnp.trace(gram)) + 1e-07
    current = turned / norm
    gram = gram / norm / norm
    identity = jnp.eye(DP, dtype=F32)
    for ns_step in range(ITERS):
        if ns_step < ITERS - 1:
            fine = HIGHEST if ns_step == 0 else HIGH
            square = dot(gram, gram, 1, 0, fine)
            step_matrix = NS_A * identity + NS_B * gram + NS_C * square
            current = dot(current, step_matrix, 1, 0, HIGH)
            gram = dot(dot(step_matrix, gram, 1, 0, fine), step_matrix, 1, 0, fine)
        else:
            applied = dot(current, gram, 1, 0, HIGH)
            current = NS_A * current + NS_B * applied + NS_C * dot(applied, gram, 1, 0, HIGH)
    pieces = current.reshape(160, 2, 4, 128).transpose(2, 1, 0, 3).reshape(8, 160, 128)
    pieces = lax.all_to_all(pieces, "wide", split_axis=0, concat_axis=0)
    pieces = pieces.reshape(4, 320, 128)
    new_moments, new_weights = [], []
    for kind, rows in enumerate((RI, RO, RG, RD)):
        count = masters[kind].shape[1]
        ortho = pieces[kind, :rows]
        new_moments.append(from_shard(new_shards[kind], count)[None])
        new_weights.append(
            (
                masters[kind] * (1.0 - MUON_RATE * WEIGHT_DECAY)
                - MUON_RATE * 0.2 * math.sqrt(count * 16) * from_shard(ortho, count)
            )[None]
        )
    table_m, table_v, table_new = adam_update(
        embed_table, table_first, table_second, factor * table_grad, TABLE_RATE, WEIGHT_DECAY
    )
    gains_m, gains_v, gains_new = adam_update(
        norm_gains, gains_first, gains_second, factor * gain_grad, GAIN_RATE, 0.0
    )
    return (
        loss_total,
        token_count,
        grad_norm,
        *new_moments,
        *new_weights,
        *[weight.astype(BF16) for weight in new_weights],
        table_m,
        table_v,
        table_new,
        table_new.astype(BF16),
        gains_m,
        gains_v,
        gains_new,
    )


def solution(mesh):
    whole = P()
    by_sequence = P(None, "narrow", None)
    matrix = P(None, "wide", "narrow")
    table = P(("wide", "narrow"), None)
    return jax.shard_map(
        body,
        mesh=mesh,
        in_specs=(
            (by_sequence, by_sequence, P(None, "narrow"), by_sequence)
            + (matrix,) * 4
            + (whole, table)
            + (matrix,) * 4
            + (table, table, whole, whole)
        ),
        out_specs=(whole,) * 3 + (matrix,) * 12 + (table,) * 4 + (whole,) * 3,
        check_vma=False,
    )
```

```python
import functools
import math

import jax
import jax.numpy as jnp
from jax import lax
from jax.experimental import pallas as pl
from jax.experimental.pallas import tpu as pltpu
from jax.sharding import PartitionSpec as P

D = 960
H = 15
KVH = 5
HD = 64
FF = 2560
V = 49152
QKV = 1600
ITERS = 5
STEP = 10
MB = 2
SEQ = 1024
ROWS = 128
PICK = 16
DP = 1024

NORM_EPS = 1e-05
ROPE_THETA = 100000.0
SMOOTH = 0.1
ZLOSS_WEIGHT = 0.0001
CLIP_NORM = 0.02
MOMENTUM = 0.95
NS_A = 3.4445
NS_B = -4.775
NS_C = 2.0315
MUON_RATE = 0.1
WEIGHT_DECAY = 0.1
BETA_ONE = 0.9
BETA_TWO = 0.95
TABLE_RATE = 0.03
GAIN_RATE = 0.4
ADAM_EPS = 1e-08
NEGATIVE = -1e30

HIGHEST = lax.Precision.HIGHEST
HIGH = lax.Precision.HIGH
F32 = jnp.float32
BF16 = jnp.bfloat16
MESH = pl.DeviceIdType.MESH
ANY = pl.BlockSpec(memory_space=pl.ANY)
VMEM = pl.BlockSpec(memory_space=pltpu.VMEM)

RI, RO, RG, RD = 112, 64, 320, 160


def my_place():
    wide = lax.axis_index("wide")
    narrow = lax.axis_index("narrow")
    return {
        "y": lax.div(wide, 2),
        "c": lax.rem(wide, 2),
        "z": lax.div(narrow, 4),
        "x": lax.rem(narrow, 4),
    }


def device(place):
    return (place["y"] * 2 + place["c"], place["z"] * 4 + place["x"])


def at_step(place, axis, step):
    return {**place, axis: lax.rem(place[axis] + step, 4)}


def other_core(place):
    return {**place, "c": 1 - place["c"]}


def greet(targets):
    barrier = pltpu.get_barrier_semaphore()
    for target in targets:
        pl.semaphore_signal(barrier, inc=1, device_id=device(target), device_id_type=MESH)
    pl.semaphore_wait(barrier, len(targets))


class Net:
    def __init__(self, send, recv):
        self.send = send
        self.recv = recv
        self.copies = []

    def put(self, src, dst, target):
        k = len(self.copies)
        copy = pltpu.make_async_remote_copy(
            src_ref=src,
            dst_ref=dst,
            send_sem=self.send.at[k],
            recv_sem=self.recv.at[k],
            device_id=device(target),
            device_id_type=MESH,
        )
        copy.start()
        self.copies.append(copy)
        return copy

    def finish(self):
        for copy in self.copies:
            copy.wait_send()


class Spread:
    def __init__(self, net, place, axes, items, with_core):
        self.net, self.place, self.axes, self.items = net, place, axes, items
        self.with_core = with_core
        self.sel = dict(place)
        self.phase = 0
        self.core = []

    def to_core(self, region, sel, half):
        if self.with_core and self.phase == len(self.axes) - 1:
            ref = region(sel, half)
            self.core.append(self.net.put(ref, ref, other_core(self.place)))

    def begin(self):
        self.axis = self.axes[self.phase]
        self.up, self.across, self.down = [at_step(self.place, self.axis, k) for k in (1, 2, 3)]
        self.first, self.second, self.onward = [], [], []
        for group, first_half in ((self.first, 0), (self.second, 1)):
            for region, halves in self.items:
                for target, origin, half in (
                    (self.up, self.down, first_half),
                    (self.down, self.up, 1 - first_half),
                ):
                    if halves[half] is not None:
                        ref = region(self.sel, halves[half])
                        copy = self.net.put(ref, ref, target)
                        group.append((copy, origin, target, region, halves[half]))
        for region, halves in self.items:
            for half in halves:
                if half is not None:
                    self.to_core(region, self.sel, half)

    def relay(self):
        for copy, origin, target, region, half in self.first:
            copy.wait_recv()
            sel = {**self.sel, self.axis: origin[self.axis]}
            ref = region(sel, half)
            self.onward.append((self.net.put(ref, ref, target), region, half))
            self.to_core(region, sel, half)

    def near(self):
        for copy, origin, _, region, half in self.second:
            copy.wait_recv()
            self.to_core(region, {**self.sel, self.axis: origin[self.axis]}, half)

    def far(self):
        for copy, region, half in self.onward:
            copy.wait_recv()
            self.to_core(region, {**self.sel, self.axis: self.across[self.axis]}, half)
        self.sel[self.axis] = None
        self.phase += 1

    def end(self):
        for copy in self.core:
            copy.wait_recv()


def gather_streams(net, place, streams, with_core):
    spreads = [Spread(net, place, axes, items, with_core) for axes, items in streams]
    for _ in range(len(streams[0][0])):
        for step in ("begin", "relay", "near", "far"):
            for spread in spreads:
                getattr(spread, step)()
    for spread in spreads:
        spread.end()


def pick(index):
    return slice(None) if index is None else index


def lanes_of(sel):
    if sel["y"] is None:
        return pl.ds(pl.multiple_of(sel["c"] * 512, 512), 512)
    return pl.ds(pl.multiple_of((sel["c"] * 4 + sel["y"]) * 128, 128), 128)


def halved(low, high):
    cut = low + (high - low) // 32 * 16
    return ((low, cut - low), (cut, high - cut))


def neighbours(place, axes=("x", "y", "z"), core=True):
    found = [at_step(place, axis, step) for axis in axes for step in (1, 3)]
    return found + ([other_core(place)] if core else [])


def fetch_kernel(
    gi, go, gg, gd, meta, table, ids, wi, wo, wg, wd, info, x0, *scratch
):
    slab, packed, theirs, got, send, recv, local = scratch
    place = my_place()

    def in_wi(sel, rows):
        return wi.at[pick(sel["z"]), pick(sel["x"]), pl.ds(*rows), lanes_of(sel)]

    def in_wo(sel, rows):
        z, x = sel["z"], sel["x"]
        xh, xl = (None, None) if x is None else (lax.div(x, 2), lax.rem(x, 2))
        return wo.at[pick(xh), pick(z), pick(xl), pl.ds(*rows), lanes_of(sel)]

    def in_wg(half):
        def region(sel, rows):
            z, x = sel["z"], sel["x"]
            zh, zl = (None, None) if z is None else (lax.div(z, 2), lax.rem(z, 2))
            return wg.at[pick(zh), half, pick(zl), pick(x), pl.ds(*rows), lanes_of(sel)]

        return region

    def in_wd(sel, rows):
        z, x = sel["z"], sel["x"]
        xh, xl = (None, None) if x is None else (lax.div(x, 2), lax.rem(x, 2))
        return wd.at[pick(xl), pick(z), pick(xh), pl.ds(*rows), lanes_of(sel)]

    def in_info(sel, rows):
        return info.at[pick(sel["z"]), pick(sel["x"]), pick(sel["y"]), sel["c"], :, :]

    owns = [
        (gi, in_wi(place, (0, RI))),
        (go, in_wo(place, (0, RO))),
        (gg.at[pl.ds(0, 160)], in_wg(0)(place, (0, 160))),
        (gg.at[pl.ds(160, 160)], in_wg(1)(place, (0, 160))),
        (gd, in_wd(place, (0, RD))),
        (meta, in_info(place, None)),
        (table.at[pl.ds(0, 192)], slab.at[pl.ds((place["z"] * 4 + place["x"]) * 192, 192)]),
        (table.at[pl.ds(192, 192)], slab.at[pl.ds((16 + place["x"] * 4 + place["z"]) * 192, 192)]),
    ]
    copies = [pltpu.make_async_copy(src, dst, local.at[k]) for k, (src, dst) in enumerate(owns)]
    for copy in copies:
        copy.start()
    for copy in copies:
        copy.wait()
    greet(neighbours(place))
    net = Net(send, recv)
    slab[pl.ds(6144, 8)] = jnp.zeros((8, 8, 128), BF16)

    def in_slab(major, minor, first):
        def region(sel, half):
            start = (first + sel[major] * 4) * 192
            if sel[minor] is None:
                return slab.at[pl.ds(start + half * 384, 384)]
            return slab.at[pl.ds(start + sel[minor] * 192 + half * 96, 96)]

        return region

    tables = [
        Spread(net, place, ("x", "z"), [(in_slab("z", "x", 0), (0, 1))], False),
        Spread(net, place, ("z", "x"), [(in_slab("x", "z", 16), (0, 1))], False),
    ]
    weights = [
        Spread(net, place, axes, items, True)
        for axes, items in (
            (("x", "z", "y"), [(in_wg(0), halved(0, 160)), (in_wo, halved(0, 64))]),
            (("z", "x", "y"), [(in_wg(1), halved(0, 160)), (in_wi, halved(0, 64))]),
            (
                ("y", "z", "x"),
                [(in_wd, halved(0, 160)), (in_wi, halved(64, 112)), (in_info, ((0, 8), None))],
            ),
        )
    ]

    def each(spreads, *steps):
        for step in steps:
            for spread in spreads:
                getattr(spread, step)()

    each(tables, "begin")
    each(weights, "begin")
    each(tables, "relay")
    each(weights, "relay")
    each(tables, "near", "far", "begin")
    each(weights, "near", "far", "begin")
    each(tables, "relay")
    each(weights, "relay", "near", "far", "begin")
    each(tables, "near", "far")

    @pl.loop(0, 128)
    def _(block):
        for k in range(16):
            token = block * 16 + k
            packed[token] = slab[ids[token]]

    swap = net.put(
        packed.at[pl.ds((1 - place["c"]) * 1024, 1024)], theirs, other_core(place)
    )
    each(weights, "relay")
    swap.wait_recv()
    add_up(theirs, [packed.at[pl.ds(place["c"] * 1024, 1024)], theirs])
    ring = Ring(
        net,
        place,
        "y",
        lambda k, half: theirs.at[pl.ds(k * 256 + half * 128, 128)],
        lambda k: got.at[k],
        lambda half: x0.at[pl.ds(half * 128, 128)],
    )
    ring.send_all()
    each(weights, "near")
    ring.pass_on()
    each(weights, "far")
    ring.close()
    each(weights, "end")
    net.finish()


def fetch(gi, go, gg, gd, meta, table, ids):
    shapes = [
        jax.ShapeDtypeStruct((4, 4, RI, DP), BF16),
        jax.ShapeDtypeStruct((2, 4, 2, RO, DP), BF16),
        jax.ShapeDtypeStruct((2, 2, 2, 4, 160, DP), BF16),
        jax.ShapeDtypeStruct((2, 4, 2, 160, DP), BF16),
        jax.ShapeDtypeStruct((4, 4, 4, 2, 8, 128), jnp.int32),
        jax.ShapeDtypeStruct((256, 8, 128), BF16),
    ]
    count = 202
    return pl.pallas_call(
        fetch_kernel,
        out_shape=shapes,
        in_specs=[ANY] * 6 + [pl.BlockSpec(memory_space=pltpu.SMEM)],
        out_specs=[ANY] * 5 + [VMEM],
        scratch_shapes=[
            pltpu.VMEM((6152, 8, 128), BF16),
            pltpu.VMEM((2048, 8, 128), BF16),
            pltpu.VMEM((1024, 8, 128), BF16),
            pltpu.VMEM((6, 128, 8, 128), BF16),
            pltpu.SemaphoreType.DMA((count,)),
            pltpu.SemaphoreType.DMA((count,)),
            pltpu.SemaphoreType.DMA((8,)),
        ],
        compiler_params=pltpu.CompilerParams(
            collective_id=0, has_side_effects=True, vmem_limit_bytes=56 << 20
        ),
        name="fetch",
    )(gi, go, gg, gd, meta, table, ids)


LANE_PARTS = ((0, 384), (384, 384), (768, 256))
ORDERS = (("x", "z", "y"), ("z", "y", "x"), ("y", "x", "z"))


def rows_kernel(own, rows, send, recv, local):
    place = my_place()
    greet(neighbours(place))

    def in_rows(lanes):
        def region(sel, part):
            return rows.at[
                pick(sel["z"]), pick(sel["x"]), pick(sel["y"]), sel["c"], pl.ds(*part), pl.ds(*lanes)
            ]

        return region

    copy = pltpu.make_async_copy(
        own, rows.at[place["z"], place["x"], place["y"], place["c"]], local
    )
    copy.start()
    copy.wait()
    streams = [
        (axes, [(in_rows(lanes), ((0, 16), (16, 16)))]) for axes, lanes in zip(ORDERS, LANE_PARTS)
    ]
    net = Net(send, recv)
    gather_streams(net, place, streams, True)
    net.finish()


def gather_rows(own):
    count = 90
    return pl.pallas_call(
        rows_kernel,
        out_shape=jax.ShapeDtypeStruct((4, 4, 4, 2, 32, DP), BF16),
        in_specs=[VMEM],
        out_specs=VMEM,
        scratch_shapes=[
            pltpu.SemaphoreType.DMA((count,)),
            pltpu.SemaphoreType.DMA((count,)),
            pltpu.SemaphoreType.DMA,
        ],
        compiler_params=pltpu.CompilerParams(
            collective_id=1, has_side_effects=True, vmem_limit_bytes=24 << 20
        ),
        name="gather_rows",
    )(own)


def small_kernel(combine, last, own, out, held, narrow_slots, wide_slots, send, recv):
    place = my_place()
    plane = [
        at_step(at_step(place, "z", k // 4), "x", k % 4) for k in range(1, 16)
    ]
    column = [
        {**at_step(place, "y", k // 2), "c": lax.rem(place["c"] + k % 2, 2)} for k in range(1, 8)
    ]
    greet(plane + column)
    net = Net(send, recv)
    value = own
    for number, (slots, index, targets) in enumerate(
        (
            (narrow_slots, place["z"] * 4 + place["x"], plane),
            (wide_slots, place["y"] * 2 + place["c"], column),
        )
    ):
        copies = [net.put(value, slots.at[index], target) for target in targets]
        slots[index] = value[...]
        for copy in copies:
            copy.wait_recv()
        total = slots[0]
        for k in range(1, slots.shape[0]):
            total = combine(total, slots[k])
        if number == 0:
            held[...] = total
            value = held
    out[...] = last(total)
    net.finish()


def small_all(value, combine, last, out_shape, collective_id, name):
    shape = value.shape
    count = 22
    return pl.pallas_call(
        functools.partial(small_kernel, combine, last),
        out_shape=jax.ShapeDtypeStruct(out_shape, F32),
        in_specs=[VMEM],
        out_specs=VMEM,
        scratch_shapes=[
            pltpu.VMEM(shape, F32),
            pltpu.VMEM((16,) + shape, F32),
            pltpu.VMEM((8,) + shape, F32),
            pltpu.SemaphoreType.DMA((count,)),
            pltpu.SemaphoreType.DMA((count,)),
        ],
        compiler_params=pltpu.CompilerParams(collective_id=collective_id, has_side_effects=True),
        name=name,
    )(value)


def combine_stats(one, two):
    highest = jnp.maximum(one[0], two[0])
    total = one[1] * jnp.exp(one[0] - highest) + two[1] * jnp.exp(two[0] - highest)
    return jnp.stack([highest, total])


def log_of_stats(stats):
    return stats[0] + jnp.log(stats[1])


def add_up(dst, parts):
    if len(dst.shape) == 3:
        step = max(1, min(dst.shape[0], 32768 // (dst.shape[1] * dst.shape[2])))

        @pl.loop(0, dst.shape[0] // step)
        def _(k):
            block = pl.ds(k * step, step)
            total = parts[0][block].astype(F32)
            for part in parts[1:]:
                total = total + part[block].astype(F32)
            dst[block] = total.astype(dst.dtype)

        return
    total = parts[0][...].astype(F32)
    for part in parts[1:]:
        total = total + part[...].astype(F32)
    dst[...] = total.astype(dst.dtype)


class Ring:
    def __init__(self, net, place, axis, source, got, result):
        self.net, self.source, self.got, self.result = net, source, got, result
        steps = [at_step(place, axis, step) for step in range(4)]
        self.own, self.up, self.across, self.down = [step[axis] for step in steps]
        self.to_up, self.to_down = steps[1], steps[3]

    def send_across(self):
        self.far_up = self.net.put(self.source(self.across, 0), self.got(0), self.to_up)
        self.far_down = self.net.put(self.source(self.across, 1), self.got(1), self.to_down)

    def send_up(self):
        self.near_up = self.net.put(self.source(self.up, 1), self.got(2), self.to_up)

    def send_down(self):
        self.near_down = self.net.put(self.source(self.down, 0), self.got(3), self.to_down)

    def send_all(self):
        self.send_across()
        self.send_up()
        self.send_down()

    def pass_on(self):
        self.far_up.wait_recv()
        add_up(self.got(0), [self.source(self.up, 0), self.got(0)])
        self.on_up = self.net.put(self.got(0), self.got(4), self.to_up)
        self.far_down.wait_recv()
        add_up(self.got(1), [self.source(self.down, 1), self.got(1)])
        self.on_down = self.net.put(self.got(1), self.got(5), self.to_down)

    def close(self):
        for copy in (self.near_up, self.near_down, self.on_up, self.on_down):
            copy.wait_recv()
        add_up(self.result(0), [self.source(self.own, 0), self.got(4), self.got(3)])
        add_up(self.result(1), [self.source(self.own, 1), self.got(2), self.got(5)])


FAR_FIRST = (2, 1, 3, 0)


def start_scatter(net, place, order, source, gots, out, acc=None):
    rows = out.shape[0] // 2
    halves = (pl.ds(0, rows), pl.ds(rows, rows))
    lead = ("z", "x", "y")[: len(order)]

    def block(sel, half):
        return source.at[tuple(pick(sel.get(axis)) for axis in lead) + (halves[half],)]

    def summed(sel, half):
        if acc is None:
            return block({order[0]: place[order[0]], **sel}, half)
        return acc.at[tuple(pick(sel.get(axis)) for axis in order[1:]) + (halves[half],)]

    stream = {"first": {}, "rest": []}
    one, two = order[:2]
    for sub, far in enumerate(FAR_FIRST):
        at_two = at_step(place, two, far)[two]
        stream["first"][far] = Ring(
            net,
            place,
            one,
            lambda k, half, at_two=at_two: block({one: k, two: at_two}, half),
            lambda k, sub=sub: gots[0].at[sub, k],
            lambda half, at_two=at_two: summed({two: at_two}, half),
        )
    for number in range(1, len(order)):
        done = {axis: place[axis] for axis in order[1:number]}

        def part(k, half, done=done, axis=order[number]):
            return summed({**done, axis: k}, half)

        if number + 1 < len(order):
            result = lambda half, part=part, axis=order[number]: part(place[axis], half)
        else:
            result = lambda half: out.at[halves[half]]
        stream["rest"].append(
            Ring(net, place, order[number], part, lambda k, n=number: gots[n].at[k], result)
        )
    return stream


def send_first(streams):
    for far in FAR_FIRST:
        for stream in streams:
            stream["first"][far].send_across()
    for far in FAR_FIRST:
        for stream in streams:
            stream["first"][far].send_up()
            stream["first"][far].send_down()


def finish_scatter(streams, passed=False):
    if not passed:
        for far in FAR_FIRST:
            for stream in streams:
                stream["first"][far].pass_on()
    for far in FAR_FIRST:
        for stream in streams:
            stream["first"][far].close()
            following = stream["rest"][0]
            if far == 2:
                following.send_across()
            if far == 1:
                following.send_up()
            if far == 3:
                following.send_down()
    for number in range(max(len(stream["rest"]) for stream in streams)):
        active = [stream["rest"] for stream in streams if number < len(stream["rest"])]
        for rest in active:
            rest[number].pass_on()
        for rest in active:
            rest[number].close()
            if number + 1 < len(rest):
                rest[number + 1].send_all()


def got_shapes(depth, rows, lanes, first, later):
    half = rows // 2
    return [
        pltpu.VMEM(
            ((4, 6) if number == 0 else (6,)) + (4,) * (depth - max(number, 1) - 1) + (half, lanes),
            later if number else first,
        )
        for number in range(depth)
    ]


def row_sums_kernel(part, out, *scratch):
    held = scratch[0:3]
    accs = scratch[12:15]
    send, recv, local = scratch[15:]
    place = my_place()
    copies = [
        pltpu.make_async_copy(part.at[:, :, :, :, pl.ds(*lanes)], held[k], local.at[k])
        for k, lanes in enumerate(LANE_PARTS)
    ]
    for copy in copies:
        copy.start()
    greet(neighbours(place, core=False))
    for copy in copies:
        copy.wait()
    net = Net(send, recv)
    streams = [
        start_scatter(
            net,
            place,
            order,
            held[k],
            scratch[3 + 3 * k : 6 + 3 * k],
            out.at[:, pl.ds(*lanes)],
            accs[k],
        )
        for k, (order, lanes) in enumerate(zip(ORDERS, LANE_PARTS))
    ]
    send_first(streams)
    finish_scatter(streams)
    net.finish()


def scatter_rows(part):
    scratch = [pltpu.VMEM((4, 4, 4, 32, lanes), part.dtype) for _, lanes in LANE_PARTS]
    for _, lanes in LANE_PARTS:
        scratch += got_shapes(3, 32, lanes, part.dtype, F32)
    scratch += [pltpu.VMEM((4, 4, 32, lanes), F32) for _, lanes in LANE_PARTS]
    scratch += [
        pltpu.SemaphoreType.DMA((108,)),
        pltpu.SemaphoreType.DMA((108,)),
        pltpu.SemaphoreType.DMA((3,)),
    ]
    return pl.pallas_call(
        row_sums_kernel,
        out_shape=jax.ShapeDtypeStruct((32, DP), F32),
        in_specs=[ANY],
        out_specs=VMEM,
        scratch_shapes=scratch,
        compiler_params=pltpu.CompilerParams(
            collective_id=3, has_side_effects=True, vmem_limit_bytes=40 << 20
        ),
        name="scatter_rows",
    )(part)


GRAD_ORDERS = (("y", "x", "z"), ("y", "z", "x"), ("x", "z", "y"))


def grads_kernel(dx, ids, di, do, dg, dd, out, weights_out, *scratch):
    rows, table, chosen = scratch[:3]
    held = scratch[3:6]
    gots = scratch[6:10]
    weight_gots = scratch[10:19]
    accs = scratch[19:22]
    send, recv, local = scratch[22:]
    place = my_place()
    moves = [(dx, rows.at[place["y"], place["c"]])]
    for y in range(4):
        lanes = pl.ds(y * 128, 128)
        for z in range(4):
            for half in range(2):
                moves.append(
                    (
                        dg.at[z // 2, half, z % 2, :, :, lanes],
                        held[half].at[z, :, y, pl.ds(0, 160)],
                    )
                )
        for x in range(4):
            moves.append((dd.at[x % 2, :, x // 2, :, lanes], held[2].at[:, x, y, pl.ds(0, 160)]))
            moves.append((do.at[x // 2, :, x % 2, :, lanes], held[0].at[:, x, y, pl.ds(160, 64)]))
        for z in range(4):
            moves.append((di.at[z, :, pl.ds(0, 64), lanes], held[1].at[z, :, y, pl.ds(160, 64)]))
            moves.append((di.at[z, :, pl.ds(64, 48), lanes], held[2].at[z, :, y, pl.ds(160, 48)]))
    copies = [pltpu.make_async_copy(src, dst, local.at[k]) for k, (src, dst) in enumerate(moves)]
    for copy in copies:
        copy.start()
    held[2][:, :, :, 208:224, :] = jnp.zeros((4, 4, 4, 16, 128), BF16)
    greet(neighbours(place))
    copies[0].wait()

    def in_rows(sel, part):
        return rows.at[pick(sel["y"]), sel["c"], pl.ds(*part)]

    net = Net(send, recv)
    spread = Spread(net, place, ("y",), [(in_rows, ((0, 128), (128, 128)))], True)
    spread.begin()
    for copy in copies[1:]:
        copy.wait()
    weight_streams = [
        start_scatter(
            net, place, order, held[k], weight_gots[3 * k : 3 * k + 3], weights_out.at[k], accs[k]
        )
        for k, order in enumerate(GRAD_ORDERS)
    ]
    send_first(weight_streams[2:])
    spread.relay()
    spread.near()
    spread.far()
    send_first(weight_streams[:2])
    spread.end()
    base = (place["y"] * 2 + place["c"]) * 16

    def parts(count, place_of):
        @pl.loop(0, count)
        def _(k):
            z, x = place_of(k)
            start = (base + z * 4 + x) * 384

            @pl.loop(0, 24)
            def _(r):
                row = pl.multiple_of(r * 16, 16)
                number = lax.broadcasted_iota(jnp.int32, (16, 2048), 0) + (start + row)
                chosen[pl.ds(row, 16), :] = (number == ids[...]).astype(F32).astype(BF16)

            @pl.loop(0, 4)
            def _(l):
                lanes = pl.ds(pl.multiple_of(l * 256, 256), 256)
                values = rows[:, :, :, lanes].reshape(2048, 256)
                total = jnp.dot(chosen[...], values, preferred_element_type=F32)
                table[z, x, :, lanes] = total.astype(BF16)

    def further(axis, step):
        return lax.rem(place[axis] + step, 4)

    streams = [
        start_scatter(
            net,
            place,
            order,
            table.at[:, :, pl.ds(192 * k, 192)],
            gots[2 * k : 2 * k + 2],
            out.at[pl.ds(192 * k, 192)],
        )
        for k, order in enumerate((("x", "z"), ("z", "x")))
    ]
    by_x, by_z = streams[0]["first"], streams[1]["first"]
    parts(4, lambda k: (further("z", 2), further("x", k + 2)))
    for step in FAR_FIRST:
        by_z[step].send_across()
    by_x[2].send_across()
    parts(3, lambda k: (further("z", k + 3), further("x", 2)))
    for step in (1, 3, 0):
        by_x[step].send_across()
    by_x[2].send_up()
    by_x[2].send_down()
    by_z[2].send_up()
    by_z[2].send_down()
    for step in FAR_FIRST:
        weight_streams[2]["first"][step].pass_on()
    parts(9, lambda k: (further("z", lax.div(k, 3) + 3), further("x", lax.rem(k, 3) + 3)))
    for step in (1, 3, 0):
        by_x[step].send_up()
        by_x[step].send_down()
        by_z[step].send_up()
        by_z[step].send_down()
    for step in FAR_FIRST:
        for stream in streams + weight_streams[:2]:
            stream["first"][step].pass_on()
    finish_scatter(streams + weight_streams, passed=True)
    net.finish()


def scatter_grads(dx, ids, di, do, dg, dd):
    count = 3 * 36 + 2 * 30 + 16
    scratch = [
        pltpu.VMEM((4, 2, 256, DP), BF16),
        pltpu.VMEM((4, 4, 384, DP), BF16),
        pltpu.VMEM((384, 2048), BF16),
    ]
    scratch += [pltpu.VMEM((4, 4, 4, 224, 128), BF16)] * 3
    scratch += got_shapes(2, 192, DP, BF16, BF16) * 2
    scratch += got_shapes(3, 224, 128, BF16, F32) * 3
    scratch += [pltpu.VMEM((4, 4, 224, 128), F32)] * 3
    scratch += [
        pltpu.SemaphoreType.DMA((count,)),
        pltpu.SemaphoreType.DMA((count,)),
        pltpu.SemaphoreType.DMA((97,)),
    ]
    return pl.pallas_call(
        grads_kernel,
        out_shape=[
            jax.ShapeDtypeStruct((384, DP), F32),
            jax.ShapeDtypeStruct((3, 224, 128), F32),
        ],
        in_specs=[ANY, VMEM] + [ANY] * 4,
        out_specs=[VMEM, VMEM],
        scratch_shapes=scratch,
        compiler_params=pltpu.CompilerParams(
            collective_id=2, has_side_effects=True, vmem_limit_bytes=60 << 20
        ),
        name="scatter_grads",
    )(dx, ids, di, do, dg, dd)


def lanes_of_wide(y, c):
    return pl.ds(pl.multiple_of((y * 2 + c) * 128, 128), 128)


def keys_kernel(own, out, send, recv, local):
    place = my_place()
    copy = pltpu.make_async_copy(own, out.at[:, :, lanes_of_wide(place["y"], place["c"])], local)
    copy.start()
    greet(neighbours(place, ("y",)))
    copy.wait()

    def region(sel, rows):
        return out.at[:, pl.ds(*rows), lanes_of_wide(sel["y"], sel["c"])]

    net = Net(send, recv)
    gather_streams(net, place, [(("y",), [(region, ((0, 160), (160, 160)))])], True)
    net.finish()


def gather_keys(own):
    return pl.pallas_call(
        keys_kernel,
        out_shape=jax.ShapeDtypeStruct((4, 320, SEQ), BF16),
        in_specs=[VMEM],
        out_specs=VMEM,
        scratch_shapes=[
            pltpu.SemaphoreType.DMA((14,)),
            pltpu.SemaphoreType.DMA((14,)),
            pltpu.SemaphoreType.DMA,
        ],
        compiler_params=pltpu.CompilerParams(
            collective_id=6, has_side_effects=True, vmem_limit_bytes=16 << 20
        ),
        name="gather_keys",
    )(own)


def key_sums_kernel(*refs):
    parts, out = refs[:4], refs[4]
    theirs, held, got, send, recv = refs[5:]
    place = my_place()
    greet(neighbours(place, ("y",)))
    net = Net(send, recv)
    swaps = [
        [
            net.put(
                part.at[:, lanes_of_wide(at_step(place, "y", step)["y"], 1 - place["c"])],
                theirs.at[at_step(place, "y", step)["y"], k],
                other_core(place),
            )
            for k, part in enumerate(parts)
        ]
        for step in FAR_FIRST
    ]
    ring = Ring(
        net,
        place,
        "y",
        lambda k, half: held.at[k, pl.ds(2 * half, 2)],
        lambda k: got.at[k],
        lambda half: out.at[pl.ds(2 * half, 2)],
    )
    for step, swap in zip(FAR_FIRST, swaps):
        y = at_step(place, "y", step)["y"]
        for k, part in enumerate(parts):
            swap[k].wait_recv()
            own = part[:, lanes_of_wide(y, place["c"])]
            held[y, k] = (own + theirs[y, k]).astype(BF16)
        if step == 2:
            ring.send_across()
        if step == 1:
            ring.send_up()
        if step == 3:
            ring.send_down()
    ring.pass_on()
    ring.close()
    net.finish()


def sum_keys(parts):
    return pl.pallas_call(
        key_sums_kernel,
        out_shape=jax.ShapeDtypeStruct((4, 320, 128), F32),
        in_specs=[VMEM] * 4,
        out_specs=VMEM,
        scratch_shapes=[
            pltpu.VMEM((4, 4, 320, 128), F32),
            pltpu.VMEM((4, 4, 320, 128), BF16),
            pltpu.VMEM((6, 2, 320, 128), BF16),
            pltpu.SemaphoreType.DMA((22,)),
            pltpu.SemaphoreType.DMA((22,)),
        ],
        compiler_params=pltpu.CompilerParams(
            collective_id=8, has_side_effects=True, vmem_limit_bytes=32 << 20
        ),
        name="sum_keys",
    )(*parts)


def gram_kernel(pieces, turned, gram, part, *scratch):
    gots = scratch[:4]
    send, recv, local = scratch[4:]
    place = my_place()
    wides = [
        {**at_step(place, "y", step), "c": core}
        for step in (2, 1, 3, 0)
        for core in (place["c"], 1 - place["c"])
    ][:-2] + [other_core(place)]
    greet(wides + neighbours(place, ("x", "z"), False))
    net = Net(send, recv)

    def lanes_from(who):
        return pl.ds(pl.multiple_of((who["c"] * 4 + who["y"]) * 128, 128), 128)

    arrivals = [net.put(pieces.at[who["y"]], turned.at[:, lanes_from(place)], who) for who in wides]
    copy = pltpu.make_async_copy(pieces.at[place["y"]], turned.at[:, lanes_from(place)], local)
    copy.start()
    copy.wait()
    for arrival in arrivals:
        arrival.wait_recv()
    @pl.loop(0, 4)
    def _(k):
        rows = pl.ds(pl.multiple_of(place["c"] * 512 + k * 128, 128), 128)
        left = turned[:, rows].T
        for l in range(2):
            lanes = pl.ds(l * 512, 512)
            product = jnp.dot(left, turned[:, lanes], precision=HIGHEST, preferred_element_type=F32)
            for m in range(4):
                part[k, m, :, lanes] = product[m * 32 : m * 32 + 32]

    orders = (("x", "z"), ("z", "x"))
    lanes = (pl.ds(0, 512), pl.ds(512, 512))
    mine = gram.at[place["c"], place["z"], place["x"]]
    streams = [
        start_scatter(
            net, place, order, part.at[:, :, :, lane], gots[2 * k : 2 * k + 2], mine.at[:, lane]
        )
        for k, (order, lane) in enumerate(zip(orders, lanes))
    ]
    send_first(streams)
    finish_scatter(streams)

    def in_gram(lane):
        def region(sel, rows):
            return gram.at[sel["c"], pick(sel["z"]), pick(sel["x"]), pl.ds(*rows), lane]

        return region

    streams = [
        (order[::-1], [(in_gram(lane), ((0, 16), (16, 16)))]) for order, lane in zip(orders, lanes)
    ]
    gather_streams(net, place, streams, True)
    net.finish()


def gram_of(pieces):
    count = 7 + 2 * 30 + 44
    scratch = [pltpu.VMEM((4, 4, 32, DP), F32)]
    scratch += got_shapes(2, 32, 512, F32, F32) * 2
    scratch += [
        pltpu.SemaphoreType.DMA((count,)),
        pltpu.SemaphoreType.DMA((count,)),
        pltpu.SemaphoreType.DMA,
    ]
    return pl.pallas_call(
        gram_kernel,
        out_shape=[
            jax.ShapeDtypeStruct((320, DP), F32),
            jax.ShapeDtypeStruct((2, 4, 4, 32, DP), F32),
        ],
        in_specs=[VMEM],
        out_specs=[VMEM, VMEM],
        scratch_shapes=scratch,
        compiler_params=pltpu.CompilerParams(
            collective_id=7, has_side_effects=True, vmem_limit_bytes=40 << 20
        ),
        name="gram_sums",
    )(pieces)


def split(value, count):
    parts = []
    for _ in range(count):
        parts.append(value.astype(BF16))
        value = value - parts[-1].astype(F32)
    return parts


def product(left, right):
    count = len(left)
    total = None
    for order in range(count):
        for k in range(order + 1):
            term = jnp.dot(left[k], right[order - k], preferred_element_type=F32)
            total = term if total is None else total + term
    return total


def newton_kernel(gram, turned, out, power, *scratch):
    a_parts, q_parts, t_parts = scratch[0:3], scratch[3:6], scratch[6:8]

    def blocks(k):
        return pl.ds(pl.multiple_of(k * 256, 256), 256)

    def put(parts, i, j, value, count):
        for ref, part in zip(parts, split(value, count)):
            ref[blocks(i), blocks(j)] = part

    def mirrored(left, right, count, emit):
        @pl.loop(0, 10)
        def _(p):
            i = (p >= 4).astype(jnp.int32) + (p >= 7).astype(jnp.int32) + (p >= 9).astype(jnp.int32)
            j = p - lax.div(i * (7 - i), 2)
            value = product(
                [ref[blocks(i), :] for ref in left[:count]],
                [ref[:, blocks(j)] for ref in right[:count]],
            )
            emit(i, j, value)

    def diagonal(i, j):
        rows = lax.broadcasted_iota(jnp.int32, (256, 256), 0) + i * 256
        columns = lax.broadcasted_iota(jnp.int32, (256, 256), 1) + j * 256
        return rows == columns

    trace = jnp.zeros((), F32)
    for k in range(4):
        block = gram[k * 256 : (k + 1) * 256, k * 256 : (k + 1) * 256]
        trace = trace + jnp.sum(jnp.where(diagonal(0, 0), block, 0.0))
    scale = 1.0 / (jnp.sqrt(jnp.full((1, 1), trace, F32)) + 1e-07)

    @pl.loop(0, 16)
    def _(p):
        i, j = lax.div(p, 4), lax.rem(p, 4)
        value = gram[blocks(i), blocks(j)] * scale * scale
        power[blocks(i), blocks(j)] = value
        put(a_parts, i, j, value, 3)

    out[...] = turned[...] * scale

    for step in range(ITERS - 1):
        count = 3 if step == 0 else 2

        def emit_step(i, j, value):
            value = NS_B * power[blocks(i), blocks(j)] + NS_C * value
            value = value + jnp.where(diagonal(i, j), NS_A, 0.0)
            put(q_parts, i, j, value, count)
            put(q_parts, j, i, value.T, count)

        def emit_half(i, j, value):
            put(t_parts, i, j, value, 2)
            put(t_parts, j, i, value.T, 2)

        def emit_power(i, j, value):
            power[blocks(i), blocks(j)] = value
            put(a_parts, i, j, value, 2)
            put(a_parts, j, i, value.T, 2)

        mirrored(a_parts, a_parts, 2, emit_step)
        mirrored(q_parts, a_parts, count, emit_half)
        mirrored(t_parts, q_parts, 2, emit_power)
        current = split(out[...], 2)

        @pl.loop(0, 4)
        def _(j):
            out[:, blocks(j)] = product(current, [ref[:, blocks(j)] for ref in q_parts[:2]])

    current = split(out[...], 2)
    once = power

    @pl.loop(0, 4)
    def _(j):
        once[0:160, blocks(j)] = product(current, [ref[:, blocks(j)] for ref in a_parts[:2]])

    applied = split(once[0:160, :], 2)

    @pl.loop(0, 4)
    def _(j):
        twice = product(applied, [ref[:, blocks(j)] for ref in a_parts[:2]])
        out[:, blocks(j)] = (
            NS_A * out[:, blocks(j)] + NS_B * once[0:160, blocks(j)] + NS_C * twice
        )


def newton(gram, turned):
    return pl.pallas_call(
        newton_kernel,
        out_shape=jax.ShapeDtypeStruct((160, DP), F32),
        in_specs=[VMEM, VMEM],
        out_specs=VMEM,
        scratch_shapes=[pltpu.VMEM((DP, DP), F32)] + [pltpu.VMEM((DP, DP), BF16)] * 8,
        compiler_params=pltpu.CompilerParams(vmem_limit_bytes=48 << 20),
        name="newton",
    )(gram, turned)


def pad_features(values):
    lead = values.shape[:-1]
    blocks = values.reshape(lead + (4, 2, 2, 60))
    blocks = jnp.moveaxis(blocks, -3, -4)
    blocks = jnp.pad(blocks, [(0, 0)] * (len(lead) + 3) + [(0, 4)])
    return blocks.reshape(lead + (DP,))


def unpad_features(values):
    blocks = values.reshape(values.shape[0], 2, 4, 2, 64)[..., :60]
    return blocks.transpose(0, 2, 1, 3, 4).reshape(values.shape[0], D)


def feature_table():
    feature = lax.broadcasted_iota(jnp.int32, (D, DP), 0)
    place = lax.broadcasted_iota(jnp.int32, (D, DP), 1)
    wide, rest = feature // 120, feature % 120
    where = ((wide % 2) * 4 + wide // 2) * 128 + (rest // 60) * 64 + rest % 60
    return (where == place).astype(BF16)


def column_table():
    column = lax.broadcasted_iota(jnp.int32, (QKV, 16 * RI), 0)
    place = lax.broadcasted_iota(jnp.int32, (QKV, 16 * RI), 1)
    return ((column // 100) * RI + column % 100 == place).astype(BF16)


def to_shard(matrix, rows):
    columns = matrix.shape[1]
    turned = matrix.T.reshape(columns, 2, 60)
    turned = jnp.pad(turned, ((0, rows - columns), (0, 0), (0, 4)))
    return turned.reshape(rows, 128)


def from_shard(shard, columns):
    return shard[:columns].reshape(columns, 2, 64)[:, :, :60].reshape(columns, 120).T


def dot(left, right, left_axis, right_axis, precision=None):
    return lax.dot_general(
        left,
        right,
        (((left_axis,), (right_axis,)), ((), ())),
        preferred_element_type=F32,
        precision=precision,
    )


def rms_norm(values, gain_row):
    mean = jnp.sum(values * values, axis=-1, keepdims=True) * (1.0 / D)
    return values * lax.rsqrt(mean + NORM_EPS) * gain_row


def rotate(values, places):
    half_width = HD // 2
    frequency = ROPE_THETA ** (-2.0 * jnp.arange(half_width).astype(F32) / HD)
    angles = places.astype(F32)[:, None] * frequency[None, :]
    cosine = jnp.concatenate([jnp.cos(angles), jnp.cos(angles)], axis=-1)[:, None, :]
    sine_part = jnp.concatenate([jnp.sin(angles), jnp.sin(angles)], axis=-1)[:, None, :]
    turned = jnp.concatenate([-values[..., half_width:], values[..., :half_width]], axis=-1)
    return values * cosine + turned * sine_part


def gated(gate_up):
    return gate_up[:, :FF] * jax.nn.sigmoid(gate_up[:, :FF]) * gate_up[:, FF:]


def adam_update(weight, first_moment, second_moment, gradient, step_rate, decay_rate):
    first_new = BETA_ONE * first_moment + (1.0 - BETA_ONE) * gradient
    second_new = BETA_TWO * second_moment + (1.0 - BETA_TWO) * gradient * gradient
    update = (
        first_new
        / (1.0 - BETA_ONE**STEP)
        / (jnp.sqrt(second_new / (1.0 - BETA_TWO**STEP)) + ADAM_EPS)
    )
    return (first_new, second_new, weight * (1.0 - step_rate * decay_rate) - step_rate * update)


def partner(value):
    return lax.ppermute(value, "wide", [(k, k ^ 1) for k in range(8)])


def body(
    token_ids,
    target_ids,
    prefix_lengths,
    loss_positions,
    w_input,
    w_output,
    w_gate_up,
    w_down,
    norm_gains,
    embed_table,
    moment_input,
    moment_output,
    moment_gate_up,
    moment_down,
    table_first,
    table_second,
    gains_first,
    gains_second,
):
    wide = lax.axis_index("wide")
    narrow = lax.axis_index("narrow")
    core = wide % 2
    masters = (w_input[0], w_output[0], w_gate_up[0], w_down[0])
    moments = (moment_input[0], moment_output[0], moment_gate_up[0], moment_down[0])
    group_size = H // KVH
    kv_width = KVH * HD
    scale_factor = HD ** (-0.5)
    features = feature_table()
    columns = column_table()
    gains = pad_features(norm_gains)
    own_places = wide * ROWS + jnp.arange(ROWS)
    key_places = jnp.arange(SEQ)
    tokens = token_ids[:, 0]
    targets = target_ids[:, 0]
    prefixes = prefix_lengths[:, 0]
    positions = loss_positions[:, 0]

    own_positions = lax.dynamic_slice_in_dim(positions, wide * PICK, PICK, axis=1)
    own_targets = jnp.take_along_axis(targets, own_positions, axis=1).reshape(MB * PICK)
    own_counted = (own_positions >= prefixes[:, None]).astype(jnp.int32).reshape(MB * PICK)
    meta = jnp.pad(jnp.stack([own_targets, own_counted]), ((0, 6), (0, 128 - MB * PICK)))

    table_low = dot(embed_table.astype(BF16), features, 1, 0).astype(BF16)
    table_other = partner(table_low)

    shards = [
        to_shard(master.astype(BF16), rows) for master, rows in zip(masters, (RI, RO, RG, RD))
    ]
    ordered = tokens.reshape(MB, 8, ROWS).swapaxes(0, 1).reshape(2048)
    by_core = tokens.reshape(MB, 4, 2, ROWS).transpose(2, 1, 0, 3).reshape(2048)
    local_ids = by_core - wide * (16 * 384)
    holder, row = local_ids // 384, local_ids % 384
    swapped = holder % 4 * 4 + holder // 4
    found = jnp.where(row < 192, holder * 192 + row, (15 + swapped) * 192 + row)
    found = jnp.where((local_ids >= 0) & (local_ids < 16 * 384), found, 6144).astype(jnp.int32)
    wi, wo, wg, wd, info, x0 = fetch(
        *shards, meta, table_low.reshape(384, 8, 128), found
    )
    x0 = x0.reshape(256, DP).astype(F32)
    wi = wi.reshape(16, RI, DP)[:, :100].reshape(QKV, DP)
    wo = wo.reshape(DP, DP)
    wg = wg.reshape(2 * FF, DP)
    wd = wd.reshape(FF, DP)
    info = info.reshape(128, 8, 128)
    all_targets = info[:, 0, : MB * PICK].reshape(4096)
    all_counted = info[:, 1, : MB * PICK].reshape(4096).astype(F32)

    a = rms_norm(x0, gains[0]).astype(BF16)
    projected = dot(a, wi, 1, 1)
    places_all = jnp.concatenate([own_places, own_places])
    rows_count = MB * ROWS
    query = rotate(projected[:, : H * HD].reshape(rows_count, H, HD), places_all).astype(BF16)
    key_own = rotate(
        projected[:, H * HD : H * HD + kv_width].reshape(rows_count, KVH, HD), places_all
    ).astype(BF16)
    value_own = projected[:, H * HD + kv_width :].astype(BF16)
    kv_own = [
        part.reshape(MB, ROWS, kv_width).swapaxes(1, 2)
        for part in (key_own.reshape(rows_count, kv_width), value_own)
    ]
    kv_all = gather_keys(jnp.concatenate(kv_own)).reshape(4, KVH, HD, SEQ)

    def allowed_of(batch):
        return (key_places[None, :] <= own_places[:, None]) | (
            key_places[None, :] < prefixes[batch]
        )

    kept = []
    mixed_parts = []
    for batch in range(MB):
        q = query.reshape(MB, ROWS, KVH, group_size, HD)[batch]
        k, v = kv_all[batch], kv_all[MB + batch]
        scores = jnp.einsum("qkgd,kdt->kgqt", q, k, preferred_element_type=F32) * scale_factor
        scores = jnp.where(allowed_of(batch), scores, NEGATIVE)
        highest = jnp.max(scores, axis=-1, keepdims=True)
        exp_part = jnp.exp(scores - highest)
        exp_total = jnp.sum(exp_part, axis=-1, keepdims=True)
        log_total = highest + jnp.log(exp_total)
        probs = (exp_part / exp_total).astype(BF16)
        mixed = jnp.einsum("kgqt,kdt->qkgd", probs, v, preferred_element_type=F32)
        mixed_parts.append(mixed.reshape(ROWS, H * HD).astype(BF16))
        kept.append((q, k, v, log_total))
    o_pad = dot(jnp.concatenate(mixed_parts), features, 1, 0).astype(BF16)
    x1 = x0 + dot(o_pad, wo, 1, 1)

    b = rms_norm(x1, gains[1]).astype(BF16)
    gate_up = dot(b, wg, 1, 1)
    activated = gated(gate_up).astype(BF16)
    x2 = x1 + dot(activated, wd, 1, 0)

    final = rms_norm(x2, gains[2]).astype(BF16)
    own_offsets = (own_positions - wide * ROWS + jnp.arange(MB)[:, None] * ROWS).reshape(-1)
    all_rows = gather_rows(final[own_offsets]).reshape(4096, DP)
    logits = dot(all_rows, table_low, 1, 1)
    vocab_start = (wide * 16 + narrow) * 384
    hit = jnp.arange(384)[None, :] == (all_targets - vocab_start)[:, None]
    highest = jnp.max(logits, axis=-1)
    exp_total = jnp.sum(jnp.exp(logits - highest[:, None]), axis=-1)
    stats = jnp.stack([highest.reshape(32, 128), exp_total.reshape(32, 128)])
    log_total = small_all(stats, combine_stats, log_of_stats, (32, 128), 4, "row_totals")
    log_total = log_total.reshape(4096)
    hit_sum = jnp.sum(jnp.where(hit, logits, 0.0) * all_counted[:, None])
    logit_sum = jnp.sum(logits * all_counted[:, None])
    token_count = jnp.sum(all_counted)
    loss_known = jnp.sum(all_counted * (log_total + ZLOSS_WEIGHT * log_total * log_total))
    d_logits = (
        all_counted[:, None]
        * (
            (1.0 + 2.0 * ZLOSS_WEIGHT * log_total)[:, None] * jnp.exp(logits - log_total[:, None])
            - (1.0 - SMOOTH) * hit.astype(F32)
            - SMOOTH / V
        )
    ).astype(BF16)
    table_grad_rows = dot(d_logits, all_rows, 0, 0)
    d_by_core = d_logits.reshape(64, 2, 32, 384)
    d_mine = lax.dynamic_index_in_dim(d_by_core, core, 1, keepdims=False).reshape(2048, 384)
    d_theirs = lax.dynamic_index_in_dim(d_by_core, 1 - core, 1, keepdims=False).reshape(2048, 384)
    d_theirs = partner(d_theirs)
    row_part = dot(d_mine, table_low, 1, 0) + dot(d_theirs, table_other, 1, 0)
    d_rows = scatter_rows(row_part.astype(BF16).reshape(4, 4, 4, 32, DP))

    d_final = jnp.zeros((rows_count, DP), F32).at[own_offsets].add(d_rows)
    d_x2, d_gain_final = jax.vjp(rms_norm, x2, gains[2])[1](d_final)
    d_branch = d_x2.astype(BF16)
    d_activated = dot(d_branch, wd, 1, 1)
    d_gate_up = jax.vjp(gated, gate_up)[1](d_activated)[0].astype(BF16)
    d_b = dot(d_gate_up, wg, 1, 0)
    d_x1_part, d_gain_mlp = jax.vjp(rms_norm, x1, gains[1])[1](d_b)
    d_x1 = d_x2 + d_x1_part
    d_out = d_x1.astype(BF16)
    d_mixed_pad = dot(d_out, wo, 1, 0).astype(BF16)
    d_mixed = dot(d_mixed_pad, features, 1, 1).astype(BF16)
    d_queries, d_kv = [], []
    for batch in range(MB):
        q, k, v, log_sum = kept[batch]
        d_m = d_mixed.reshape(MB, ROWS, KVH, group_size, HD)[batch]
        scores = jnp.einsum("qkgd,kdt->kgqt", q, k, preferred_element_type=F32) * scale_factor
        scores = jnp.where(allowed_of(batch), scores, NEGATIVE)
        probs = jnp.exp(scores - log_sum)
        d_probs = jnp.einsum("qkgd,kdt->kgqt", d_m, v, preferred_element_type=F32)
        d_scores = (
            probs * (d_probs - jnp.sum(probs * d_probs, axis=-1, keepdims=True))
        ).astype(BF16)
        d_q = jnp.einsum("kgqt,kdt->qkgd", d_scores, k, preferred_element_type=F32) * scale_factor
        d_k = jnp.einsum("kgqt,qkgd->kdt", d_scores, q, preferred_element_type=F32) * scale_factor
        d_v = jnp.einsum(
            "kgqt,qkgd->kdt", probs.astype(BF16), d_m, preferred_element_type=F32
        )
        d_queries.append(d_q.reshape(ROWS, H, HD))
        d_kv.append((d_k.reshape(kv_width, SEQ), d_v.reshape(kv_width, SEQ)))
    d_kv_own = sum_keys([d_kv[0][0], d_kv[1][0], d_kv[0][1], d_kv[1][1]])
    d_kv_own = d_kv_own.swapaxes(1, 2).reshape(2, rows_count, kv_width)

    def unrotate(gradient, heads):
        primal = jnp.zeros((rows_count, heads, HD), F32)
        return jax.vjp(lambda values: rotate(values, places_all), primal)[1](gradient)[0]

    d_projected = jnp.concatenate(
        [
            unrotate(jnp.concatenate(d_queries), H).reshape(rows_count, H * HD),
            unrotate(d_kv_own[0].reshape(rows_count, KVH, HD), KVH).reshape(
                rows_count, kv_width
            ),
            d_kv_own[1],
        ],
        axis=1,
    ).astype(BF16)
    d_a = dot(d_projected, wi, 1, 0)
    d_x0_part, d_gain_attn = jax.vjp(rms_norm, x0, gains[0])[1](d_a)
    d_x0 = (d_x1 + d_x0_part).astype(BF16)

    def half_pair(value):
        mine = lax.dynamic_slice_in_dim(value, core * 512, 512, axis=1)
        theirs = lax.dynamic_slice_in_dim(value, (1 - core) * 512, 512, axis=1)
        return jnp.concatenate([mine, partner(theirs)])

    def both(value):
        return jnp.concatenate([value, partner(value)])

    d_projected_pad = dot(d_projected, columns, 1, 0).astype(BF16)
    grad_wd = dot(both(activated), half_pair(d_branch), 0, 0).astype(BF16)
    grad_wg = dot(both(d_gate_up), half_pair(b), 0, 0).astype(BF16)
    grad_wo = dot(both(d_out), half_pair(o_pad), 0, 0).astype(BF16)
    grad_wi = dot(both(d_projected_pad), half_pair(a), 0, 0).astype(BF16)
    table_grad, summed_grads = scatter_grads(
        d_x0,
        ordered[None, :],
        grad_wi.reshape(4, 4, RI, 512),
        grad_wo.reshape(2, 4, 2, RO, 512),
        grad_wg.reshape(2, 2, 2, 4, 160, 512),
        grad_wd.reshape(2, 4, 2, 160, 512),
    )
    grad_shards = (
        jnp.concatenate([summed_grads[1, 160:224], summed_grads[2, 160:208]]),
        summed_grads[0, 160:224],
        jnp.concatenate([summed_grads[0, :160], summed_grads[1, :160]]),
        summed_grads[2, :160],
    )

    table_grad = table_grad + table_grad_rows

    squares = sum(jnp.sum(shard * shard) for shard in grad_shards) + jnp.sum(
        table_grad * table_grad
    )
    table_grad = dot(table_grad, features, 1, 1, HIGH)
    gain_grads = jnp.stack([d_gain_attn, d_gain_mlp, d_gain_final]).reshape(24, 128)
    scalars = jnp.pad(jnp.stack([squares, hit_sum, logit_sum]), (0, 125))
    packed = jnp.pad(jnp.concatenate([gain_grads, scalars[None]]), ((0, 7), (0, 0)))
    summed = small_all(packed, jnp.add, lambda v: v, (32, 128), 5, "global_sums")
    gain_grad = unpad_features(summed[:24].reshape(3, DP))
    loss_total = loss_known - (1.0 - SMOOTH) * summed[24, 1] - SMOOTH / V * summed[24, 2]
    grad_norm = jnp.sqrt(summed[24, 0] + jnp.sum(gain_grad * gain_grad)) / token_count
    factor = jnp.minimum(1.0, CLIP_NORM / grad_norm) / token_count

    new_shards = [
        MOMENTUM * to_shard(moment, rows) + factor * grad
        for moment, rows, grad in zip(moments, (RI, RO, RG, RD), grad_shards)
    ]
    pieces = jnp.stack([jnp.pad(s, ((0, 320 - s.shape[0]), (0, 0))) for s in new_shards])
    turned, gram = gram_of(pieces)
    gram = gram.reshape(DP, DP)
    turned = lax.dynamic_slice_in_dim(turned, core * 160, 160)
    current = newton(gram, turned)
    pieces = current.reshape(160, 2, 4, 128).transpose(2, 1, 0, 3).reshape(8, 160, 128)
    pieces = lax.all_to_all(pieces, "wide", split_axis=0, concat_axis=0)
    pieces = pieces.reshape(4, 320, 128)
    new_moments, new_weights = [], []
    for kind, rows in enumerate((RI, RO, RG, RD)):
        count = masters[kind].shape[1]
        ortho = pieces[kind, :rows]
        new_moments.append(from_shard(new_shards[kind], count)[None])
        new_weights.append(
            (
                masters[kind] * (1.0 - MUON_RATE * WEIGHT_DECAY)
                - MUON_RATE * 0.2 * math.sqrt(count * 16) * from_shard(ortho, count)
            )[None]
        )
    table_m, table_v, table_new = adam_update(
        embed_table, table_first, table_second, factor * table_grad, TABLE_RATE, WEIGHT_DECAY
    )
    gains_m, gains_v, gains_new = adam_update(
        norm_gains, gains_first, gains_second, factor * gain_grad, GAIN_RATE, 0.0
    )
    return (
        loss_total,
        token_count,
        grad_norm,
        *new_moments,
        *new_weights,
        *[weight.astype(BF16) for weight in new_weights],
        table_m,
        table_v,
        table_new,
        table_new.astype(BF16),
        gains_m,
        gains_v,
        gains_new,
    )


def solution(mesh):
    whole = P()
    by_sequence = P(None, "narrow", None)
    matrix = P(None, "wide", "narrow")
    table = P(("wide", "narrow"), None)
    return jax.shard_map(
        body,
        mesh=mesh,
        in_specs=(
            (by_sequence, by_sequence, P(None, "narrow"), by_sequence)
            + (matrix,) * 4
            + (whole, table)
            + (matrix,) * 4
            + (table, table, whole, whole)
        ),
        out_specs=(whole,) * 3 + (matrix,) * 12 + (table,) * 4 + (whole,) * 3,
        check_vma=False,
    )
```

```python
import functools
import math

import jax
import jax.numpy as jnp
from jax import lax
from jax.experimental import pallas as pl
from jax.experimental.pallas import tpu as pltpu
from jax.sharding import PartitionSpec as P

D = 960
H = 15
KVH = 5
HD = 64
FF = 2560
V = 49152
QKV = 1600
ITERS = 5
STEP = 10
MB = 2
SEQ = 1024
ROWS = 128
PICK = 16
DP = 1024

NORM_EPS = 1e-05
ROPE_THETA = 100000.0
SMOOTH = 0.1
ZLOSS_WEIGHT = 0.0001
CLIP_NORM = 0.02
MOMENTUM = 0.95
NS_A = 3.4445
NS_B = -4.775
NS_C = 2.0315
MUON_RATE = 0.1
WEIGHT_DECAY = 0.1
BETA_ONE = 0.9
BETA_TWO = 0.95
TABLE_RATE = 0.03
GAIN_RATE = 0.4
ADAM_EPS = 1e-08
NEGATIVE = -1e30

HIGHEST = lax.Precision.HIGHEST
HIGH = lax.Precision.HIGH
F32 = jnp.float32
BF16 = jnp.bfloat16
MESH = pl.DeviceIdType.MESH
ANY = pl.BlockSpec(memory_space=pl.ANY)
VMEM = pl.BlockSpec(memory_space=pltpu.VMEM)

RI, RO, RG, RD = 112, 64, 320, 160


def my_place():
    wide = lax.axis_index("wide")
    narrow = lax.axis_index("narrow")
    return {
        "y": lax.div(wide, 2),
        "c": lax.rem(wide, 2),
        "z": lax.div(narrow, 4),
        "x": lax.rem(narrow, 4),
    }


def device(place):
    return (place["y"] * 2 + place["c"], place["z"] * 4 + place["x"])


def at_step(place, axis, step):
    return {**place, axis: lax.rem(place[axis] + step, 4)}


def other_core(place):
    return {**place, "c": 1 - place["c"]}


def greet(targets):
    barrier = pltpu.get_barrier_semaphore()
    for target in targets:
        pl.semaphore_signal(barrier, inc=1, device_id=device(target), device_id_type=MESH)
    pl.semaphore_wait(barrier, len(targets))


class Net:
    def __init__(self, send, recv):
        self.send = send
        self.recv = recv
        self.copies = []

    def put(self, src, dst, target):
        k = len(self.copies)
        copy = pltpu.make_async_remote_copy(
            src_ref=src,
            dst_ref=dst,
            send_sem=self.send.at[k],
            recv_sem=self.recv.at[k],
            device_id=device(target),
            device_id_type=MESH,
        )
        copy.start()
        self.copies.append(copy)
        return copy

    def finish(self):
        for copy in self.copies:
            copy.wait_send()


class Spread:
    def __init__(self, net, place, axes, items, with_core):
        self.net, self.place, self.axes, self.items = net, place, axes, items
        self.with_core = with_core
        self.sel = dict(place)
        self.phase = 0
        self.core = []

    def to_core(self, region, sel, half):
        if self.with_core and self.phase == len(self.axes) - 1:
            ref = region(sel, half)
            self.core.append(self.net.put(ref, ref, other_core(self.place)))

    def begin(self):
        self.axis = self.axes[self.phase]
        self.up, self.across, self.down = [at_step(self.place, self.axis, k) for k in (1, 2, 3)]
        self.first, self.second, self.onward = [], [], []
        for group, first_half in ((self.first, 0), (self.second, 1)):
            for region, halves in self.items:
                for target, origin, half in (
                    (self.up, self.down, first_half),
                    (self.down, self.up, 1 - first_half),
                ):
                    if halves[half] is not None:
                        ref = region(self.sel, halves[half])
                        copy = self.net.put(ref, ref, target)
                        group.append((copy, origin, target, region, halves[half]))
        for region, halves in self.items:
            for half in halves:
                if half is not None:
                    self.to_core(region, self.sel, half)

    def relay(self):
        for copy, origin, target, region, half in self.first:
            copy.wait_recv()
            sel = {**self.sel, self.axis: origin[self.axis]}
            ref = region(sel, half)
            self.onward.append((self.net.put(ref, ref, target), region, half))
            self.to_core(region, sel, half)

    def near(self):
        for copy, origin, _, region, half in self.second:
            copy.wait_recv()
            self.to_core(region, {**self.sel, self.axis: origin[self.axis]}, half)

    def far(self):
        for copy, region, half in self.onward:
            copy.wait_recv()
            self.to_core(region, {**self.sel, self.axis: self.across[self.axis]}, half)
        self.sel[self.axis] = None
        self.phase += 1

    def end(self):
        for copy in self.core:
            copy.wait_recv()


def gather_streams(net, place, streams, with_core):
    spreads = [Spread(net, place, axes, items, with_core) for axes, items in streams]
    for _ in range(len(streams[0][0])):
        for step in ("begin", "relay", "near", "far"):
            for spread in spreads:
                getattr(spread, step)()
    for spread in spreads:
        spread.end()


def pick(index):
    return slice(None) if index is None else index


def lanes_of(sel):
    if sel["y"] is None:
        return pl.ds(pl.multiple_of(sel["c"] * 512, 512), 512)
    return pl.ds(pl.multiple_of((sel["c"] * 4 + sel["y"]) * 128, 128), 128)


def halved(low, high):
    cut = low + (high - low) // 32 * 16
    return ((low, cut - low), (cut, high - cut))


def neighbours(place, axes=("x", "y", "z"), core=True):
    found = [at_step(place, axis, step) for axis in axes for step in (1, 3)]
    return found + ([other_core(place)] if core else [])


def fetch_kernel(
    gi, go, gg, gd, meta, table, ids, wi, wo, wg, wd, info, x0, *scratch
):
    slab, packed, theirs, got, send, recv, local = scratch
    place = my_place()

    def in_wi(sel, rows):
        return wi.at[pick(sel["z"]), pick(sel["x"]), pl.ds(*rows), lanes_of(sel)]

    def in_wo(sel, rows):
        z, x = sel["z"], sel["x"]
        xh, xl = (None, None) if x is None else (lax.div(x, 2), lax.rem(x, 2))
        return wo.at[pick(xh), pick(z), pick(xl), pl.ds(*rows), lanes_of(sel)]

    def in_wg(half):
        def region(sel, rows):
            z, x = sel["z"], sel["x"]
            zh, zl = (None, None) if z is None else (lax.div(z, 2), lax.rem(z, 2))
            return wg.at[pick(zh), half, pick(zl), pick(x), pl.ds(*rows), lanes_of(sel)]

        return region

    def in_wd(sel, rows):
        z, x = sel["z"], sel["x"]
        xh, xl = (None, None) if x is None else (lax.div(x, 2), lax.rem(x, 2))
        return wd.at[pick(xl), pick(z), pick(xh), pl.ds(*rows), lanes_of(sel)]

    def in_info(sel, rows):
        return info.at[pick(sel["z"]), pick(sel["x"]), pick(sel["y"]), sel["c"], :, :]

    owns = [
        (gi, in_wi(place, (0, RI))),
        (go, in_wo(place, (0, RO))),
        (gg.at[pl.ds(0, 160)], in_wg(0)(place, (0, 160))),
        (gg.at[pl.ds(160, 160)], in_wg(1)(place, (0, 160))),
        (gd, in_wd(place, (0, RD))),
        (meta, in_info(place, None)),
        (table.at[pl.ds(0, 192)], slab.at[pl.ds((place["z"] * 4 + place["x"]) * 192, 192)]),
        (table.at[pl.ds(192, 192)], slab.at[pl.ds((16 + place["x"] * 4 + place["z"]) * 192, 192)]),
    ]
    copies = [pltpu.make_async_copy(src, dst, local.at[k]) for k, (src, dst) in enumerate(owns)]
    for copy in copies:
        copy.start()
    for copy in copies:
        copy.wait()
    greet(neighbours(place))
    net = Net(send, recv)
    slab[pl.ds(6144, 8)] = jnp.zeros((8, 8, 128), BF16)

    def in_slab(major, minor, first):
        def region(sel, half):
            start = (first + sel[major] * 4) * 192
            if sel[minor] is None:
                return slab.at[pl.ds(start + half * 384, 384)]
            return slab.at[pl.ds(start + sel[minor] * 192 + half * 96, 96)]

        return region

    tables = [
        Spread(net, place, ("x", "z"), [(in_slab("z", "x", 0), (0, 1))], False),
        Spread(net, place, ("z", "x"), [(in_slab("x", "z", 16), (0, 1))], False),
    ]
    weights = [
        Spread(net, place, axes, items, True)
        for axes, items in (
            (("x", "z", "y"), [(in_wg(0), halved(0, 160)), (in_wo, halved(0, 64))]),
            (("z", "x", "y"), [(in_wg(1), halved(0, 160)), (in_wi, halved(0, 64))]),
            (("z", "y", "x"), [(in_wd, halved(0, 80)), (in_wi, halved(64, 112))]),
            (("x", "y", "z"), [(in_wd, halved(80, 160)), (in_info, ((0, 8), None))]),
        )
    ]

    def each(spreads, *steps):
        for step in steps:
            for spread in spreads:
                getattr(spread, step)()

    each(tables, "begin")
    each(weights, "begin")
    each(tables, "relay")
    each(weights, "relay")
    each(tables, "near", "far", "begin")
    each(weights, "near", "far", "begin", "relay", "near", "far", "begin")
    each(tables, "relay")
    each(weights, "relay")
    each(tables, "near")
    each(weights, "near")
    each(tables, "far")

    @pl.loop(0, 128)
    def _(block):
        for k in range(16):
            token = block * 16 + k
            packed[token] = slab[ids[token]]

    swap = net.put(
        packed.at[pl.ds((1 - place["c"]) * 1024, 1024)], theirs, other_core(place)
    )
    each(weights, "far")
    swap.wait_recv()
    add_up(theirs, [packed.at[pl.ds(place["c"] * 1024, 1024)], theirs])
    ring = Ring(
        net,
        place,
        "y",
        lambda k, half: theirs.at[pl.ds(k * 256 + half * 128, 128)],
        lambda k: got.at[k],
        lambda half: x0.at[pl.ds(half * 128, 128)],
    )
    ring.send_all()
    ring.pass_on()
    ring.close()
    each(weights, "end")
    net.finish()


def fetch(gi, go, gg, gd, meta, table, ids):
    shapes = [
        jax.ShapeDtypeStruct((4, 4, RI, DP), BF16),
        jax.ShapeDtypeStruct((2, 4, 2, RO, DP), BF16),
        jax.ShapeDtypeStruct((2, 2, 2, 4, 160, DP), BF16),
        jax.ShapeDtypeStruct((2, 4, 2, 160, DP), BF16),
        jax.ShapeDtypeStruct((4, 4, 4, 2, 8, 128), jnp.int32),
        jax.ShapeDtypeStruct((256, 8, 128), BF16),
    ]
    count = 226
    return pl.pallas_call(
        fetch_kernel,
        out_shape=shapes,
        in_specs=[ANY] * 6 + [pl.BlockSpec(memory_space=pltpu.SMEM)],
        out_specs=[ANY] * 5 + [VMEM],
        scratch_shapes=[
            pltpu.VMEM((6152, 8, 128), BF16),
            pltpu.VMEM((2048, 8, 128), BF16),
            pltpu.VMEM((1024, 8, 128), BF16),
            pltpu.VMEM((6, 128, 8, 128), BF16),
            pltpu.SemaphoreType.DMA((count,)),
            pltpu.SemaphoreType.DMA((count,)),
            pltpu.SemaphoreType.DMA((8,)),
        ],
        compiler_params=pltpu.CompilerParams(
            collective_id=0, has_side_effects=True, vmem_limit_bytes=56 << 20
        ),
        name="fetch",
    )(gi, go, gg, gd, meta, table, ids)


LANE_PARTS = ((0, 384), (384, 384), (768, 256))
ORDERS = (("x", "z", "y"), ("z", "y", "x"), ("y", "x", "z"))


def rows_kernel(own, rows, send, recv, local):
    place = my_place()
    greet(neighbours(place))

    def in_rows(lanes):
        def region(sel, part):
            return rows.at[
                pick(sel["z"]), pick(sel["x"]), pick(sel["y"]), sel["c"], pl.ds(*part), pl.ds(*lanes)
            ]

        return region

    copy = pltpu.make_async_copy(
        own, rows.at[place["z"], place["x"], place["y"], place["c"]], local
    )
    copy.start()
    copy.wait()
    streams = [
        (axes, [(in_rows(lanes), ((0, 16), (16, 16)))]) for axes, lanes in zip(ORDERS, LANE_PARTS)
    ]
    net = Net(send, recv)
    gather_streams(net, place, streams, True)
    net.finish()


def gather_rows(own):
    count = 90
    return pl.pallas_call(
        rows_kernel,
        out_shape=jax.ShapeDtypeStruct((4, 4, 4, 2, 32, DP), BF16),
        in_specs=[VMEM],
        out_specs=VMEM,
        scratch_shapes=[
            pltpu.SemaphoreType.DMA((count,)),
            pltpu.SemaphoreType.DMA((count,)),
            pltpu.SemaphoreType.DMA,
        ],
        compiler_params=pltpu.CompilerParams(
            collective_id=1, has_side_effects=True, vmem_limit_bytes=24 << 20
        ),
        name="gather_rows",
    )(own)


def small_kernel(combine, last, own, out, held, narrow_slots, wide_slots, send, recv):
    place = my_place()
    plane = [
        at_step(at_step(place, "z", k // 4), "x", k % 4) for k in range(1, 16)
    ]
    column = [
        {**at_step(place, "y", k // 2), "c": lax.rem(place["c"] + k % 2, 2)} for k in range(1, 8)
    ]
    greet(plane + column)
    net = Net(send, recv)
    value = own
    for number, (slots, index, targets) in enumerate(
        (
            (narrow_slots, place["z"] * 4 + place["x"], plane),
            (wide_slots, place["y"] * 2 + place["c"], column),
        )
    ):
        copies = [net.put(value, slots.at[index], target) for target in targets]
        slots[index] = value[...]
        for copy in copies:
            copy.wait_recv()
        total = slots[0]
        for k in range(1, slots.shape[0]):
            total = combine(total, slots[k])
        if number == 0:
            held[...] = total
            value = held
    out[...] = last(total)
    net.finish()


def small_all(value, combine, last, out_shape, collective_id, name):
    shape = value.shape
    count = 22
    return pl.pallas_call(
        functools.partial(small_kernel, combine, last),
        out_shape=jax.ShapeDtypeStruct(out_shape, F32),
        in_specs=[VMEM],
        out_specs=VMEM,
        scratch_shapes=[
            pltpu.VMEM(shape, F32),
            pltpu.VMEM((16,) + shape, F32),
            pltpu.VMEM((8,) + shape, F32),
            pltpu.SemaphoreType.DMA((count,)),
            pltpu.SemaphoreType.DMA((count,)),
        ],
        compiler_params=pltpu.CompilerParams(collective_id=collective_id, has_side_effects=True),
        name=name,
    )(value)


def combine_stats(one, two):
    highest = jnp.maximum(one[0], two[0])
    total = one[1] * jnp.exp(one[0] - highest) + two[1] * jnp.exp(two[0] - highest)
    return jnp.stack([highest, total])


def log_of_stats(stats):
    return stats[0] + jnp.log(stats[1])


def add_up(dst, parts):
    if len(dst.shape) == 3:
        step = max(1, min(dst.shape[0], 32768 // (dst.shape[1] * dst.shape[2])))

        @pl.loop(0, dst.shape[0] // step)
        def _(k):
            block = pl.ds(k * step, step)
            total = parts[0][block].astype(F32)
            for part in parts[1:]:
                total = total + part[block].astype(F32)
            dst[block] = total.astype(dst.dtype)

        return
    total = parts[0][...].astype(F32)
    for part in parts[1:]:
        total = total + part[...].astype(F32)
    dst[...] = total.astype(dst.dtype)


class Ring:
    def __init__(self, net, place, axis, source, got, result):
        self.net, self.source, self.got, self.result = net, source, got, result
        steps = [at_step(place, axis, step) for step in range(4)]
        self.own, self.up, self.across, self.down = [step[axis] for step in steps]
        self.to_up, self.to_down = steps[1], steps[3]

    def send_across(self):
        self.far_up = self.net.put(self.source(self.across, 0), self.got(0), self.to_up)
        self.far_down = self.net.put(self.source(self.across, 1), self.got(1), self.to_down)

    def send_up(self):
        self.near_up = self.net.put(self.source(self.up, 1), self.got(2), self.to_up)

    def send_down(self):
        self.near_down = self.net.put(self.source(self.down, 0), self.got(3), self.to_down)

    def send_all(self):
        self.send_across()
        self.send_up()
        self.send_down()

    def pass_on(self):
        self.far_up.wait_recv()
        add_up(self.got(0), [self.source(self.up, 0), self.got(0)])
        self.on_up = self.net.put(self.got(0), self.got(4), self.to_up)
        self.far_down.wait_recv()
        add_up(self.got(1), [self.source(self.down, 1), self.got(1)])
        self.on_down = self.net.put(self.got(1), self.got(5), self.to_down)

    def close(self):
        for copy in (self.near_up, self.near_down, self.on_up, self.on_down):
            copy.wait_recv()
        add_up(self.result(0), [self.source(self.own, 0), self.got(4), self.got(3)])
        add_up(self.result(1), [self.source(self.own, 1), self.got(2), self.got(5)])


FAR_FIRST = (2, 1, 3, 0)


def start_scatter(net, place, order, source, gots, out, acc=None):
    rows = out.shape[0] // 2
    halves = (pl.ds(0, rows), pl.ds(rows, rows))
    lead = ("z", "x", "y")[: len(order)]

    def block(sel, half):
        return source.at[tuple(pick(sel.get(axis)) for axis in lead) + (halves[half],)]

    def summed(sel, half):
        if acc is None:
            return block({order[0]: place[order[0]], **sel}, half)
        return acc.at[tuple(pick(sel.get(axis)) for axis in order[1:]) + (halves[half],)]

    stream = {"first": {}, "rest": []}
    one, two = order[:2]
    for sub, far in enumerate(FAR_FIRST):
        at_two = at_step(place, two, far)[two]
        stream["first"][far] = Ring(
            net,
            place,
            one,
            lambda k, half, at_two=at_two: block({one: k, two: at_two}, half),
            lambda k, sub=sub: gots[0].at[sub, k],
            lambda half, at_two=at_two: summed({two: at_two}, half),
        )
    for number in range(1, len(order)):
        done = {axis: place[axis] for axis in order[1:number]}

        def part(k, half, done=done, axis=order[number]):
            return summed({**done, axis: k}, half)

        if number + 1 < len(order):
            result = lambda half, part=part, axis=order[number]: part(place[axis], half)
        else:
            result = lambda half: out.at[halves[half]]
        stream["rest"].append(
            Ring(net, place, order[number], part, lambda k, n=number: gots[n].at[k], result)
        )
    return stream


def send_first(streams):
    for far in FAR_FIRST:
        for stream in streams:
            stream["first"][far].send_across()
    for far in FAR_FIRST:
        for stream in streams:
            stream["first"][far].send_up()
            stream["first"][far].send_down()


def pass_first(streams):
    for far in FAR_FIRST:
        for stream in streams:
            stream["first"][far].pass_on()


def close_first(streams):
    for far in FAR_FIRST:
        for stream in streams:
            stream["first"][far].close()
            following = stream["rest"][0]
            if far == 2:
                following.send_across()
            if far == 1:
                following.send_up()
            if far == 3:
                following.send_down()


def pass_rest(streams, number):
    for stream in streams:
        stream["rest"][number].pass_on()


def close_rest(streams, number):
    for stream in streams:
        stream["rest"][number].close()
        if number + 1 < len(stream["rest"]):
            stream["rest"][number + 1].send_all()


def finish_scatter(streams):
    pass_first(streams)
    close_first(streams)
    for number in range(len(streams[0]["rest"])):
        pass_rest(streams, number)
        close_rest(streams, number)


def got_shapes(depth, rows, lanes, first, later):
    half = rows // 2
    return [
        pltpu.VMEM(
            ((4, 6) if number == 0 else (6,)) + (4,) * (depth - max(number, 1) - 1) + (half, lanes),
            later if number else first,
        )
        for number in range(depth)
    ]


def row_sums_kernel(part, out, *scratch):
    held = scratch[0:3]
    accs = scratch[12:15]
    send, recv, local = scratch[15:]
    place = my_place()
    copies = [
        pltpu.make_async_copy(part.at[:, :, :, :, pl.ds(*lanes)], held[k], local.at[k])
        for k, lanes in enumerate(LANE_PARTS)
    ]
    for copy in copies:
        copy.start()
    greet(neighbours(place, core=False))
    for copy in copies:
        copy.wait()
    net = Net(send, recv)
    streams = [
        start_scatter(
            net,
            place,
            order,
            held[k],
            scratch[3 + 3 * k : 6 + 3 * k],
            out.at[:, pl.ds(*lanes)],
            accs[k],
        )
        for k, (order, lanes) in enumerate(zip(ORDERS, LANE_PARTS))
    ]
    send_first(streams)
    finish_scatter(streams)
    net.finish()


def scatter_rows(part):
    scratch = [pltpu.VMEM((4, 4, 4, 32, lanes), part.dtype) for _, lanes in LANE_PARTS]
    for _, lanes in LANE_PARTS:
        scratch += got_shapes(3, 32, lanes, part.dtype, F32)
    scratch += [pltpu.VMEM((4, 4, 32, lanes), F32) for _, lanes in LANE_PARTS]
    scratch += [
        pltpu.SemaphoreType.DMA((108,)),
        pltpu.SemaphoreType.DMA((108,)),
        pltpu.SemaphoreType.DMA((3,)),
    ]
    return pl.pallas_call(
        row_sums_kernel,
        out_shape=jax.ShapeDtypeStruct((32, DP), F32),
        in_specs=[ANY],
        out_specs=VMEM,
        scratch_shapes=scratch,
        compiler_params=pltpu.CompilerParams(
            collective_id=3, has_side_effects=True, vmem_limit_bytes=40 << 20
        ),
        name="scatter_rows",
    )(part)


GRAD_STREAMS = (
    (("y", "x", "z"), 0, 0, 224),
    (("y", "z", "x"), 1, 0, 224),
    (("x", "y", "z"), 2, 0, 128),
    (("z", "y", "x"), 2, 128, 96),
)


def grads_kernel(dx, ids, di, do, dg, dd, out, weights_out, *scratch):
    rows, table, chosen = scratch[:3]
    held = scratch[3:6]
    gots = scratch[6:10]
    weight_gots = scratch[10:22]
    accs = scratch[22:26]
    send, recv, local = scratch[26:]
    place = my_place()
    moves = [(dx, rows.at[place["y"], place["c"]])]
    for y in range(4):
        lanes = pl.ds(y * 128, 128)
        for z in range(4):
            for half in range(2):
                moves.append(
                    (
                        dg.at[z // 2, half, z % 2, :, :, lanes],
                        held[half].at[z, :, y, pl.ds(0, 160)],
                    )
                )
        for x in range(4):
            moves.append((dd.at[x % 2, :, x // 2, :, lanes], held[2].at[:, x, y, pl.ds(0, 160)]))
            moves.append((do.at[x // 2, :, x % 2, :, lanes], held[0].at[:, x, y, pl.ds(160, 64)]))
        for z in range(4):
            moves.append((di.at[z, :, pl.ds(0, 64), lanes], held[1].at[z, :, y, pl.ds(160, 64)]))
            moves.append((di.at[z, :, pl.ds(64, 48), lanes], held[2].at[z, :, y, pl.ds(160, 48)]))
    copies = [pltpu.make_async_copy(src, dst, local.at[k]) for k, (src, dst) in enumerate(moves)]
    for copy in copies:
        copy.start()
    held[2][:, :, :, 208:224, :] = jnp.zeros((4, 4, 4, 16, 128), BF16)
    greet(neighbours(place))
    copies[0].wait()

    def in_rows(sel, part):
        return rows.at[pick(sel["y"]), sel["c"], pl.ds(*part)]

    net = Net(send, recv)
    spread = Spread(net, place, ("y",), [(in_rows, ((0, 128), (128, 128)))], True)
    spread.begin()
    for copy in copies[1:]:
        copy.wait()
    weights = [
        start_scatter(
            net,
            place,
            order,
            held[which].at[:, :, :, pl.ds(first, count)],
            weight_gots[3 * k : 3 * k + 3],
            weights_out.at[which, pl.ds(first, count)],
            accs[k],
        )
        for k, (order, which, first, count) in enumerate(GRAD_STREAMS)
    ]
    send_first(weights[2:])
    spread.relay()
    spread.near()
    spread.far()
    send_first(weights[:2])
    spread.end()
    base = (place["y"] * 2 + place["c"]) * 16

    def parts(count, place_of):
        @pl.loop(0, count)
        def _(k):
            z, x = place_of(k)
            start = (base + z * 4 + x) * 384

            @pl.loop(0, 24)
            def _(r):
                row = pl.multiple_of(r * 16, 16)
                number = lax.broadcasted_iota(jnp.int32, (16, 2048), 0) + (start + row)
                chosen[pl.ds(row, 16), :] = (number == ids[...]).astype(F32).astype(BF16)

            @pl.loop(0, 4)
            def _(l):
                lanes = pl.ds(pl.multiple_of(l * 256, 256), 256)
                values = rows[:, :, :, lanes].reshape(2048, 256)
                total = jnp.dot(chosen[...], values, preferred_element_type=F32)
                table[z, x, :, lanes] = total.astype(BF16)

    def further(axis, step):
        return lax.rem(place[axis] + step, 4)

    streams = [
        start_scatter(
            net,
            place,
            order,
            table.at[:, :, pl.ds(192 * k, 192)],
            gots[2 * k : 2 * k + 2],
            out.at[pl.ds(192 * k, 192)],
        )
        for k, order in enumerate((("x", "z"), ("z", "x")))
    ]
    by_x, by_z = streams[0]["first"], streams[1]["first"]
    parts(4, lambda k: (further("z", 2), further("x", k + 2)))
    for step in FAR_FIRST:
        by_z[step].send_across()
    by_x[2].send_across()
    parts(3, lambda k: (further("z", k + 3), further("x", 2)))
    for step in (1, 3, 0):
        by_x[step].send_across()
    by_x[2].send_up()
    by_x[2].send_down()
    by_z[2].send_up()
    by_z[2].send_down()
    pass_first(weights[2:])
    third = lambda dz: parts(3, lambda k: (further("z", dz), further("x", k + 3)))
    third(1)
    for ring in (by_x[1], by_z[1], by_z[3], by_z[0]):
        ring.send_up()
    by_x[1].send_down()
    pass_first(weights[:2])
    close_first(weights[2:])
    third(3)
    for ring in (by_x[3], by_z[1], by_z[3], by_z[0]):
        ring.send_down()
    by_x[3].send_up()
    close_first(weights[:2])
    third(0)
    by_x[0].send_up()
    by_x[0].send_down()
    pass_first(streams)
    pass_rest(weights[2:], 0)
    close_rest(weights[2:], 0)
    pass_rest(weights[:2], 0)
    close_rest(weights[:2], 0)
    close_first(streams)
    pass_rest(weights, 1)
    close_rest(weights, 1)
    pass_rest(streams, 0)
    close_rest(streams, 0)
    net.finish()


def scatter_grads(dx, ids, di, do, dg, dd):
    count = 4 * 36 + 2 * 30 + 14
    scratch = [
        pltpu.VMEM((4, 2, 256, DP), BF16),
        pltpu.VMEM((4, 4, 384, DP), BF16),
        pltpu.VMEM((384, 2048), BF16),
    ]
    scratch += [pltpu.VMEM((4, 4, 4, 224, 128), BF16)] * 3
    scratch += got_shapes(2, 192, DP, BF16, BF16) * 2
    for _, _, _, rows in GRAD_STREAMS:
        scratch += got_shapes(3, rows, 128, BF16, F32)
    scratch += [pltpu.VMEM((4, 4, rows, 128), F32) for _, _, _, rows in GRAD_STREAMS]
    scratch += [
        pltpu.SemaphoreType.DMA((count,)),
        pltpu.SemaphoreType.DMA((count,)),
        pltpu.SemaphoreType.DMA((97,)),
    ]
    return pl.pallas_call(
        grads_kernel,
        out_shape=[
            jax.ShapeDtypeStruct((384, DP), F32),
            jax.ShapeDtypeStruct((3, 224, 128), F32),
        ],
        in_specs=[ANY, VMEM] + [ANY] * 4,
        out_specs=[VMEM, VMEM],
        scratch_shapes=scratch,
        compiler_params=pltpu.CompilerParams(
            collective_id=2, has_side_effects=True, vmem_limit_bytes=60 << 20
        ),
        name="scatter_grads",
    )(dx, ids, di, do, dg, dd)


def lanes_of_wide(y, c):
    return pl.ds(pl.multiple_of((y * 2 + c) * 128, 128), 128)


def keys_kernel(own, out, send, recv, local):
    place = my_place()
    copy = pltpu.make_async_copy(own, out.at[:, :, lanes_of_wide(place["y"], place["c"])], local)
    copy.start()
    greet(neighbours(place, ("y",)))
    copy.wait()

    def region(sel, rows):
        return out.at[:, pl.ds(*rows), lanes_of_wide(sel["y"], sel["c"])]

    net = Net(send, recv)
    gather_streams(net, place, [(("y",), [(region, ((0, 160), (160, 160)))])], True)
    net.finish()


def gather_keys(own):
    return pl.pallas_call(
        keys_kernel,
        out_shape=jax.ShapeDtypeStruct((4, 320, SEQ), BF16),
        in_specs=[VMEM],
        out_specs=VMEM,
        scratch_shapes=[
            pltpu.SemaphoreType.DMA((14,)),
            pltpu.SemaphoreType.DMA((14,)),
            pltpu.SemaphoreType.DMA,
        ],
        compiler_params=pltpu.CompilerParams(
            collective_id=6, has_side_effects=True, vmem_limit_bytes=16 << 20
        ),
        name="gather_keys",
    )(own)


def key_sums_kernel(*refs):
    parts, out = refs[:4], refs[4]
    theirs, held, got, send, recv = refs[5:]
    place = my_place()
    greet(neighbours(place, ("y",)))
    net = Net(send, recv)
    swaps = [
        [
            net.put(
                part.at[:, lanes_of_wide(at_step(place, "y", step)["y"], 1 - place["c"])],
                theirs.at[at_step(place, "y", step)["y"], k],
                other_core(place),
            )
            for k, part in enumerate(parts)
        ]
        for step in FAR_FIRST
    ]
    ring = Ring(
        net,
        place,
        "y",
        lambda k, half: held.at[k, pl.ds(2 * half, 2)],
        lambda k: got.at[k],
        lambda half: out.at[pl.ds(2 * half, 2)],
    )
    for step, swap in zip(FAR_FIRST, swaps):
        y = at_step(place, "y", step)["y"]
        for k, part in enumerate(parts):
            swap[k].wait_recv()
            own = part[:, lanes_of_wide(y, place["c"])]
            held[y, k] = (own + theirs[y, k]).astype(BF16)
        if step == 2:
            ring.send_across()
        if step == 1:
            ring.send_up()
        if step == 3:
            ring.send_down()
    ring.pass_on()
    ring.close()
    net.finish()


def sum_keys(parts):
    return pl.pallas_call(
        key_sums_kernel,
        out_shape=jax.ShapeDtypeStruct((4, 320, 128), F32),
        in_specs=[VMEM] * 4,
        out_specs=VMEM,
        scratch_shapes=[
            pltpu.VMEM((4, 4, 320, 128), F32),
            pltpu.VMEM((4, 4, 320, 128), BF16),
            pltpu.VMEM((6, 2, 320, 128), BF16),
            pltpu.SemaphoreType.DMA((22,)),
            pltpu.SemaphoreType.DMA((22,)),
        ],
        compiler_params=pltpu.CompilerParams(
            collective_id=8, has_side_effects=True, vmem_limit_bytes=32 << 20
        ),
        name="sum_keys",
    )(*parts)


def gram_kernel(pieces, turned, gram, part, *scratch):
    gots = scratch[:4]
    send, recv, local = scratch[4:]
    place = my_place()
    wides = [
        {**at_step(place, "y", step), "c": core}
        for step in (2, 1, 3, 0)
        for core in (place["c"], 1 - place["c"])
    ][:-2] + [other_core(place)]
    greet(wides + neighbours(place, ("x", "z"), False))
    net = Net(send, recv)

    def lanes_from(who):
        return pl.ds(pl.multiple_of((who["c"] * 4 + who["y"]) * 128, 128), 128)

    arrivals = [net.put(pieces.at[who["y"]], turned.at[:, lanes_from(place)], who) for who in wides]
    copy = pltpu.make_async_copy(pieces.at[place["y"]], turned.at[:, lanes_from(place)], local)
    copy.start()
    copy.wait()
    for arrival in arrivals:
        arrival.wait_recv()
    @pl.loop(0, 4)
    def _(k):
        rows = pl.ds(pl.multiple_of(place["c"] * 512 + k * 128, 128), 128)
        left = turned[:, rows].T
        for l in range(2):
            lanes = pl.ds(l * 512, 512)
            product = jnp.dot(left, turned[:, lanes], precision=HIGHEST, preferred_element_type=F32)
            for m in range(4):
                part[k, m, :, lanes] = product[m * 32 : m * 32 + 32]

    orders = (("x", "z"), ("z", "x"))
    lanes = (pl.ds(0, 512), pl.ds(512, 512))
    mine = gram.at[place["c"], place["z"], place["x"]]
    streams = [
        start_scatter(
            net, place, order, part.at[:, :, :, lane], gots[2 * k : 2 * k + 2], mine.at[:, lane]
        )
        for k, (order, lane) in enumerate(zip(orders, lanes))
    ]
    send_first(streams)
    finish_scatter(streams)

    def in_gram(lane):
        def region(sel, rows):
            return gram.at[sel["c"], pick(sel["z"]), pick(sel["x"]), pl.ds(*rows), lane]

        return region

    streams = [
        (order[::-1], [(in_gram(lane), ((0, 16), (16, 16)))]) for order, lane in zip(orders, lanes)
    ]
    gather_streams(net, place, streams, True)
    net.finish()


def gram_of(pieces):
    count = 7 + 2 * 30 + 44
    scratch = [pltpu.VMEM((4, 4, 32, DP), F32)]
    scratch += got_shapes(2, 32, 512, F32, F32) * 2
    scratch += [
        pltpu.SemaphoreType.DMA((count,)),
        pltpu.SemaphoreType.DMA((count,)),
        pltpu.SemaphoreType.DMA,
    ]
    return pl.pallas_call(
        gram_kernel,
        out_shape=[
            jax.ShapeDtypeStruct((320, DP), F32),
            jax.ShapeDtypeStruct((2, 4, 4, 32, DP), F32),
        ],
        in_specs=[VMEM],
        out_specs=[VMEM, VMEM],
        scratch_shapes=scratch,
        compiler_params=pltpu.CompilerParams(
            collective_id=7, has_side_effects=True, vmem_limit_bytes=40 << 20
        ),
        name="gram_sums",
    )(pieces)


def split(value, count):
    parts = []
    for _ in range(count):
        parts.append(value.astype(BF16))
        value = value - parts[-1].astype(F32)
    return parts


def product(left, right):
    count = len(left)
    total = None
    for order in range(count):
        for k in range(order + 1):
            term = jnp.dot(left[k], right[order - k], preferred_element_type=F32)
            total = term if total is None else total + term
    return total


def newton_kernel(gram, turned, out, power, *scratch):
    a_parts, q_parts, t_parts = scratch[0:3], scratch[3:6], scratch[6:8]

    def blocks(k):
        return pl.ds(pl.multiple_of(k * 256, 256), 256)

    def put(parts, i, j, value, count, mirror=True):
        for ref, part in zip(parts, split(value, count)):
            ref[blocks(i), blocks(j)] = part
            if mirror:
                ref[blocks(j), blocks(i)] = part.T

    def mirrored(left, right, count, emit):
        @pl.loop(0, 2)
        def _(half):
            for k in range(5):
                p = half * 5 + k
                i = sum((p >= edge).astype(jnp.int32) for edge in (4, 7, 9))
                j = p - lax.div(i * (7 - i), 2)
                value = product(
                    [ref[blocks(i), :] for ref in left[:count]],
                    [ref[:, blocks(j)] for ref in right[:count]],
                )
                emit(i, j, value)

    def diagonal(i, j):
        rows = lax.broadcasted_iota(jnp.int32, (256, 256), 0) + i * 256
        columns = lax.broadcasted_iota(jnp.int32, (256, 256), 1) + j * 256
        return rows == columns

    trace = jnp.zeros((), F32)
    for k in range(4):
        block = gram[k * 256 : (k + 1) * 256, k * 256 : (k + 1) * 256]
        trace = trace + jnp.sum(jnp.where(diagonal(0, 0), block, 0.0))
    scale = 1.0 / (jnp.sqrt(jnp.full((1, 1), trace, F32)) + 1e-07)

    @pl.loop(0, 16)
    def _(p):
        i, j = lax.div(p, 4), lax.rem(p, 4)
        value = gram[blocks(i), blocks(j)] * scale * scale
        power[blocks(i), blocks(j)] = value
        put(a_parts, i, j, value, 3, False)

    out[...] = turned[...] * scale

    def advance(count):
        def emit_step(i, j, value):
            value = NS_B * power[blocks(i), blocks(j)] + NS_C * value
            put(q_parts, i, j, value + jnp.where(diagonal(i, j), NS_A, 0.0), count)

        def emit_half(i, j, value):
            put(t_parts, i, j, value, 2)

        def emit_power(i, j, value):
            power[blocks(i), blocks(j)] = value
            put(a_parts, i, j, value, 2)

        mirrored(a_parts, a_parts, 2, emit_step)
        mirrored(q_parts, a_parts, count, emit_half)
        mirrored(t_parts, q_parts, 2, emit_power)
        current = split(out[...], 2)

        @pl.loop(0, 4)
        def _(j):
            out[:, blocks(j)] = product(current, [ref[:, blocks(j)] for ref in q_parts[:2]])

    advance(3)

    @pl.loop(0, ITERS - 2)
    def _(_step):
        advance(2)

    current = split(out[...], 2)
    once = power

    @pl.loop(0, 4)
    def _(j):
        once[0:160, blocks(j)] = product(current, [ref[:, blocks(j)] for ref in a_parts[:2]])

    applied = split(once[0:160, :], 2)

    @pl.loop(0, 4)
    def _(j):
        twice = product(applied, [ref[:, blocks(j)] for ref in a_parts[:2]])
        out[:, blocks(j)] = (
            NS_A * out[:, blocks(j)] + NS_B * once[0:160, blocks(j)] + NS_C * twice
        )


def newton(gram, turned):
    return pl.pallas_call(
        newton_kernel,
        out_shape=jax.ShapeDtypeStruct((160, DP), F32),
        in_specs=[VMEM, VMEM],
        out_specs=VMEM,
        scratch_shapes=[pltpu.VMEM((DP, DP), F32)] + [pltpu.VMEM((DP, DP), BF16)] * 8,
        compiler_params=pltpu.CompilerParams(vmem_limit_bytes=48 << 20),
        name="newton",
    )(gram, turned)


def pad_features(values):
    lead = values.shape[:-1]
    blocks = values.reshape(lead + (4, 2, 2, 60))
    blocks = jnp.moveaxis(blocks, -3, -4)
    blocks = jnp.pad(blocks, [(0, 0)] * (len(lead) + 3) + [(0, 4)])
    return blocks.reshape(lead + (DP,))


def unpad_features(values):
    blocks = values.reshape(values.shape[0], 2, 4, 2, 64)[..., :60]
    return blocks.transpose(0, 2, 1, 3, 4).reshape(values.shape[0], D)


def feature_table():
    feature = lax.broadcasted_iota(jnp.int32, (D, DP), 0)
    place = lax.broadcasted_iota(jnp.int32, (D, DP), 1)
    wide, rest = feature // 120, feature % 120
    where = ((wide % 2) * 4 + wide // 2) * 128 + (rest // 60) * 64 + rest % 60
    return (where == place).astype(BF16)


def column_table():
    column = lax.broadcasted_iota(jnp.int32, (QKV, 16 * RI), 0)
    place = lax.broadcasted_iota(jnp.int32, (QKV, 16 * RI), 1)
    return ((column // 100) * RI + column % 100 == place).astype(BF16)


def to_shard(matrix, rows):
    columns = matrix.shape[1]
    turned = matrix.T.reshape(columns, 2, 60)
    turned = jnp.pad(turned, ((0, rows - columns), (0, 0), (0, 4)))
    return turned.reshape(rows, 128)


def from_shard(shard, columns):
    return shard[:columns].reshape(columns, 2, 64)[:, :, :60].reshape(columns, 120).T


def dot(left, right, left_axis, right_axis, precision=None):
    return lax.dot_general(
        left,
        right,
        (((left_axis,), (right_axis,)), ((), ())),
        preferred_element_type=F32,
        precision=precision,
    )


def rms_norm(values, gain_row):
    mean = jnp.sum(values * values, axis=-1, keepdims=True) * (1.0 / D)
    return values * lax.rsqrt(mean + NORM_EPS) * gain_row


def rotate(values, places):
    half_width = HD // 2
    frequency = ROPE_THETA ** (-2.0 * jnp.arange(half_width).astype(F32) / HD)
    angles = places.astype(F32)[:, None] * frequency[None, :]
    cosine = jnp.concatenate([jnp.cos(angles), jnp.cos(angles)], axis=-1)[:, None, :]
    sine_part = jnp.concatenate([jnp.sin(angles), jnp.sin(angles)], axis=-1)[:, None, :]
    turned = jnp.concatenate([-values[..., half_width:], values[..., :half_width]], axis=-1)
    return values * cosine + turned * sine_part


def gated(gate_up):
    return gate_up[:, :FF] * jax.nn.sigmoid(gate_up[:, :FF]) * gate_up[:, FF:]


def adam_update(weight, first_moment, second_moment, gradient, step_rate, decay_rate):
    first_new = BETA_ONE * first_moment + (1.0 - BETA_ONE) * gradient
    second_new = BETA_TWO * second_moment + (1.0 - BETA_TWO) * gradient * gradient
    update = (
        first_new
        / (1.0 - BETA_ONE**STEP)
        / (jnp.sqrt(second_new / (1.0 - BETA_TWO**STEP)) + ADAM_EPS)
    )
    return (first_new, second_new, weight * (1.0 - step_rate * decay_rate) - step_rate * update)


def partner(value):
    return lax.ppermute(value, "wide", [(k, k ^ 1) for k in range(8)])


def body(
    token_ids,
    target_ids,
    prefix_lengths,
    loss_positions,
    w_input,
    w_output,
    w_gate_up,
    w_down,
    norm_gains,
    embed_table,
    moment_input,
    moment_output,
    moment_gate_up,
    moment_down,
    table_first,
    table_second,
    gains_first,
    gains_second,
):
    wide = lax.axis_index("wide")
    narrow = lax.axis_index("narrow")
    core = wide % 2
    masters = (w_input[0], w_output[0], w_gate_up[0], w_down[0])
    moments = (moment_input[0], moment_output[0], moment_gate_up[0], moment_down[0])
    group_size = H // KVH
    kv_width = KVH * HD
    scale_factor = HD ** (-0.5)
    features = feature_table()
    columns = column_table()
    gains = pad_features(norm_gains)
    own_places = wide * ROWS + jnp.arange(ROWS)
    key_places = jnp.arange(SEQ)
    tokens = token_ids[:, 0]
    targets = target_ids[:, 0]
    prefixes = prefix_lengths[:, 0]
    positions = loss_positions[:, 0]

    own_positions = lax.dynamic_slice_in_dim(positions, wide * PICK, PICK, axis=1)
    own_targets = jnp.take_along_axis(targets, own_positions, axis=1).reshape(MB * PICK)
    own_counted = (own_positions >= prefixes[:, None]).astype(jnp.int32).reshape(MB * PICK)
    meta = jnp.pad(jnp.stack([own_targets, own_counted]), ((0, 6), (0, 128 - MB * PICK)))

    table_low = dot(embed_table.astype(BF16), features, 1, 0).astype(BF16)
    table_other = partner(table_low)

    shards = [
        to_shard(master.astype(BF16), rows) for master, rows in zip(masters, (RI, RO, RG, RD))
    ]
    ordered = tokens.reshape(MB, 8, ROWS).swapaxes(0, 1).reshape(2048)
    by_core = tokens.reshape(MB, 4, 2, ROWS).transpose(2, 1, 0, 3).reshape(2048)
    local_ids = by_core - wide * (16 * 384)
    holder, row = local_ids // 384, local_ids % 384
    swapped = holder % 4 * 4 + holder // 4
    found = jnp.where(row < 192, holder * 192 + row, (15 + swapped) * 192 + row)
    found = jnp.where((local_ids >= 0) & (local_ids < 16 * 384), found, 6144).astype(jnp.int32)
    wi, wo, wg, wd, info, x0 = fetch(
        *shards, meta, table_low.reshape(384, 8, 128), found
    )
    x0 = x0.reshape(256, DP).astype(F32)
    wi = wi.reshape(16, RI, DP)[:, :100].reshape(QKV, DP)
    wo = wo.reshape(DP, DP)
    wg = wg.reshape(2 * FF, DP)
    wd = wd.reshape(FF, DP)
    info = info.reshape(128, 8, 128)
    all_targets = info[:, 0, : MB * PICK].reshape(4096)
    all_counted = info[:, 1, : MB * PICK].reshape(4096).astype(F32)

    a = rms_norm(x0, gains[0]).astype(BF16)
    projected = dot(a, wi, 1, 1)
    places_all = jnp.concatenate([own_places, own_places])
    rows_count = MB * ROWS
    query = rotate(projected[:, : H * HD].reshape(rows_count, H, HD), places_all).astype(BF16)
    key_own = rotate(
        projected[:, H * HD : H * HD + kv_width].reshape(rows_count, KVH, HD), places_all
    ).astype(BF16)
    value_own = projected[:, H * HD + kv_width :].astype(BF16)
    kv_own = [
        part.reshape(MB, ROWS, kv_width).swapaxes(1, 2)
        for part in (key_own.reshape(rows_count, kv_width), value_own)
    ]
    kv_all = gather_keys(jnp.concatenate(kv_own)).reshape(4, KVH, HD, SEQ)

    def allowed_of(batch):
        return (key_places[None, :] <= own_places[:, None]) | (
            key_places[None, :] < prefixes[batch]
        )

    kept = []
    mixed_parts = []
    for batch in range(MB):
        q = query.reshape(MB, ROWS, KVH, group_size, HD)[batch]
        k, v = kv_all[batch], kv_all[MB + batch]
        scores = jnp.einsum("qkgd,kdt->kgqt", q, k, preferred_element_type=F32) * scale_factor
        scores = jnp.where(allowed_of(batch), scores, NEGATIVE)
        highest = jnp.max(scores, axis=-1, keepdims=True)
        exp_part = jnp.exp(scores - highest)
        exp_total = jnp.sum(exp_part, axis=-1, keepdims=True)
        log_total = highest + jnp.log(exp_total)
        probs = (exp_part / exp_total).astype(BF16)
        mixed = jnp.einsum("kgqt,kdt->qkgd", probs, v, preferred_element_type=F32)
        mixed_parts.append(mixed.reshape(ROWS, H * HD).astype(BF16))
        kept.append((q, k, v, log_total))
    o_pad = dot(jnp.concatenate(mixed_parts), features, 1, 0).astype(BF16)
    x1 = x0 + dot(o_pad, wo, 1, 1)

    b = rms_norm(x1, gains[1]).astype(BF16)
    gate_up = dot(b, wg, 1, 1)
    activated = gated(gate_up).astype(BF16)
    x2 = x1 + dot(activated, wd, 1, 0)

    final = rms_norm(x2, gains[2]).astype(BF16)
    own_offsets = (own_positions - wide * ROWS + jnp.arange(MB)[:, None] * ROWS).reshape(-1)
    all_rows = gather_rows(final[own_offsets]).reshape(4096, DP)
    logits = dot(all_rows, table_low, 1, 1)
    vocab_start = (wide * 16 + narrow) * 384
    hit = jnp.arange(384)[None, :] == (all_targets - vocab_start)[:, None]
    highest = jnp.max(logits, axis=-1)
    exp_total = jnp.sum(jnp.exp(logits - highest[:, None]), axis=-1)
    stats = jnp.stack([highest.reshape(32, 128), exp_total.reshape(32, 128)])
    log_total = small_all(stats, combine_stats, log_of_stats, (32, 128), 4, "row_totals")
    log_total = log_total.reshape(4096)
    hit_sum = jnp.sum(jnp.where(hit, logits, 0.0) * all_counted[:, None])
    logit_sum = jnp.sum(logits * all_counted[:, None])
    token_count = jnp.sum(all_counted)
    loss_known = jnp.sum(all_counted * (log_total + ZLOSS_WEIGHT * log_total * log_total))
    d_logits = (
        all_counted[:, None]
        * (
            (1.0 + 2.0 * ZLOSS_WEIGHT * log_total)[:, None] * jnp.exp(logits - log_total[:, None])
            - (1.0 - SMOOTH) * hit.astype(F32)
            - SMOOTH / V
        )
    ).astype(BF16)
    table_grad_rows = dot(d_logits, all_rows, 0, 0)
    d_by_core = d_logits.reshape(64, 2, 32, 384)
    d_mine = lax.dynamic_index_in_dim(d_by_core, core, 1, keepdims=False).reshape(2048, 384)
    d_theirs = lax.dynamic_index_in_dim(d_by_core, 1 - core, 1, keepdims=False).reshape(2048, 384)
    d_theirs = partner(d_theirs)
    row_part = dot(d_mine, table_low, 1, 0) + dot(d_theirs, table_other, 1, 0)
    d_rows = scatter_rows(row_part.astype(BF16).reshape(4, 4, 4, 32, DP))

    d_final = jnp.zeros((rows_count, DP), F32).at[own_offsets].add(d_rows)
    d_x2, d_gain_final = jax.vjp(rms_norm, x2, gains[2])[1](d_final)
    d_branch = d_x2.astype(BF16)
    d_activated = dot(d_branch, wd, 1, 1)
    d_gate_up = jax.vjp(gated, gate_up)[1](d_activated)[0].astype(BF16)
    d_b = dot(d_gate_up, wg, 1, 0)
    d_x1_part, d_gain_mlp = jax.vjp(rms_norm, x1, gains[1])[1](d_b)
    d_x1 = d_x2 + d_x1_part
    d_out = d_x1.astype(BF16)
    d_mixed_pad = dot(d_out, wo, 1, 0).astype(BF16)
    d_mixed = dot(d_mixed_pad, features, 1, 1).astype(BF16)
    d_queries, d_kv = [], []
    for batch in range(MB):
        q, k, v, log_sum = kept[batch]
        d_m = d_mixed.reshape(MB, ROWS, KVH, group_size, HD)[batch]
        scores = jnp.einsum("qkgd,kdt->kgqt", q, k, preferred_element_type=F32) * scale_factor
        scores = jnp.where(allowed_of(batch), scores, NEGATIVE)
        probs = jnp.exp(scores - log_sum)
        d_probs = jnp.einsum("qkgd,kdt->kgqt", d_m, v, preferred_element_type=F32)
        d_scores = (
            probs * (d_probs - jnp.sum(probs * d_probs, axis=-1, keepdims=True))
        ).astype(BF16)
        d_q = jnp.einsum("kgqt,kdt->qkgd", d_scores, k, preferred_element_type=F32) * scale_factor
        d_k = jnp.einsum("kgqt,qkgd->kdt", d_scores, q, preferred_element_type=F32) * scale_factor
        d_v = jnp.einsum(
            "kgqt,qkgd->kdt", probs.astype(BF16), d_m, preferred_element_type=F32
        )
        d_queries.append(d_q.reshape(ROWS, H, HD))
        d_kv.append((d_k.reshape(kv_width, SEQ), d_v.reshape(kv_width, SEQ)))
    d_kv_own = sum_keys([d_kv[0][0], d_kv[1][0], d_kv[0][1], d_kv[1][1]])
    d_kv_own = d_kv_own.swapaxes(1, 2).reshape(2, rows_count, kv_width)

    def unrotate(gradient, heads):
        primal = jnp.zeros((rows_count, heads, HD), F32)
        return jax.vjp(lambda values: rotate(values, places_all), primal)[1](gradient)[0]

    d_projected = jnp.concatenate(
        [
            unrotate(jnp.concatenate(d_queries), H).reshape(rows_count, H * HD),
            unrotate(d_kv_own[0].reshape(rows_count, KVH, HD), KVH).reshape(
                rows_count, kv_width
            ),
            d_kv_own[1],
        ],
        axis=1,
    ).astype(BF16)
    d_a = dot(d_projected, wi, 1, 0)
    d_x0_part, d_gain_attn = jax.vjp(rms_norm, x0, gains[0])[1](d_a)
    d_x0 = (d_x1 + d_x0_part).astype(BF16)

    def half_pair(value):
        mine = lax.dynamic_slice_in_dim(value, core * 512, 512, axis=1)
        theirs = lax.dynamic_slice_in_dim(value, (1 - core) * 512, 512, axis=1)
        return jnp.concatenate([mine, partner(theirs)])

    def both(value):
        return jnp.concatenate([value, partner(value)])

    d_projected_pad = dot(d_projected, columns, 1, 0).astype(BF16)
    grad_wd = dot(both(activated), half_pair(d_branch), 0, 0).astype(BF16)
    grad_wg = dot(both(d_gate_up), half_pair(b), 0, 0).astype(BF16)
    grad_wo = dot(both(d_out), half_pair(o_pad), 0, 0).astype(BF16)
    grad_wi = dot(both(d_projected_pad), half_pair(a), 0, 0).astype(BF16)
    table_grad, summed_grads = scatter_grads(
        d_x0,
        ordered[None, :],
        grad_wi.reshape(4, 4, RI, 512),
        grad_wo.reshape(2, 4, 2, RO, 512),
        grad_wg.reshape(2, 2, 2, 4, 160, 512),
        grad_wd.reshape(2, 4, 2, 160, 512),
    )
    grad_shards = (
        jnp.concatenate([summed_grads[1, 160:224], summed_grads[2, 160:208]]),
        summed_grads[0, 160:224],
        jnp.concatenate([summed_grads[0, :160], summed_grads[1, :160]]),
        summed_grads[2, :160],
    )

    table_grad = table_grad + table_grad_rows

    squares = sum(jnp.sum(shard * shard) for shard in grad_shards) + jnp.sum(
        table_grad * table_grad
    )
    table_grad = dot(table_grad, features, 1, 1, HIGH)
    gain_grads = jnp.stack([d_gain_attn, d_gain_mlp, d_gain_final]).reshape(24, 128)
    scalars = jnp.pad(jnp.stack([squares, hit_sum, logit_sum]), (0, 125))
    packed = jnp.pad(jnp.concatenate([gain_grads, scalars[None]]), ((0, 7), (0, 0)))
    summed = small_all(packed, jnp.add, lambda v: v, (32, 128), 5, "global_sums")
    gain_grad = unpad_features(summed[:24].reshape(3, DP))
    loss_total = loss_known - (1.0 - SMOOTH) * summed[24, 1] - SMOOTH / V * summed[24, 2]
    grad_norm = jnp.sqrt(summed[24, 0] + jnp.sum(gain_grad * gain_grad)) / token_count
    factor = jnp.minimum(1.0, CLIP_NORM / grad_norm) / token_count

    new_shards = [
        MOMENTUM * to_shard(moment, rows) + factor * grad
        for moment, rows, grad in zip(moments, (RI, RO, RG, RD), grad_shards)
    ]
    pieces = jnp.stack([jnp.pad(s, ((0, 320 - s.shape[0]), (0, 0))) for s in new_shards])
    turned, gram = gram_of(pieces)
    gram = gram.reshape(DP, DP)
    turned = lax.dynamic_slice_in_dim(turned, core * 160, 160)
    current = newton(gram, turned)
    pieces = current.reshape(160, 2, 4, 128).transpose(2, 1, 0, 3).reshape(8, 160, 128)
    pieces = lax.all_to_all(pieces, "wide", split_axis=0, concat_axis=0)
    pieces = pieces.reshape(4, 320, 128)
    new_moments, new_weights = [], []
    for kind, rows in enumerate((RI, RO, RG, RD)):
        count = masters[kind].shape[1]
        ortho = pieces[kind, :rows]
        new_moments.append(from_shard(new_shards[kind], count)[None])
        new_weights.append(
            (
                masters[kind] * (1.0 - MUON_RATE * WEIGHT_DECAY)
                - MUON_RATE * 0.2 * math.sqrt(count * 16) * from_shard(ortho, count)
            )[None]
        )
    table_m, table_v, table_new = adam_update(
        embed_table, table_first, table_second, factor * table_grad, TABLE_RATE, WEIGHT_DECAY
    )
    gains_m, gains_v, gains_new = adam_update(
        norm_gains, gains_first, gains_second, factor * gain_grad, GAIN_RATE, 0.0
    )
    return (
        loss_total,
        token_count,
        grad_norm,
        *new_moments,
        *new_weights,
        *[weight.astype(BF16) for weight in new_weights],
        table_m,
        table_v,
        table_new,
        table_new.astype(BF16),
        gains_m,
        gains_v,
        gains_new,
    )


def solution(mesh):
    whole = P()
    by_sequence = P(None, "narrow", None)
    matrix = P(None, "wide", "narrow")
    table = P(("wide", "narrow"), None)
    return jax.shard_map(
        body,
        mesh=mesh,
        in_specs=(
            (by_sequence, by_sequence, P(None, "narrow"), by_sequence)
            + (matrix,) * 4
            + (whole, table)
            + (matrix,) * 4
            + (table, table, whole, whole)
        ),
        out_specs=(whole,) * 3 + (matrix,) * 12 + (table,) * 4 + (whole,) * 3,
        check_vma=False,
    )
```

```python
import functools
import math

import jax
import jax.numpy as jnp
from jax import lax
from jax.experimental import pallas as pl
from jax.experimental.pallas import tpu as pltpu
from jax.sharding import PartitionSpec as P

D = 960
H = 15
KVH = 5
HD = 64
FF = 2560
V = 49152
QKV = 1600
ITERS = 5
STEP = 10
MB = 2
SEQ = 1024
ROWS = 128
PICK = 16
DP = 1024

NORM_EPS = 1e-05
ROPE_THETA = 100000.0
SMOOTH = 0.1
ZLOSS_WEIGHT = 0.0001
CLIP_NORM = 0.02
MOMENTUM = 0.95
NS_A = 3.4445
NS_B = -4.775
NS_C = 2.0315
MUON_RATE = 0.1
WEIGHT_DECAY = 0.1
BETA_ONE = 0.9
BETA_TWO = 0.95
TABLE_RATE = 0.03
GAIN_RATE = 0.4
ADAM_EPS = 1e-08
NEGATIVE = -1e30

HIGHEST = lax.Precision.HIGHEST
HIGH = lax.Precision.HIGH
F32 = jnp.float32
BF16 = jnp.bfloat16
MESH = pl.DeviceIdType.MESH
ANY = pl.BlockSpec(memory_space=pl.ANY)
VMEM = pl.BlockSpec(memory_space=pltpu.VMEM)

RI, RO, RG, RD = 112, 64, 320, 160


def my_place():
    wide = lax.axis_index("wide")
    narrow = lax.axis_index("narrow")
    return {
        "y": lax.div(wide, 2),
        "c": lax.rem(wide, 2),
        "z": lax.div(narrow, 4),
        "x": lax.rem(narrow, 4),
    }


def device(place):
    return (place["y"] * 2 + place["c"], place["z"] * 4 + place["x"])


def at_step(place, axis, step):
    return {**place, axis: lax.rem(place[axis] + step, 4)}


def other_core(place):
    return {**place, "c": 1 - place["c"]}


def greet(targets):
    barrier = pltpu.get_barrier_semaphore()
    for target in targets:
        pl.semaphore_signal(barrier, inc=1, device_id=device(target), device_id_type=MESH)
    pl.semaphore_wait(barrier, len(targets))


class Net:
    def __init__(self, send, recv):
        self.send = send
        self.recv = recv
        self.copies = []

    def put(self, src, dst, target):
        k = len(self.copies)
        copy = pltpu.make_async_remote_copy(
            src_ref=src,
            dst_ref=dst,
            send_sem=self.send.at[k],
            recv_sem=self.recv.at[k],
            device_id=device(target),
            device_id_type=MESH,
        )
        copy.start()
        self.copies.append(copy)
        return copy

    def finish(self):
        for copy in self.copies:
            copy.wait_send()


class Spread:
    def __init__(self, net, place, axes, items, with_core):
        self.net, self.place, self.axes, self.items = net, place, axes, items
        self.with_core = with_core
        self.sel = dict(place)
        self.phase = 0
        self.core = []

    def to_core(self, region, sel, half):
        if self.with_core and self.phase == len(self.axes) - 1:
            ref = region(sel, half)
            self.core.append(self.net.put(ref, ref, other_core(self.place)))

    def begin(self):
        self.axis = self.axes[self.phase]
        self.up, self.across, self.down = [at_step(self.place, self.axis, k) for k in (1, 2, 3)]
        self.first, self.second, self.onward = [], [], []
        for group, first_half in ((self.first, 0), (self.second, 1)):
            for region, halves in self.items:
                for target, origin, half in (
                    (self.up, self.down, first_half),
                    (self.down, self.up, 1 - first_half),
                ):
                    if halves[half] is not None:
                        ref = region(self.sel, halves[half])
                        copy = self.net.put(ref, ref, target)
                        group.append((copy, origin, target, region, halves[half]))
        for region, halves in self.items:
            for half in halves:
                if half is not None:
                    self.to_core(region, self.sel, half)

    def relay(self):
        for copy, origin, target, region, half in self.first:
            copy.wait_recv()
            sel = {**self.sel, self.axis: origin[self.axis]}
            ref = region(sel, half)
            self.onward.append((self.net.put(ref, ref, target), region, half))
            self.to_core(region, sel, half)

    def near(self):
        for copy, origin, _, region, half in self.second:
            copy.wait_recv()
            self.to_core(region, {**self.sel, self.axis: origin[self.axis]}, half)

    def far(self):
        for copy, region, half in self.onward:
            copy.wait_recv()
            self.to_core(region, {**self.sel, self.axis: self.across[self.axis]}, half)
        self.sel[self.axis] = None
        self.phase += 1

    def end(self):
        for copy in self.core:
            copy.wait_recv()


def gather_streams(net, place, streams, with_core):
    spreads = [Spread(net, place, axes, items, with_core) for axes, items in streams]
    for _ in range(len(streams[0][0])):
        for step in ("begin", "relay", "near", "far"):
            for spread in spreads:
                getattr(spread, step)()
    for spread in spreads:
        spread.end()


def pick(index):
    return slice(None) if index is None else index


def lanes_of(sel):
    if sel["y"] is None:
        return pl.ds(pl.multiple_of(sel["c"] * 512, 512), 512)
    return pl.ds(pl.multiple_of((sel["c"] * 4 + sel["y"]) * 128, 128), 128)


def halved(low, high):
    cut = low + (high - low) // 32 * 16
    return ((low, cut - low), (cut, high - cut))


def neighbours(place, axes=("x", "y", "z"), core=True):
    found = [at_step(place, axis, step) for axis in axes for step in (1, 3)]
    return found + ([other_core(place)] if core else [])


def fetch_kernel(
    gi, go, gg, gd, meta, table, ids, wi, wo, wg, wd, info, x0, *scratch
):
    slab, packed, theirs, got, send, recv, local = scratch
    place = my_place()

    def in_wi(sel, rows):
        return wi.at[pick(sel["z"]), pick(sel["x"]), pl.ds(*rows), lanes_of(sel)]

    def in_wo(sel, rows):
        z, x = sel["z"], sel["x"]
        xh, xl = (None, None) if x is None else (lax.div(x, 2), lax.rem(x, 2))
        return wo.at[pick(xh), pick(z), pick(xl), pl.ds(*rows), lanes_of(sel)]

    def in_wg(half):
        def region(sel, rows):
            z, x = sel["z"], sel["x"]
            zh, zl = (None, None) if z is None else (lax.div(z, 2), lax.rem(z, 2))
            return wg.at[pick(zh), half, pick(zl), pick(x), pl.ds(*rows), lanes_of(sel)]

        return region

    def in_wd(sel, rows):
        z, x = sel["z"], sel["x"]
        xh, xl = (None, None) if x is None else (lax.div(x, 2), lax.rem(x, 2))
        return wd.at[pick(xl), pick(z), pick(xh), pl.ds(*rows), lanes_of(sel)]

    def in_info(sel, rows):
        return info.at[pick(sel["z"]), pick(sel["x"]), pick(sel["y"]), sel["c"], :, :]

    owns = [
        (gi, in_wi(place, (0, RI))),
        (go, in_wo(place, (0, RO))),
        (gg.at[pl.ds(0, 160)], in_wg(0)(place, (0, 160))),
        (gg.at[pl.ds(160, 160)], in_wg(1)(place, (0, 160))),
        (gd, in_wd(place, (0, RD))),
        (meta, in_info(place, None)),
        (table.at[pl.ds(0, 192)], slab.at[pl.ds((place["z"] * 4 + place["x"]) * 192, 192)]),
        (table.at[pl.ds(192, 192)], slab.at[pl.ds((16 + place["x"] * 4 + place["z"]) * 192, 192)]),
    ]
    copies = [pltpu.make_async_copy(src, dst, local.at[k]) for k, (src, dst) in enumerate(owns)]
    for copy in copies:
        copy.start()
    for copy in copies:
        copy.wait()
    greet(neighbours(place))
    net = Net(send, recv)
    slab[pl.ds(6144, 8)] = jnp.zeros((8, 8, 128), BF16)

    def in_slab(major, minor, first):
        def region(sel, half):
            start = (first + sel[major] * 4) * 192
            if sel[minor] is None:
                return slab.at[pl.ds(start + half * 384, 384)]
            return slab.at[pl.ds(start + sel[minor] * 192 + half * 96, 96)]

        return region

    tables = [
        Spread(net, place, ("x", "z"), [(in_slab("z", "x", 0), (0, 1))], False),
        Spread(net, place, ("z", "x"), [(in_slab("x", "z", 16), (0, 1))], False),
    ]
    weights = [
        Spread(net, place, axes, items, True)
        for axes, items in (
            (("x", "z", "y"), [(in_wg(0), halved(0, 160)), (in_wo, halved(0, 64))]),
            (("z", "x", "y"), [(in_wg(1), halved(0, 160)), (in_wi, halved(0, 64))]),
            (("z", "y", "x"), [(in_wd, halved(0, 80)), (in_wi, halved(64, 112))]),
            (("x", "y", "z"), [(in_wd, halved(80, 160)), (in_info, ((0, 8), None))]),
        )
    ]

    def each(spreads, *steps):
        for step in steps:
            for spread in spreads:
                getattr(spread, step)()

    each(tables, "begin")
    each(weights, "begin")
    each(tables, "relay")
    each(weights, "relay")
    each(tables, "near", "far", "begin")
    each(weights, "near", "far", "begin", "relay", "near", "far", "begin")
    each(tables, "relay")
    each(weights, "relay")
    each(tables, "near")
    each(weights, "near")
    each(tables, "far")

    @pl.loop(0, 128)
    def _(block):
        for k in range(16):
            token = block * 16 + k
            packed[token] = slab[ids[token]]

    swap = net.put(
        packed.at[pl.ds((1 - place["c"]) * 1024, 1024)], theirs, other_core(place)
    )
    each(weights, "far")
    swap.wait_recv()
    add_up(theirs, [packed.at[pl.ds(place["c"] * 1024, 1024)], theirs])
    ring = Ring(
        net,
        place,
        "y",
        lambda k, half: theirs.at[pl.ds(k * 256 + half * 128, 128)],
        lambda k: got.at[k],
        lambda half: x0.at[pl.ds(half * 128, 128)],
    )
    ring.send_all()
    ring.pass_on()
    ring.close()
    each(weights, "end")
    net.finish()


def fetch(gi, go, gg, gd, meta, table, ids):
    shapes = [
        jax.ShapeDtypeStruct((4, 4, RI, DP), BF16),
        jax.ShapeDtypeStruct((2, 4, 2, RO, DP), BF16),
        jax.ShapeDtypeStruct((2, 2, 2, 4, 160, DP), BF16),
        jax.ShapeDtypeStruct((2, 4, 2, 160, DP), BF16),
        jax.ShapeDtypeStruct((4, 4, 4, 2, 8, 128), jnp.int32),
        jax.ShapeDtypeStruct((256, 8, 128), BF16),
    ]
    count = 226
    return pl.pallas_call(
        fetch_kernel,
        out_shape=shapes,
        in_specs=[ANY] * 6 + [pl.BlockSpec(memory_space=pltpu.SMEM)],
        out_specs=[ANY] * 5 + [VMEM],
        scratch_shapes=[
            pltpu.VMEM((6152, 8, 128), BF16),
            pltpu.VMEM((2048, 8, 128), BF16),
            pltpu.VMEM((1024, 8, 128), BF16),
            pltpu.VMEM((6, 128, 8, 128), BF16),
            pltpu.SemaphoreType.DMA((count,)),
            pltpu.SemaphoreType.DMA((count,)),
            pltpu.SemaphoreType.DMA((8,)),
        ],
        compiler_params=pltpu.CompilerParams(
            collective_id=0, has_side_effects=True, vmem_limit_bytes=56 << 20
        ),
        name="fetch",
    )(gi, go, gg, gd, meta, table, ids)


LANE_PARTS = ((0, 384), (384, 384), (768, 256))
ORDERS = (("x", "z", "y"), ("z", "y", "x"), ("y", "x", "z"))


def rows_kernel(own, rows, send, recv, local):
    place = my_place()
    greet(neighbours(place))

    def in_rows(lanes):
        def region(sel, part):
            return rows.at[
                pick(sel["z"]), pick(sel["x"]), pick(sel["y"]), sel["c"], pl.ds(*part), pl.ds(*lanes)
            ]

        return region

    copy = pltpu.make_async_copy(
        own, rows.at[place["z"], place["x"], place["y"], place["c"]], local
    )
    copy.start()
    copy.wait()
    streams = [
        (axes, [(in_rows(lanes), ((0, 16), (16, 16)))]) for axes, lanes in zip(ORDERS, LANE_PARTS)
    ]
    net = Net(send, recv)
    gather_streams(net, place, streams, True)
    net.finish()


def gather_rows(own):
    count = 90
    return pl.pallas_call(
        rows_kernel,
        out_shape=jax.ShapeDtypeStruct((4, 4, 4, 2, 32, DP), BF16),
        in_specs=[VMEM],
        out_specs=VMEM,
        scratch_shapes=[
            pltpu.SemaphoreType.DMA((count,)),
            pltpu.SemaphoreType.DMA((count,)),
            pltpu.SemaphoreType.DMA,
        ],
        compiler_params=pltpu.CompilerParams(
            collective_id=1, has_side_effects=True, vmem_limit_bytes=24 << 20
        ),
        name="gather_rows",
    )(own)


def small_peers(place):
    plane = [at_step(at_step(place, "z", k // 4), "x", k % 4) for k in range(1, 16)]
    column = [
        {**at_step(place, "y", k // 2), "c": lax.rem(place["c"] + k % 2, 2)} for k in range(1, 8)
    ]
    return plane, column


def combine_all(net, place, combine, own, held, narrow_slots, wide_slots):
    plane, column = small_peers(place)
    value = own
    for number, (slots, index, targets) in enumerate(
        (
            (narrow_slots, place["z"] * 4 + place["x"], plane),
            (wide_slots, place["y"] * 2 + place["c"], column),
        )
    ):
        copies = [net.put(value, slots.at[index], target) for target in targets]
        slots[index] = value[...]
        for copy in copies:
            copy.wait_recv()
        total = slots[0]
        for k in range(1, slots.shape[0]):
            total = combine(total, slots[k])
        if number == 0:
            held[...] = total
            value = held
    return total


def small_kernel(combine, last, own, out, held, narrow_slots, wide_slots, send, recv):
    place = my_place()
    plane, column = small_peers(place)
    greet(plane + column)
    net = Net(send, recv)
    out[...] = last(combine_all(net, place, combine, own, held, narrow_slots, wide_slots))
    net.finish()


def small_all(value, combine, last, out_shape, collective_id, name):
    shape = value.shape
    count = 22
    return pl.pallas_call(
        functools.partial(small_kernel, combine, last),
        out_shape=jax.ShapeDtypeStruct(out_shape, F32),
        in_specs=[VMEM],
        out_specs=VMEM,
        scratch_shapes=[
            pltpu.VMEM(shape, F32),
            pltpu.VMEM((16,) + shape, F32),
            pltpu.VMEM((8,) + shape, F32),
            pltpu.SemaphoreType.DMA((count,)),
            pltpu.SemaphoreType.DMA((count,)),
        ],
        compiler_params=pltpu.CompilerParams(collective_id=collective_id, has_side_effects=True),
        name=name,
    )(value)


def combine_stats(one, two):
    highest = jnp.maximum(one[0], two[0])
    total = one[1] * jnp.exp(one[0] - highest) + two[1] * jnp.exp(two[0] - highest)
    return jnp.stack([highest, total])


def log_of_stats(stats):
    return stats[0] + jnp.log(stats[1])


def add_up(dst, parts):
    if len(dst.shape) == 4:

        @pl.loop(0, dst.shape[0])
        def _(k):
            add_up(dst.at[k], [part.at[k] for part in parts])

        return
    if len(dst.shape) == 3:
        step = max(1, min(dst.shape[0], 32768 // (dst.shape[1] * dst.shape[2])))

        @pl.loop(0, dst.shape[0] // step)
        def _(k):
            block = pl.ds(k * step, step)
            total = parts[0][block].astype(F32)
            for part in parts[1:]:
                total = total + part[block].astype(F32)
            dst[block] = total.astype(dst.dtype)

        return
    total = parts[0][...].astype(F32)
    for part in parts[1:]:
        total = total + part[...].astype(F32)
    dst[...] = total.astype(dst.dtype)


class Ring:
    def __init__(self, net, place, axis, source, got, result):
        self.net, self.source, self.got, self.result = net, source, got, result
        steps = [at_step(place, axis, step) for step in range(4)]
        self.own, self.up, self.across, self.down = [step[axis] for step in steps]
        self.to_up, self.to_down = steps[1], steps[3]

    def send_across(self):
        self.far_up = self.net.put(self.source(self.across, 0), self.got(0), self.to_up)
        self.far_down = self.net.put(self.source(self.across, 1), self.got(1), self.to_down)

    def send_up(self):
        self.near_up = self.net.put(self.source(self.up, 1), self.got(2), self.to_up)

    def send_down(self):
        self.near_down = self.net.put(self.source(self.down, 0), self.got(3), self.to_down)

    def send_all(self):
        self.send_across()
        self.send_up()
        self.send_down()

    def pass_on(self):
        self.far_up.wait_recv()
        add_up(self.got(0), [self.source(self.up, 0), self.got(0)])
        self.on_up = self.net.put(self.got(0), self.got(4), self.to_up)
        self.far_down.wait_recv()
        add_up(self.got(1), [self.source(self.down, 1), self.got(1)])
        self.on_down = self.net.put(self.got(1), self.got(5), self.to_down)

    def close(self):
        for copy in (self.near_up, self.near_down, self.on_up, self.on_down):
            copy.wait_recv()
        add_up(self.result(0), [self.source(self.own, 0), self.got(4), self.got(3)])
        add_up(self.result(1), [self.source(self.own, 1), self.got(2), self.got(5)])


FAR_FIRST = (2, 1, 3, 0)


def start_scatter(net, place, order, source, gots, out, acc=None, parts=4):
    rows = out.shape[0] // 2
    halves = (pl.ds(0, rows), pl.ds(rows, rows))
    lead = ("z", "x", "y")[: len(order)]

    def block(sel, half):
        return source.at[tuple(pick(sel.get(axis)) for axis in lead) + (halves[half],)]

    def summed(sel, half):
        if acc is None:
            return block({order[0]: place[order[0]], **sel}, half)
        rest = [axis for axis in lead if axis != order[0]]
        return acc.at[tuple(pick(sel.get(axis)) for axis in rest) + (halves[half],)]

    stream = {"first": {}, "rest": []}
    one, two = order[:2]
    for sub, far in enumerate(FAR_FIRST if parts == 4 else ()):
        at_two = at_step(place, two, far)[two]
        stream["first"][far] = Ring(
            net,
            place,
            one,
            lambda k, half, at_two=at_two: block({one: k, two: at_two}, half),
            lambda k, sub=sub: gots[0].at[sub, k],
            lambda half, at_two=at_two: summed({two: at_two}, half),
        )
    if parts == 1:
        stream["rest"].append(
            Ring(
                net,
                place,
                one,
                lambda k, half: block({one: k}, half),
                lambda k: gots[0].at[k],
                lambda half: summed({}, half),
            )
        )
    for number in range(1, len(order)):
        done = {axis: place[axis] for axis in order[1:number]}

        def part(k, half, done=done, axis=order[number]):
            return summed({**done, axis: k}, half)

        if number + 1 < len(order):
            result = lambda half, part=part, axis=order[number]: part(place[axis], half)
        else:
            result = lambda half: out.at[halves[half]]
        stream["rest"].append(
            Ring(net, place, order[number], part, lambda k, n=number: gots[n].at[k], result)
        )
    return stream


def send_first(streams):
    for far in FAR_FIRST:
        for stream in streams:
            stream["first"][far].send_across()
    for far in FAR_FIRST:
        for stream in streams:
            stream["first"][far].send_up()
            stream["first"][far].send_down()


def pass_first(streams):
    for far in FAR_FIRST:
        for stream in streams:
            stream["first"][far].pass_on()


def close_first(streams):
    for far in FAR_FIRST:
        for stream in streams:
            stream["first"][far].close()
            following = stream["rest"][0]
            if far == 2:
                following.send_across()
            if far == 1:
                following.send_up()
            if far == 3:
                following.send_down()


def pass_rest(streams, number):
    for stream in streams:
        stream["rest"][number].pass_on()


def close_rest(streams, number):
    for stream in streams:
        stream["rest"][number].close()
        if number + 1 < len(stream["rest"]):
            stream["rest"][number + 1].send_all()


def send_whole(streams):
    for stream in streams:
        stream["rest"][0].send_all()


def finish_whole(streams):
    for number in range(len(streams[0]["rest"])):
        pass_rest(streams, number)
        close_rest(streams, number)


def got_shapes(depth, rows, lanes, first, later, parts=4):
    half = rows // 2
    shapes = []
    for number in range(depth):
        if number == 0 and parts == 4:
            lead = (4, 6) + (4,) * (depth - 2)
        else:
            lead = (6,) + (4,) * (depth - 1 - number)
        shapes.append(pltpu.VMEM(lead + (half, lanes), later if number else first))
    return shapes


def row_sums_kernel(part, out, *scratch):
    held = scratch[0:3]
    accs = scratch[12:15]
    send, recv, local = scratch[15:]
    place = my_place()
    copies = [
        pltpu.make_async_copy(part.at[:, :, :, :, pl.ds(*lanes)], held[k], local.at[k])
        for k, lanes in enumerate(LANE_PARTS)
    ]
    for copy in copies:
        copy.start()
    greet(neighbours(place, core=False))
    for copy in copies:
        copy.wait()
    net = Net(send, recv)
    streams = [
        start_scatter(
            net,
            place,
            order,
            held[k],
            scratch[3 + 3 * k : 6 + 3 * k],
            out.at[:, pl.ds(*lanes)],
            accs[k],
            1,
        )
        for k, (order, lanes) in enumerate(zip(ORDERS, LANE_PARTS))
    ]
    send_whole(streams)
    finish_whole(streams)
    net.finish()


def scatter_rows(part):
    scratch = [pltpu.VMEM((4, 4, 4, 32, lanes), part.dtype) for _, lanes in LANE_PARTS]
    for _, lanes in LANE_PARTS:
        scratch += got_shapes(3, 32, lanes, part.dtype, F32, 1)
    scratch += [pltpu.VMEM((4, 4, 32, lanes), F32) for _, lanes in LANE_PARTS]
    scratch += [
        pltpu.SemaphoreType.DMA((54,)),
        pltpu.SemaphoreType.DMA((54,)),
        pltpu.SemaphoreType.DMA((3,)),
    ]
    return pl.pallas_call(
        row_sums_kernel,
        out_shape=jax.ShapeDtypeStruct((32, DP), F32),
        in_specs=[ANY],
        out_specs=VMEM,
        scratch_shapes=scratch,
        compiler_params=pltpu.CompilerParams(
            collective_id=3, has_side_effects=True, vmem_limit_bytes=40 << 20
        ),
        name="scatter_rows",
    )(part)


GRAD_ORDERS = (("y", "x", "z"), ("y", "z", "x"), ("x", "z", "y"))


def grads_kernel(dx, ids, di, do, dg, dd, out, weights_out, *scratch):
    rows, table, chosen = scratch[:3]
    held = scratch[3:6]
    gots = scratch[6:10]
    weight_gots = scratch[10:19]
    accs = scratch[19:22]
    send, recv, local = scratch[22:]
    place = my_place()
    moves = [(dx, rows.at[place["y"], place["c"]])]
    for y in range(4):
        lanes = pl.ds(y * 128, 128)
        for z in range(4):
            for half in range(2):
                moves.append(
                    (
                        dg.at[z // 2, half, z % 2, :, :, lanes],
                        held[half].at[z, :, y, pl.ds(0, 160)],
                    )
                )
        for x in range(4):
            moves.append((dd.at[x % 2, :, x // 2, :, lanes], held[2].at[:, x, y, pl.ds(0, 160)]))
            moves.append((do.at[x // 2, :, x % 2, :, lanes], held[0].at[:, x, y, pl.ds(160, 64)]))
        for z in range(4):
            moves.append((di.at[z, :, pl.ds(0, 64), lanes], held[1].at[z, :, y, pl.ds(160, 64)]))
            moves.append((di.at[z, :, pl.ds(64, 48), lanes], held[2].at[z, :, y, pl.ds(160, 48)]))
    copies = [pltpu.make_async_copy(src, dst, local.at[k]) for k, (src, dst) in enumerate(moves)]
    copies[0].start()
    greet(neighbours(place))
    copies[0].wait()

    def in_rows(sel, part):
        return rows.at[pick(sel["y"]), sel["c"], pl.ds(*part)]

    net = Net(send, recv)
    spread = Spread(net, place, ("y",), [(in_rows, ((0, 128), (128, 128)))], True)
    spread.begin()
    for copy in copies[1:]:
        copy.start()
    held[2][:, :, :, 208:224, :] = jnp.zeros((4, 4, 4, 16, 128), BF16)
    spread.relay()
    for copy in copies[1:]:
        copy.wait()
    weights = [
        start_scatter(
            net,
            place,
            order,
            held[k],
            weight_gots[3 * k : 3 * k + 3],
            weights_out.at[k],
            accs[k],
            1,
        )
        for k, order in enumerate(GRAD_ORDERS)
    ]
    spread.near()
    spread.far()
    send_whole(weights)
    spread.end()
    base = (place["y"] * 2 + place["c"]) * 16

    def parts(count, place_of):
        @pl.loop(0, count)
        def _(k):
            z, x = place_of(k)
            start = (base + z * 4 + x) * 384

            @pl.loop(0, 24)
            def _(r):
                row = pl.multiple_of(r * 16, 16)
                number = lax.broadcasted_iota(jnp.int32, (16, 2048), 0) + (start + row)
                chosen[pl.ds(row, 16), :] = (number == ids[...]).astype(F32).astype(BF16)

            @pl.loop(0, 4)
            def _(l):
                lanes = pl.ds(pl.multiple_of(l * 256, 256), 256)
                values = rows[:, :, :, lanes].reshape(2048, 256)
                total = jnp.dot(chosen[...], values, preferred_element_type=F32)
                table[z, x, :, lanes] = total.astype(BF16)

    def further(axis, step):
        return lax.rem(place[axis] + step, 4)

    streams = [
        start_scatter(
            net,
            place,
            order,
            table.at[:, :, pl.ds(192 * k, 192)],
            gots[2 * k : 2 * k + 2],
            out.at[pl.ds(192 * k, 192)],
        )
        for k, order in enumerate((("x", "z"), ("z", "x")))
    ]
    by_x, by_z = streams[0]["first"], streams[1]["first"]
    parts(4, lambda k: (further("z", 2), further("x", k + 2)))
    for step in FAR_FIRST:
        by_z[step].send_across()
    by_x[2].send_across()
    parts(3, lambda k: (further("z", k + 3), further("x", 2)))
    for step in (1, 3, 0):
        by_x[step].send_across()
    by_x[2].send_up()
    by_x[2].send_down()
    by_z[2].send_up()
    by_z[2].send_down()
    third = lambda dz: parts(3, lambda k: (further("z", dz), further("x", k + 3)))
    third(1)
    for ring in (by_x[1], by_z[1], by_z[3], by_z[0]):
        ring.send_up()
    by_x[1].send_down()
    pass_rest(weights, 0)
    third(3)
    for ring in (by_x[3], by_z[1], by_z[3], by_z[0]):
        ring.send_down()
    by_x[3].send_up()
    third(0)
    by_x[0].send_up()
    by_x[0].send_down()
    pass_first(streams)
    close_rest(weights, 0)
    close_first(streams)
    pass_rest(weights, 1)
    close_rest(weights, 1)
    pass_rest(streams, 0)
    pass_rest(weights, 2)
    close_rest(streams, 0)
    close_rest(weights, 2)
    net.finish()


def scatter_grads(dx, ids, di, do, dg, dd):
    count = 3 * 18 + 2 * 30 + 14
    scratch = [
        pltpu.VMEM((4, 2, 256, DP), BF16),
        pltpu.VMEM((4, 4, 384, DP), BF16),
        pltpu.VMEM((384, 2048), BF16),
    ]
    scratch += [pltpu.VMEM((4, 4, 4, 224, 128), BF16)] * 3
    scratch += got_shapes(2, 192, DP, BF16, BF16) * 2
    scratch += got_shapes(3, 224, 128, BF16, F32, 1) * 3
    scratch += [pltpu.VMEM((4, 4, 224, 128), F32)] * 3
    scratch += [
        pltpu.SemaphoreType.DMA((count,)),
        pltpu.SemaphoreType.DMA((count,)),
        pltpu.SemaphoreType.DMA((97,)),
    ]
    return pl.pallas_call(
        grads_kernel,
        out_shape=[
            jax.ShapeDtypeStruct((384, DP), F32),
            jax.ShapeDtypeStruct((3, 224, 128), F32),
        ],
        in_specs=[ANY, VMEM] + [ANY] * 4,
        out_specs=[VMEM, VMEM],
        scratch_shapes=scratch,
        compiler_params=pltpu.CompilerParams(
            collective_id=2, has_side_effects=True, vmem_limit_bytes=60 << 20
        ),
        name="scatter_grads",
    )(dx, ids, di, do, dg, dd)


def lanes_of_wide(y, c):
    return pl.ds(pl.multiple_of((y * 2 + c) * 128, 128), 128)


def keys_kernel(own, out, send, recv, local):
    place = my_place()
    copy = pltpu.make_async_copy(own, out.at[:, :, lanes_of_wide(place["y"], place["c"])], local)
    copy.start()
    greet(neighbours(place, ("y",)))
    copy.wait()

    def region(sel, rows):
        return out.at[:, pl.ds(*rows), lanes_of_wide(sel["y"], sel["c"])]

    net = Net(send, recv)
    gather_streams(net, place, [(("y",), [(region, ((0, 160), (160, 160)))])], True)
    net.finish()


def gather_keys(own):
    return pl.pallas_call(
        keys_kernel,
        out_shape=jax.ShapeDtypeStruct((4, 320, SEQ), BF16),
        in_specs=[VMEM],
        out_specs=VMEM,
        scratch_shapes=[
            pltpu.SemaphoreType.DMA((14,)),
            pltpu.SemaphoreType.DMA((14,)),
            pltpu.SemaphoreType.DMA,
        ],
        compiler_params=pltpu.CompilerParams(
            collective_id=6, has_side_effects=True, vmem_limit_bytes=16 << 20
        ),
        name="gather_keys",
    )(own)


def key_sums_kernel(*refs):
    parts, out = refs[:4], refs[4]
    theirs, held, got, send, recv = refs[5:]
    place = my_place()
    greet(neighbours(place, ("y",)))
    net = Net(send, recv)
    swaps = [
        [
            net.put(
                part.at[:, lanes_of_wide(at_step(place, "y", step)["y"], 1 - place["c"])],
                theirs.at[at_step(place, "y", step)["y"], k],
                other_core(place),
            )
            for k, part in enumerate(parts)
        ]
        for step in FAR_FIRST
    ]
    ring = Ring(
        net,
        place,
        "y",
        lambda k, half: held.at[k, pl.ds(2 * half, 2)],
        lambda k: got.at[k],
        lambda half: out.at[pl.ds(2 * half, 2)],
    )
    for step, swap in zip(FAR_FIRST, swaps):
        y = at_step(place, "y", step)["y"]
        for k, part in enumerate(parts):
            swap[k].wait_recv()
            own = part[:, lanes_of_wide(y, place["c"])]
            held[y, k] = (own + theirs[y, k]).astype(BF16)
        if step == 2:
            ring.send_across()
        if step == 1:
            ring.send_up()
        if step == 3:
            ring.send_down()
    ring.pass_on()
    ring.close()
    net.finish()


def sum_keys(parts):
    return pl.pallas_call(
        key_sums_kernel,
        out_shape=jax.ShapeDtypeStruct((4, 320, 128), F32),
        in_specs=[VMEM] * 4,
        out_specs=VMEM,
        scratch_shapes=[
            pltpu.VMEM((4, 4, 320, 128), F32),
            pltpu.VMEM((4, 4, 320, 128), BF16),
            pltpu.VMEM((6, 2, 320, 128), BF16),
            pltpu.SemaphoreType.DMA((22,)),
            pltpu.SemaphoreType.DMA((22,)),
        ],
        compiler_params=pltpu.CompilerParams(
            collective_id=8, has_side_effects=True, vmem_limit_bytes=32 << 20
        ),
        name="sum_keys",
    )(*parts)


def gram_kernel(own, moments, grads, summed, new, turned, gram, part, *scratch):
    gots = scratch[:4]
    held, narrow_slots, wide_slots, send, recv = scratch[4:]
    place = my_place()
    plane, column = small_peers(place)
    greet(plane + column)
    net = Net(send, recv)
    total = combine_all(net, place, jnp.add, own, held, narrow_slots, wide_slots)
    summed[...] = total
    count = total[24:25, 3:4] * (1.0 / 128.0)
    squares = total[24:25, 0:1] + jnp.sum(total[:24] * total[:24], keepdims=True)
    factor = jnp.minimum(1.0, CLIP_NORM / (jnp.sqrt(squares) / count)) / count

    @pl.loop(0, 4)
    def _(k):
        new[k] = MOMENTUM * moments[k] + factor * grads[k]

    def lanes_from(y, c):
        return pl.ds(pl.multiple_of((c * 4 + y) * 128, 128), 128)

    mine = lanes_from(place["y"], place["c"])
    arrivals = []
    for step in (2, 1, 3):
        who = at_step(place, "y", step)
        arrivals.append(net.put(new.at[who["y"]], turned.at[:, mine], who))
    turned[:, mine] = new[place["y"]]
    for arrival in arrivals:
        arrival.wait_recv()
    half = turned.at[:, pl.ds(pl.multiple_of(place["c"] * 512, 512), 512)]
    net.put(half, half, other_core(place)).wait_recv()
    @pl.loop(0, 4)
    def _(k):
        rows = pl.ds(pl.multiple_of(place["c"] * 512 + k * 128, 128), 128)
        left = turned[:, rows].T
        for l in range(2):
            lanes = pl.ds(l * 512, 512)
            product = jnp.dot(left, turned[:, lanes], precision=HIGHEST, preferred_element_type=F32)
            for m in range(4):
                part[k, m, :, lanes] = product[m * 32 : m * 32 + 32]

    orders = (("x", "z"), ("z", "x"))
    lanes = (pl.ds(0, 512), pl.ds(512, 512))
    mine = gram.at[place["c"], place["z"], place["x"]]
    streams = [
        start_scatter(
            net,
            place,
            order,
            part.at[:, :, :, lane],
            gots[2 * k : 2 * k + 2],
            mine.at[:, lane],
            None,
            1,
        )
        for k, (order, lane) in enumerate(zip(orders, lanes))
    ]
    send_whole(streams)
    finish_whole(streams)

    def in_gram(lane):
        def region(sel, rows):
            return gram.at[sel["c"], pick(sel["z"]), pick(sel["x"]), pl.ds(*rows), lane]

        return region

    streams = [
        (order[::-1], [(in_gram(lane), ((0, 16), (16, 16)))]) for order, lane in zip(orders, lanes)
    ]
    gather_streams(net, place, streams, True)
    net.finish()


def gram_of(packed, moments, grads):
    count = 22 + 4 + 2 * 12 + 40
    scratch = [pltpu.VMEM((4, 4, 32, DP), F32)]
    scratch += got_shapes(2, 32, 512, F32, F32, 1) * 2
    scratch += [
        pltpu.VMEM((32, 128), F32),
        pltpu.VMEM((16, 32, 128), F32),
        pltpu.VMEM((8, 32, 128), F32),
        pltpu.SemaphoreType.DMA((count,)),
        pltpu.SemaphoreType.DMA((count,)),
    ]
    return pl.pallas_call(
        gram_kernel,
        out_shape=[
            jax.ShapeDtypeStruct((32, 128), F32),
            jax.ShapeDtypeStruct((4, 320, 128), F32),
            jax.ShapeDtypeStruct((320, DP), F32),
            jax.ShapeDtypeStruct((2, 4, 4, 32, DP), F32),
        ],
        in_specs=[VMEM] * 3,
        out_specs=[VMEM] * 4,
        scratch_shapes=scratch,
        compiler_params=pltpu.CompilerParams(
            collective_id=7, has_side_effects=True, vmem_limit_bytes=40 << 20
        ),
        name="gram_sums",
    )(packed, moments, grads)


def split(value, count):
    parts = []
    for _ in range(count):
        parts.append(value.astype(BF16))
        value = value - parts[-1].astype(F32)
    return parts


def product(left, right):
    count = len(left)
    total = None
    for order in range(count):
        for k in range(order + 1):
            term = jnp.dot(left[k], right[order - k], preferred_element_type=F32)
            total = term if total is None else total + term
    return total


def newton_kernel(gram, turned, out, power, *scratch):
    a_parts, q_parts, t_parts = scratch[0:3], scratch[3:6], scratch[6:8]

    def blocks(k):
        return pl.ds(pl.multiple_of(k * 256, 256), 256)

    def put(parts, i, j, value, count, mirror=True):
        for ref, part in zip(parts, split(value, count)):
            ref[blocks(i), blocks(j)] = part
            if mirror:
                ref[blocks(j), blocks(i)] = part.T

    def mirrored(left, right, count, emit):
        @pl.loop(0, 2)
        def _(half):
            for k in range(5):
                p = half * 5 + k
                i = sum((p >= edge).astype(jnp.int32) for edge in (4, 7, 9))
                j = p - lax.div(i * (7 - i), 2)
                value = product(
                    [ref[blocks(i), :] for ref in left[:count]],
                    [ref[:, blocks(j)] for ref in right[:count]],
                )
                emit(i, j, value)

    def diagonal(i, j):
        rows = lax.broadcasted_iota(jnp.int32, (256, 256), 0) + i * 256
        columns = lax.broadcasted_iota(jnp.int32, (256, 256), 1) + j * 256
        return rows == columns

    trace = jnp.zeros((), F32)
    for k in range(4):
        block = gram[k * 256 : (k + 1) * 256, k * 256 : (k + 1) * 256]
        trace = trace + jnp.sum(jnp.where(diagonal(0, 0), block, 0.0))
    scale = 1.0 / (jnp.sqrt(jnp.full((1, 1), trace, F32)) + 1e-07)

    @pl.loop(0, 16)
    def _(p):
        i, j = lax.div(p, 4), lax.rem(p, 4)
        value = gram[blocks(i), blocks(j)] * scale * scale
        power[blocks(i), blocks(j)] = value
        put(a_parts, i, j, value, 3, False)

    out[...] = turned[...] * scale

    def advance(count):
        def emit_step(i, j, value):
            value = NS_B * power[blocks(i), blocks(j)] + NS_C * value
            put(q_parts, i, j, value + jnp.where(diagonal(i, j), NS_A, 0.0), count)

        def emit_half(i, j, value):
            put(t_parts, i, j, value, 2)

        def emit_power(i, j, value):
            power[blocks(i), blocks(j)] = value
            put(a_parts, i, j, value, 2)

        mirrored(a_parts, a_parts, 2, emit_step)
        mirrored(q_parts, a_parts, count, emit_half)
        mirrored(t_parts, q_parts, 2, emit_power)
        current = split(out[...], 2)

        @pl.loop(0, 4)
        def _(j):
            out[:, blocks(j)] = product(current, [ref[:, blocks(j)] for ref in q_parts[:2]])

    advance(3)

    @pl.loop(0, ITERS - 2)
    def _(_step):
        advance(2)

    current = split(out[...], 2)
    once = power

    @pl.loop(0, 4)
    def _(j):
        once[0:160, blocks(j)] = product(current, [ref[:, blocks(j)] for ref in a_parts[:2]])

    applied = split(once[0:160, :], 2)

    @pl.loop(0, 4)
    def _(j):
        twice = product(applied, [ref[:, blocks(j)] for ref in a_parts[:2]])
        out[:, blocks(j)] = (
            NS_A * out[:, blocks(j)] + NS_B * once[0:160, blocks(j)] + NS_C * twice
        )


def newton(gram, turned):
    return pl.pallas_call(
        newton_kernel,
        out_shape=jax.ShapeDtypeStruct((160, DP), F32),
        in_specs=[VMEM, VMEM],
        out_specs=VMEM,
        scratch_shapes=[pltpu.VMEM((DP, DP), F32)] + [pltpu.VMEM((DP, DP), BF16)] * 8,
        compiler_params=pltpu.CompilerParams(vmem_limit_bytes=48 << 20),
        name="newton",
    )(gram, turned)


def pad_features(values):
    lead = values.shape[:-1]
    blocks = values.reshape(lead + (4, 2, 2, 60))
    blocks = jnp.moveaxis(blocks, -3, -4)
    blocks = jnp.pad(blocks, [(0, 0)] * (len(lead) + 3) + [(0, 4)])
    return blocks.reshape(lead + (DP,))


def unpad_features(values):
    blocks = values.reshape(values.shape[0], 2, 4, 2, 64)[..., :60]
    return blocks.transpose(0, 2, 1, 3, 4).reshape(values.shape[0], D)


def feature_table():
    feature = lax.broadcasted_iota(jnp.int32, (D, DP), 0)
    place = lax.broadcasted_iota(jnp.int32, (D, DP), 1)
    wide, rest = feature // 120, feature % 120
    where = ((wide % 2) * 4 + wide // 2) * 128 + (rest // 60) * 64 + rest % 60
    return (where == place).astype(BF16)


def column_table():
    column = lax.broadcasted_iota(jnp.int32, (QKV, 16 * RI), 0)
    place = lax.broadcasted_iota(jnp.int32, (QKV, 16 * RI), 1)
    return ((column // 100) * RI + column % 100 == place).astype(BF16)


def to_shard(matrix, rows):
    columns = matrix.shape[1]
    turned = matrix.T.reshape(columns, 2, 60)
    turned = jnp.pad(turned, ((0, rows - columns), (0, 0), (0, 4)))
    return turned.reshape(rows, 128)


def from_shard(shard, columns):
    return shard[:columns].reshape(columns, 2, 64)[:, :, :60].reshape(columns, 120).T


def dot(left, right, left_axis, right_axis, precision=None):
    return lax.dot_general(
        left,
        right,
        (((left_axis,), (right_axis,)), ((), ())),
        preferred_element_type=F32,
        precision=precision,
    )


def rms_norm(values, gain_row):
    mean = jnp.sum(values * values, axis=-1, keepdims=True) * (1.0 / D)
    return values * lax.rsqrt(mean + NORM_EPS) * gain_row


def rotate(values, places):
    half_width = HD // 2
    frequency = ROPE_THETA ** (-2.0 * jnp.arange(half_width).astype(F32) / HD)
    angles = places.astype(F32)[:, None] * frequency[None, :]
    cosine = jnp.concatenate([jnp.cos(angles), jnp.cos(angles)], axis=-1)[:, None, :]
    sine_part = jnp.concatenate([jnp.sin(angles), jnp.sin(angles)], axis=-1)[:, None, :]
    turned = jnp.concatenate([-values[..., half_width:], values[..., :half_width]], axis=-1)
    return values * cosine + turned * sine_part


def gated(gate_up):
    return gate_up[:, :FF] * jax.nn.sigmoid(gate_up[:, :FF]) * gate_up[:, FF:]


def adam_update(weight, first_moment, second_moment, gradient, step_rate, decay_rate):
    first_new = BETA_ONE * first_moment + (1.0 - BETA_ONE) * gradient
    second_new = BETA_TWO * second_moment + (1.0 - BETA_TWO) * gradient * gradient
    update = (
        first_new
        / (1.0 - BETA_ONE**STEP)
        / (jnp.sqrt(second_new / (1.0 - BETA_TWO**STEP)) + ADAM_EPS)
    )
    return (first_new, second_new, weight * (1.0 - step_rate * decay_rate) - step_rate * update)


def partner(value):
    return lax.ppermute(value, "wide", [(k, k ^ 1) for k in range(8)])


def body(
    token_ids,
    target_ids,
    prefix_lengths,
    loss_positions,
    w_input,
    w_output,
    w_gate_up,
    w_down,
    norm_gains,
    embed_table,
    moment_input,
    moment_output,
    moment_gate_up,
    moment_down,
    table_first,
    table_second,
    gains_first,
    gains_second,
):
    wide = lax.axis_index("wide")
    narrow = lax.axis_index("narrow")
    core = wide % 2
    masters = (w_input[0], w_output[0], w_gate_up[0], w_down[0])
    moments = (moment_input[0], moment_output[0], moment_gate_up[0], moment_down[0])
    group_size = H // KVH
    kv_width = KVH * HD
    scale_factor = HD ** (-0.5)
    features = feature_table()
    columns = column_table()
    gains = pad_features(norm_gains)
    own_places = wide * ROWS + jnp.arange(ROWS)
    key_places = jnp.arange(SEQ)
    tokens = token_ids[:, 0]
    targets = target_ids[:, 0]
    prefixes = prefix_lengths[:, 0]
    positions = loss_positions[:, 0]

    own_positions = lax.dynamic_slice_in_dim(positions, wide * PICK, PICK, axis=1)
    own_targets = jnp.take_along_axis(targets, own_positions, axis=1).reshape(MB * PICK)
    own_counted = (own_positions >= prefixes[:, None]).astype(jnp.int32).reshape(MB * PICK)
    meta = jnp.pad(jnp.stack([own_targets, own_counted]), ((0, 6), (0, 128 - MB * PICK)))

    table_low = dot(embed_table.astype(BF16), features, 1, 0).astype(BF16)
    table_other = partner(table_low)

    shards = [
        to_shard(master.astype(BF16), rows) for master, rows in zip(masters, (RI, RO, RG, RD))
    ]
    ordered = tokens.reshape(MB, 8, ROWS).swapaxes(0, 1).reshape(2048)
    by_core = tokens.reshape(MB, 4, 2, ROWS).transpose(2, 1, 0, 3).reshape(2048)
    local_ids = by_core - wide * (16 * 384)
    holder, row = local_ids // 384, local_ids % 384
    swapped = holder % 4 * 4 + holder // 4
    found = jnp.where(row < 192, holder * 192 + row, (15 + swapped) * 192 + row)
    found = jnp.where((local_ids >= 0) & (local_ids < 16 * 384), found, 6144).astype(jnp.int32)
    wi, wo, wg, wd, info, x0 = fetch(
        *shards, meta, table_low.reshape(384, 8, 128), found
    )
    x0 = x0.reshape(256, DP).astype(F32)
    wi = wi.reshape(16, RI, DP)[:, :100].reshape(QKV, DP)
    wo = wo.reshape(DP, DP)
    wg = wg.reshape(2 * FF, DP)
    wd = wd.reshape(FF, DP)
    info = info.reshape(128, 8, 128)
    all_targets = info[:, 0, : MB * PICK].reshape(4096)
    all_counted = info[:, 1, : MB * PICK].reshape(4096).astype(F32)

    a = rms_norm(x0, gains[0]).astype(BF16)
    projected = dot(a, wi, 1, 1)
    places_all = jnp.concatenate([own_places, own_places])
    rows_count = MB * ROWS
    query = rotate(projected[:, : H * HD].reshape(rows_count, H, HD), places_all).astype(BF16)
    key_own = rotate(
        projected[:, H * HD : H * HD + kv_width].reshape(rows_count, KVH, HD), places_all
    ).astype(BF16)
    value_own = projected[:, H * HD + kv_width :].astype(BF16)
    kv_own = [
        part.reshape(MB, ROWS, kv_width).swapaxes(1, 2)
        for part in (key_own.reshape(rows_count, kv_width), value_own)
    ]
    kv_all = gather_keys(jnp.concatenate(kv_own)).reshape(4, KVH, HD, SEQ)

    def allowed_of(batch):
        return (key_places[None, :] <= own_places[:, None]) | (
            key_places[None, :] < prefixes[batch]
        )

    kept = []
    mixed_parts = []
    for batch in range(MB):
        q = query.reshape(MB, ROWS, KVH, group_size, HD)[batch]
        k, v = kv_all[batch], kv_all[MB + batch]
        scores = jnp.einsum("qkgd,kdt->kgqt", q, k, preferred_element_type=F32) * scale_factor
        scores = jnp.where(allowed_of(batch), scores, NEGATIVE)
        highest = jnp.max(scores, axis=-1, keepdims=True)
        exp_part = jnp.exp(scores - highest)
        exp_total = jnp.sum(exp_part, axis=-1, keepdims=True)
        log_total = highest + jnp.log(exp_total)
        probs = (exp_part / exp_total).astype(BF16)
        mixed = jnp.einsum("kgqt,kdt->qkgd", probs, v, preferred_element_type=F32)
        mixed_parts.append(mixed.reshape(ROWS, H * HD).astype(BF16))
        kept.append((q, k, v, log_total))
    o_pad = dot(jnp.concatenate(mixed_parts), features, 1, 0).astype(BF16)
    x1 = x0 + dot(o_pad, wo, 1, 1)

    b = rms_norm(x1, gains[1]).astype(BF16)
    gate_up = dot(b, wg, 1, 1)
    activated = gated(gate_up).astype(BF16)
    x2 = x1 + dot(activated, wd, 1, 0)

    final = rms_norm(x2, gains[2]).astype(BF16)
    own_offsets = (own_positions - wide * ROWS + jnp.arange(MB)[:, None] * ROWS).reshape(-1)
    all_rows = gather_rows(final[own_offsets]).reshape(4096, DP)
    logits = dot(all_rows, table_low, 1, 1)
    vocab_start = (wide * 16 + narrow) * 384
    hit = jnp.arange(384)[None, :] == (all_targets - vocab_start)[:, None]
    highest = jnp.max(logits, axis=-1)
    exp_total = jnp.sum(jnp.exp(logits - highest[:, None]), axis=-1)
    stats = jnp.stack([highest.reshape(32, 128), exp_total.reshape(32, 128)])
    log_total = small_all(stats, combine_stats, log_of_stats, (32, 128), 4, "row_totals")
    log_total = log_total.reshape(4096)
    hit_sum = jnp.sum(jnp.where(hit, logits, 0.0) * all_counted[:, None])
    logit_sum = jnp.sum(logits * all_counted[:, None])
    token_count = jnp.sum(all_counted)
    loss_known = jnp.sum(all_counted * (log_total + ZLOSS_WEIGHT * log_total * log_total))
    d_logits = (
        all_counted[:, None]
        * (
            (1.0 + 2.0 * ZLOSS_WEIGHT * log_total)[:, None] * jnp.exp(logits - log_total[:, None])
            - (1.0 - SMOOTH) * hit.astype(F32)
            - SMOOTH / V
        )
    ).astype(BF16)
    table_grad_rows = dot(d_logits, all_rows, 0, 0)
    d_by_core = d_logits.reshape(64, 2, 32, 384)
    d_mine = lax.dynamic_index_in_dim(d_by_core, core, 1, keepdims=False).reshape(2048, 384)
    d_theirs = lax.dynamic_index_in_dim(d_by_core, 1 - core, 1, keepdims=False).reshape(2048, 384)
    d_theirs = partner(d_theirs)
    row_part = dot(d_mine, table_low, 1, 0) + dot(d_theirs, table_other, 1, 0)
    d_rows = scatter_rows(row_part.astype(BF16).reshape(4, 4, 4, 32, DP))

    d_final = jnp.zeros((rows_count, DP), F32).at[own_offsets].add(d_rows)
    d_x2, d_gain_final = jax.vjp(rms_norm, x2, gains[2])[1](d_final)
    d_branch = d_x2.astype(BF16)
    d_activated = dot(d_branch, wd, 1, 1)
    d_gate_up = jax.vjp(gated, gate_up)[1](d_activated)[0].astype(BF16)
    d_b = dot(d_gate_up, wg, 1, 0)
    d_x1_part, d_gain_mlp = jax.vjp(rms_norm, x1, gains[1])[1](d_b)
    d_x1 = d_x2 + d_x1_part
    d_out = d_x1.astype(BF16)
    d_mixed_pad = dot(d_out, wo, 1, 0).astype(BF16)
    d_mixed = dot(d_mixed_pad, features, 1, 1).astype(BF16)
    d_queries, d_kv = [], []
    for batch in range(MB):
        q, k, v, log_sum = kept[batch]
        d_m = d_mixed.reshape(MB, ROWS, KVH, group_size, HD)[batch]
        scores = jnp.einsum("qkgd,kdt->kgqt", q, k, preferred_element_type=F32) * scale_factor
        scores = jnp.where(allowed_of(batch), scores, NEGATIVE)
        probs = jnp.exp(scores - log_sum)
        d_probs = jnp.einsum("qkgd,kdt->kgqt", d_m, v, preferred_element_type=F32)
        d_scores = (
            probs * (d_probs - jnp.sum(probs * d_probs, axis=-1, keepdims=True))
        ).astype(BF16)
        d_q = jnp.einsum("kgqt,kdt->qkgd", d_scores, k, preferred_element_type=F32) * scale_factor
        d_k = jnp.einsum("kgqt,qkgd->kdt", d_scores, q, preferred_element_type=F32) * scale_factor
        d_v = jnp.einsum(
            "kgqt,qkgd->kdt", probs.astype(BF16), d_m, preferred_element_type=F32
        )
        d_queries.append(d_q.reshape(ROWS, H, HD))
        d_kv.append((d_k.reshape(kv_width, SEQ), d_v.reshape(kv_width, SEQ)))
    d_kv_own = sum_keys([d_kv[0][0], d_kv[1][0], d_kv[0][1], d_kv[1][1]])
    d_kv_own = d_kv_own.swapaxes(1, 2).reshape(2, rows_count, kv_width)

    def unrotate(gradient, heads):
        primal = jnp.zeros((rows_count, heads, HD), F32)
        return jax.vjp(lambda values: rotate(values, places_all), primal)[1](gradient)[0]

    d_projected = jnp.concatenate(
        [
            unrotate(jnp.concatenate(d_queries), H).reshape(rows_count, H * HD),
            unrotate(d_kv_own[0].reshape(rows_count, KVH, HD), KVH).reshape(
                rows_count, kv_width
            ),
            d_kv_own[1],
        ],
        axis=1,
    ).astype(BF16)
    d_a = dot(d_projected, wi, 1, 0)
    d_x0_part, d_gain_attn = jax.vjp(rms_norm, x0, gains[0])[1](d_a)
    d_x0 = (d_x1 + d_x0_part).astype(BF16)

    def half_pair(value):
        mine = lax.dynamic_slice_in_dim(value, core * 512, 512, axis=1)
        theirs = lax.dynamic_slice_in_dim(value, (1 - core) * 512, 512, axis=1)
        return jnp.concatenate([mine, partner(theirs)])

    def both(value):
        return jnp.concatenate([value, partner(value)])

    d_projected_pad = dot(d_projected, columns, 1, 0).astype(BF16)
    grad_wd = dot(both(activated), half_pair(d_branch), 0, 0).astype(BF16)
    grad_wg = dot(both(d_gate_up), half_pair(b), 0, 0).astype(BF16)
    grad_wo = dot(both(d_out), half_pair(o_pad), 0, 0).astype(BF16)
    grad_wi = dot(both(d_projected_pad), half_pair(a), 0, 0).astype(BF16)
    table_grad, summed_grads = scatter_grads(
        d_x0,
        ordered[None, :],
        grad_wi.reshape(4, 4, RI, 512),
        grad_wo.reshape(2, 4, 2, RO, 512),
        grad_wg.reshape(2, 2, 2, 4, 160, 512),
        grad_wd.reshape(2, 4, 2, 160, 512),
    )
    grad_shards = (
        jnp.concatenate([summed_grads[1, 160:224], summed_grads[2, 160:208]]),
        summed_grads[0, 160:224],
        jnp.concatenate([summed_grads[0, :160], summed_grads[1, :160]]),
        summed_grads[2, :160],
    )

    def stacked(shards):
        return jnp.stack([jnp.pad(s, ((0, 320 - s.shape[0]), (0, 0))) for s in shards])

    table_grad = table_grad + table_grad_rows
    squares = jnp.sum(summed_grads * summed_grads) + jnp.sum(table_grad * table_grad)
    table_grad = dot(table_grad, features, 1, 1, HIGH)
    gain_grads = jnp.stack([d_gain_attn, d_gain_mlp, d_gain_final]).reshape(24, 128)
    scalars = jnp.pad(jnp.stack([squares, hit_sum, logit_sum, token_count]), (0, 124))
    packed = jnp.pad(jnp.concatenate([gain_grads, scalars[None]]), ((0, 7), (0, 0)))
    old_moments = stacked([to_shard(m, rows) for m, rows in zip(moments, (RI, RO, RG, RD))])

    summed, new_shards, turned, gram = gram_of(packed, old_moments, stacked(grad_shards))
    gain_grad = unpad_features(summed[:24].reshape(3, DP))
    loss_total = loss_known - (1.0 - SMOOTH) * summed[24, 1] - SMOOTH / V * summed[24, 2]
    grad_norm = jnp.sqrt(summed[24, 0] + jnp.sum(gain_grad * gain_grad)) / token_count
    factor = jnp.minimum(1.0, CLIP_NORM / grad_norm) / token_count
    gram = gram.reshape(DP, DP)
    turned = lax.dynamic_slice_in_dim(turned, core * 160, 160)
    current = newton(gram, turned)
    pieces = current.reshape(160, 2, 4, 128).transpose(2, 1, 0, 3).reshape(8, 160, 128)
    pieces = lax.all_to_all(pieces, "wide", split_axis=0, concat_axis=0)
    pieces = pieces.reshape(4, 320, 128)
    new_moments, new_weights = [], []
    for kind, rows in enumerate((RI, RO, RG, RD)):
        count = masters[kind].shape[1]
        ortho = pieces[kind, :rows]
        new_moments.append(from_shard(new_shards[kind], count)[None])
        new_weights.append(
            (
                masters[kind] * (1.0 - MUON_RATE * WEIGHT_DECAY)
                - MUON_RATE * 0.2 * math.sqrt(count * 16) * from_shard(ortho, count)
            )[None]
        )
    table_m, table_v, table_new = adam_update(
        embed_table, table_first, table_second, factor * table_grad, TABLE_RATE, WEIGHT_DECAY
    )
    gains_m, gains_v, gains_new = adam_update(
        norm_gains, gains_first, gains_second, factor * gain_grad, GAIN_RATE, 0.0
    )
    return (
        loss_total,
        token_count,
        grad_norm,
        *new_moments,
        *new_weights,
        *[weight.astype(BF16) for weight in new_weights],
        table_m,
        table_v,
        table_new,
        table_new.astype(BF16),
        gains_m,
        gains_v,
        gains_new,
    )


def solution(mesh):
    whole = P()
    by_sequence = P(None, "narrow", None)
    matrix = P(None, "wide", "narrow")
    table = P(("wide", "narrow"), None)
    return jax.shard_map(
        body,
        mesh=mesh,
        in_specs=(
            (by_sequence, by_sequence, P(None, "narrow"), by_sequence)
            + (matrix,) * 4
            + (whole, table)
            + (matrix,) * 4
            + (table, table, whole, whole)
        ),
        out_specs=(whole,) * 3 + (matrix,) * 12 + (table,) * 4 + (whole,) * 3,
        check_vma=False,
    )
```

```python
import functools
import math

import jax
import jax.numpy as jnp
from jax import lax
from jax.experimental import pallas as pl
from jax.experimental.pallas import tpu as pltpu
from jax.sharding import PartitionSpec as P

D = 960
H = 15
KVH = 5
HD = 64
FF = 2560
V = 49152
QKV = 1600
ITERS = 5
STEP = 10
MB = 2
SEQ = 1024
ROWS = 128
PICK = 16
DP = 1024

NORM_EPS = 1e-05
ROPE_THETA = 100000.0
SMOOTH = 0.1
ZLOSS_WEIGHT = 0.0001
CLIP_NORM = 0.02
MOMENTUM = 0.95
NS_A = 3.4445
NS_B = -4.775
NS_C = 2.0315
MUON_RATE = 0.1
WEIGHT_DECAY = 0.1
BETA_ONE = 0.9
BETA_TWO = 0.95
TABLE_RATE = 0.03
GAIN_RATE = 0.4
ADAM_EPS = 1e-08
NEGATIVE = -1e30

HIGHEST = lax.Precision.HIGHEST
HIGH = lax.Precision.HIGH
F32 = jnp.float32
BF16 = jnp.bfloat16
MESH = pl.DeviceIdType.MESH
ANY = pl.BlockSpec(memory_space=pl.ANY)
VMEM = pl.BlockSpec(memory_space=pltpu.VMEM)

RI, RO, RG, RD = 112, 64, 320, 160


def my_place():
    wide = lax.axis_index("wide")
    narrow = lax.axis_index("narrow")
    return {
        "y": lax.div(wide, 2),
        "c": lax.rem(wide, 2),
        "z": lax.div(narrow, 4),
        "x": lax.rem(narrow, 4),
    }


def device(place):
    return (place["y"] * 2 + place["c"], place["z"] * 4 + place["x"])


def at_step(place, axis, step):
    return {**place, axis: lax.rem(place[axis] + step, 4)}


def other_core(place):
    return {**place, "c": 1 - place["c"]}


def greet(targets):
    barrier = pltpu.get_barrier_semaphore()
    for target in targets:
        pl.semaphore_signal(barrier, inc=1, device_id=device(target), device_id_type=MESH)
    pl.semaphore_wait(barrier, len(targets))


class Net:
    def __init__(self, send, recv):
        self.send = send
        self.recv = recv
        self.copies = []

    def put(self, src, dst, target):
        k = len(self.copies)
        copy = pltpu.make_async_remote_copy(
            src_ref=src,
            dst_ref=dst,
            send_sem=self.send.at[k],
            recv_sem=self.recv.at[k],
            device_id=device(target),
            device_id_type=MESH,
        )
        copy.start()
        self.copies.append(copy)
        return copy

    def finish(self):
        for copy in self.copies:
            copy.wait_send()


class Spread:
    def __init__(self, net, place, axes, items, with_core):
        self.net, self.place, self.axes, self.items = net, place, axes, items
        self.with_core = with_core
        self.sel = dict(place)
        self.phase = 0
        self.core = []

    def to_core(self, region, sel, half):
        if self.with_core and self.phase == len(self.axes) - 1:
            ref = region(sel, half)
            self.core.append(self.net.put(ref, ref, other_core(self.place)))

    def begin(self):
        self.axis = self.axes[self.phase]
        self.up, self.across, self.down = [at_step(self.place, self.axis, k) for k in (1, 2, 3)]
        self.first, self.second, self.onward = [], [], []
        for group, first_half in ((self.first, 0), (self.second, 1)):
            for region, halves in self.items:
                for target, origin, half in (
                    (self.up, self.down, first_half),
                    (self.down, self.up, 1 - first_half),
                ):
                    if halves[half] is not None:
                        ref = region(self.sel, halves[half])
                        copy = self.net.put(ref, ref, target)
                        group.append((copy, origin, target, region, halves[half]))
        for region, halves in self.items:
            for half in halves:
                if half is not None:
                    self.to_core(region, self.sel, half)

    def relay(self):
        for copy, origin, target, region, half in self.first:
            copy.wait_recv()
            sel = {**self.sel, self.axis: origin[self.axis]}
            ref = region(sel, half)
            self.onward.append((self.net.put(ref, ref, target), region, half))
            self.to_core(region, sel, half)

    def near(self):
        for copy, origin, _, region, half in self.second:
            copy.wait_recv()
            self.to_core(region, {**self.sel, self.axis: origin[self.axis]}, half)

    def far(self):
        for copy, region, half in self.onward:
            copy.wait_recv()
            self.to_core(region, {**self.sel, self.axis: self.across[self.axis]}, half)
        self.sel[self.axis] = None
        self.phase += 1

    def end(self):
        for copy in self.core:
            copy.wait_recv()


def gather_streams(net, place, streams, with_core):
    spreads = [Spread(net, place, axes, items, with_core) for axes, items in streams]
    for _ in range(len(streams[0][0])):
        for step in ("begin", "relay", "near", "far"):
            for spread in spreads:
                getattr(spread, step)()
    for spread in spreads:
        spread.end()


def pick(index):
    return slice(None) if index is None else index


def lanes_of(sel):
    if sel["y"] is None:
        return pl.ds(pl.multiple_of(sel["c"] * 512, 512), 512)
    return pl.ds(pl.multiple_of((sel["c"] * 4 + sel["y"]) * 128, 128), 128)


def halved(low, high):
    cut = low + (high - low) // 32 * 16
    return ((low, cut - low), (cut, high - cut))


def neighbours(place, axes=("x", "y", "z"), core=True):
    found = [at_step(place, axis, step) for axis in axes for step in (1, 3)]
    return found + ([other_core(place)] if core else [])


def fetch_kernel(
    gi, go, gg, gd, meta, table, ids, wi, wo, wg, wd, info, x0, *scratch
):
    slab, packed, theirs, got, send, recv, local = scratch
    place = my_place()

    def in_wi(sel, rows):
        return wi.at[pick(sel["z"]), pick(sel["x"]), pl.ds(*rows), lanes_of(sel)]

    def in_wo(sel, rows):
        z, x = sel["z"], sel["x"]
        xh, xl = (None, None) if x is None else (lax.div(x, 2), lax.rem(x, 2))
        return wo.at[pick(xh), pick(z), pick(xl), pl.ds(*rows), lanes_of(sel)]

    def in_wg(half):
        def region(sel, rows):
            z, x = sel["z"], sel["x"]
            zh, zl = (None, None) if z is None else (lax.div(z, 2), lax.rem(z, 2))
            return wg.at[pick(zh), half, pick(zl), pick(x), pl.ds(*rows), lanes_of(sel)]

        return region

    def in_wd(sel, rows):
        z, x = sel["z"], sel["x"]
        xh, xl = (None, None) if x is None else (lax.div(x, 2), lax.rem(x, 2))
        return wd.at[pick(xl), pick(z), pick(xh), pl.ds(*rows), lanes_of(sel)]

    def in_info(sel, rows):
        return info.at[pick(sel["z"]), pick(sel["x"]), pick(sel["y"]), sel["c"], :, :]

    owns = [
        (gi, in_wi(place, (0, RI))),
        (go, in_wo(place, (0, RO))),
        (gg.at[pl.ds(0, 160)], in_wg(0)(place, (0, 160))),
        (gg.at[pl.ds(160, 160)], in_wg(1)(place, (0, 160))),
        (gd, in_wd(place, (0, RD))),
        (meta, in_info(place, None)),
        (table.at[pl.ds(0, 192)], slab.at[pl.ds((place["z"] * 4 + place["x"]) * 192, 192)]),
        (table.at[pl.ds(192, 192)], slab.at[pl.ds((16 + place["x"] * 4 + place["z"]) * 192, 192)]),
    ]
    copies = [pltpu.make_async_copy(src, dst, local.at[k]) for k, (src, dst) in enumerate(owns)]
    for copy in copies:
        copy.start()
    for copy in copies:
        copy.wait()
    greet(neighbours(place))
    net = Net(send, recv)
    slab[pl.ds(6144, 8)] = jnp.zeros((8, 8, 128), BF16)

    def in_slab(major, minor, first):
        def region(sel, half):
            start = (first + sel[major] * 4) * 192
            if sel[minor] is None:
                return slab.at[pl.ds(start + half * 384, 384)]
            return slab.at[pl.ds(start + sel[minor] * 192 + half * 96, 96)]

        return region

    tables = [
        Spread(net, place, ("x", "z"), [(in_slab("z", "x", 0), (0, 1))], False),
        Spread(net, place, ("z", "x"), [(in_slab("x", "z", 16), (0, 1))], False),
    ]
    weights = [
        Spread(net, place, axes, items, True)
        for axes, items in (
            (("x", "z", "y"), [(in_wg(0), halved(0, 160)), (in_wo, halved(0, 64))]),
            (("z", "x", "y"), [(in_wg(1), halved(0, 160)), (in_wi, halved(0, 64))]),
            (("z", "y", "x"), [(in_wd, halved(0, 80)), (in_wi, halved(64, 112))]),
            (("x", "y", "z"), [(in_wd, halved(80, 160)), (in_info, ((0, 8), None))]),
        )
    ]

    def each(spreads, *steps):
        for step in steps:
            for spread in spreads:
                getattr(spread, step)()

    each(tables, "begin")
    each(weights, "begin")
    each(tables, "relay")
    each(weights, "relay")
    each(tables, "near", "far", "begin")
    each(weights, "near", "far", "begin", "relay", "near", "far", "begin")
    each(tables, "relay")
    each(weights, "relay")
    each(tables, "near")
    each(weights, "near")
    each(tables, "far")

    @pl.loop(0, 128)
    def _(block):
        for k in range(16):
            token = block * 16 + k
            packed[token] = slab[ids[token]]

    swap = net.put(
        packed.at[pl.ds((1 - place["c"]) * 1024, 1024)], theirs, other_core(place)
    )
    each(weights, "far")
    swap.wait_recv()
    add_up(theirs, [packed.at[pl.ds(place["c"] * 1024, 1024)], theirs])
    ring = Ring(
        net,
        place,
        "y",
        lambda k, half: theirs.at[pl.ds(k * 256 + half * 128, 128)],
        lambda k: got.at[k],
        lambda half: x0.at[pl.ds(half * 128, 128)],
    )
    ring.send_all()
    ring.pass_on()
    ring.close()
    each(weights, "end")
    net.finish()


def fetch(gi, go, gg, gd, meta, table, ids):
    shapes = [
        jax.ShapeDtypeStruct((4, 4, RI, DP), BF16),
        jax.ShapeDtypeStruct((2, 4, 2, RO, DP), BF16),
        jax.ShapeDtypeStruct((2, 2, 2, 4, 160, DP), BF16),
        jax.ShapeDtypeStruct((2, 4, 2, 160, DP), BF16),
        jax.ShapeDtypeStruct((4, 4, 4, 2, 8, 128), jnp.int32),
        jax.ShapeDtypeStruct((256, 8, 128), BF16),
    ]
    count = 226
    return pl.pallas_call(
        fetch_kernel,
        out_shape=shapes,
        in_specs=[ANY] * 6 + [pl.BlockSpec(memory_space=pltpu.SMEM)],
        out_specs=[ANY] * 5 + [VMEM],
        scratch_shapes=[
            pltpu.VMEM((6152, 8, 128), BF16),
            pltpu.VMEM((2048, 8, 128), BF16),
            pltpu.VMEM((1024, 8, 128), BF16),
            pltpu.VMEM((6, 128, 8, 128), BF16),
            pltpu.SemaphoreType.DMA((count,)),
            pltpu.SemaphoreType.DMA((count,)),
            pltpu.SemaphoreType.DMA((8,)),
        ],
        compiler_params=pltpu.CompilerParams(
            collective_id=0, has_side_effects=True, vmem_limit_bytes=56 << 20
        ),
        name="fetch",
    )(gi, go, gg, gd, meta, table, ids)


LANE_PARTS = ((0, 384), (384, 384), (768, 256))
ORDERS = (("x", "z", "y"), ("z", "y", "x"), ("y", "x", "z"))


def rows_kernel(own, rows, send, recv, local):
    place = my_place()
    greet(neighbours(place))

    def in_rows(lanes):
        def region(sel, part):
            return rows.at[
                pick(sel["z"]), pick(sel["x"]), pick(sel["y"]), sel["c"], pl.ds(*part), pl.ds(*lanes)
            ]

        return region

    copy = pltpu.make_async_copy(
        own, rows.at[place["z"], place["x"], place["y"], place["c"]], local
    )
    copy.start()
    copy.wait()
    streams = [
        (axes, [(in_rows(lanes), ((0, 16), (16, 16)))]) for axes, lanes in zip(ORDERS, LANE_PARTS)
    ]
    net = Net(send, recv)
    gather_streams(net, place, streams, True)
    net.finish()


def gather_rows(own):
    count = 90
    return pl.pallas_call(
        rows_kernel,
        out_shape=jax.ShapeDtypeStruct((4, 4, 4, 2, 32, DP), BF16),
        in_specs=[VMEM],
        out_specs=VMEM,
        scratch_shapes=[
            pltpu.SemaphoreType.DMA((count,)),
            pltpu.SemaphoreType.DMA((count,)),
            pltpu.SemaphoreType.DMA,
        ],
        compiler_params=pltpu.CompilerParams(
            collective_id=1, has_side_effects=True, vmem_limit_bytes=24 << 20
        ),
        name="gather_rows",
    )(own)


def small_peers(place):
    plane = [at_step(at_step(place, "z", k // 4), "x", k % 4) for k in range(1, 16)]
    column = [
        {**at_step(place, "y", k // 2), "c": lax.rem(place["c"] + k % 2, 2)} for k in range(1, 8)
    ]
    return plane, column


def combine_all(net, place, combine, own, held, narrow_slots, wide_slots):
    plane, column = small_peers(place)
    value = own
    for number, (slots, index, targets) in enumerate(
        (
            (narrow_slots, place["z"] * 4 + place["x"], plane),
            (wide_slots, place["y"] * 2 + place["c"], column),
        )
    ):
        copies = [net.put(value, slots.at[index], target) for target in targets]
        slots[index] = value[...]
        for copy in copies:
            copy.wait_recv()
        total = slots[0]
        for k in range(1, slots.shape[0]):
            total = combine(total, slots[k])
        if number == 0:
            held[...] = total
            value = held
    return total


def small_kernel(combine, last, own, out, held, narrow_slots, wide_slots, send, recv):
    place = my_place()
    plane, column = small_peers(place)
    greet(plane + column)
    net = Net(send, recv)
    out[...] = last(combine_all(net, place, combine, own, held, narrow_slots, wide_slots))
    net.finish()


def small_all(value, combine, last, out_shape, collective_id, name):
    shape = value.shape
    count = 22
    return pl.pallas_call(
        functools.partial(small_kernel, combine, last),
        out_shape=jax.ShapeDtypeStruct(out_shape, F32),
        in_specs=[VMEM],
        out_specs=VMEM,
        scratch_shapes=[
            pltpu.VMEM(shape, F32),
            pltpu.VMEM((16,) + shape, F32),
            pltpu.VMEM((8,) + shape, F32),
            pltpu.SemaphoreType.DMA((count,)),
            pltpu.SemaphoreType.DMA((count,)),
        ],
        compiler_params=pltpu.CompilerParams(collective_id=collective_id, has_side_effects=True),
        name=name,
    )(value)


def combine_stats(one, two):
    highest = jnp.maximum(one[0], two[0])
    total = one[1] * jnp.exp(one[0] - highest) + two[1] * jnp.exp(two[0] - highest)
    return jnp.stack([highest, total])


def log_of_stats(stats):
    return stats[0] + jnp.log(stats[1])


def add_up(dst, parts):
    if len(dst.shape) == 4:

        @pl.loop(0, dst.shape[0])
        def _(k):
            add_up(dst.at[k], [part.at[k] for part in parts])

        return
    if len(dst.shape) == 3:
        step = max(1, min(dst.shape[0], 32768 // (dst.shape[1] * dst.shape[2])))

        @pl.loop(0, dst.shape[0] // step)
        def _(k):
            block = pl.ds(k * step, step)
            total = parts[0][block].astype(F32)
            for part in parts[1:]:
                total = total + part[block].astype(F32)
            dst[block] = total.astype(dst.dtype)

        return
    total = parts[0][...].astype(F32)
    for part in parts[1:]:
        total = total + part[...].astype(F32)
    dst[...] = total.astype(dst.dtype)


class Ring:
    def __init__(self, net, place, axis, source, got, result):
        self.net, self.source, self.got, self.result = net, source, got, result
        steps = [at_step(place, axis, step) for step in range(4)]
        self.own, self.up, self.across, self.down = [step[axis] for step in steps]
        self.to_up, self.to_down = steps[1], steps[3]

    def send_across(self):
        self.far_up = self.net.put(self.source(self.across, 0), self.got(0), self.to_up)
        self.far_down = self.net.put(self.source(self.across, 1), self.got(1), self.to_down)

    def send_up(self):
        self.near_up = self.net.put(self.source(self.up, 1), self.got(2), self.to_up)

    def send_down(self):
        self.near_down = self.net.put(self.source(self.down, 0), self.got(3), self.to_down)

    def send_all(self):
        self.send_across()
        self.send_up()
        self.send_down()

    def pass_on(self):
        self.far_up.wait_recv()
        add_up(self.got(0), [self.source(self.up, 0), self.got(0)])
        self.on_up = self.net.put(self.got(0), self.got(4), self.to_up)
        self.far_down.wait_recv()
        add_up(self.got(1), [self.source(self.down, 1), self.got(1)])
        self.on_down = self.net.put(self.got(1), self.got(5), self.to_down)

    def close(self):
        for copy in (self.near_up, self.near_down, self.on_up, self.on_down):
            copy.wait_recv()
        add_up(self.result(0), [self.source(self.own, 0), self.got(4), self.got(3)])
        add_up(self.result(1), [self.source(self.own, 1), self.got(2), self.got(5)])


FAR_FIRST = (2, 1, 3, 0)


def start_scatter(net, place, order, source, gots, out, acc=None, parts=4):
    rows = out.shape[0] // 2
    halves = (pl.ds(0, rows), pl.ds(rows, rows))
    lead = ("z", "x", "y")[: len(order)]

    def block(sel, half):
        return source.at[tuple(pick(sel.get(axis)) for axis in lead) + (halves[half],)]

    def summed(sel, half):
        if acc is None:
            return block({order[0]: place[order[0]], **sel}, half)
        rest = [axis for axis in lead if axis != order[0]]
        return acc.at[tuple(pick(sel.get(axis)) for axis in rest) + (halves[half],)]

    stream = {"first": {}, "rest": []}
    one, two = order[:2]
    for sub, far in enumerate(FAR_FIRST if parts == 4 else ()):
        at_two = at_step(place, two, far)[two]
        stream["first"][far] = Ring(
            net,
            place,
            one,
            lambda k, half, at_two=at_two: block({one: k, two: at_two}, half),
            lambda k, sub=sub: gots[0].at[sub, k],
            lambda half, at_two=at_two: summed({two: at_two}, half),
        )
    if parts == 1:
        stream["rest"].append(
            Ring(
                net,
                place,
                one,
                lambda k, half: block({one: k}, half),
                lambda k: gots[0].at[k],
                lambda half: summed({}, half),
            )
        )
    for number in range(1, len(order)):
        done = {axis: place[axis] for axis in order[1:number]}

        def part(k, half, done=done, axis=order[number]):
            return summed({**done, axis: k}, half)

        if number + 1 < len(order):
            result = lambda half, part=part, axis=order[number]: part(place[axis], half)
        else:
            result = lambda half: out.at[halves[half]]
        stream["rest"].append(
            Ring(net, place, order[number], part, lambda k, n=number: gots[n].at[k], result)
        )
    return stream


def send_first(streams):
    for far in FAR_FIRST:
        for stream in streams:
            stream["first"][far].send_across()
    for far in FAR_FIRST:
        for stream in streams:
            stream["first"][far].send_up()
            stream["first"][far].send_down()


def pass_first(streams):
    for far in FAR_FIRST:
        for stream in streams:
            stream["first"][far].pass_on()


def close_first(streams):
    for far in FAR_FIRST:
        for stream in streams:
            stream["first"][far].close()
            following = stream["rest"][0]
            if far == 2:
                following.send_across()
            if far == 1:
                following.send_up()
            if far == 3:
                following.send_down()


def pass_rest(streams, number):
    for stream in streams:
        stream["rest"][number].pass_on()


def close_rest(streams, number):
    for stream in streams:
        stream["rest"][number].close()
        if number + 1 < len(stream["rest"]):
            stream["rest"][number + 1].send_all()


def send_whole(streams):
    for stream in streams:
        stream["rest"][0].send_all()


def finish_whole(streams):
    for number in range(len(streams[0]["rest"])):
        pass_rest(streams, number)
        close_rest(streams, number)


def got_shapes(depth, rows, lanes, first, later, parts=4):
    half = rows // 2
    shapes = []
    for number in range(depth):
        if number == 0 and parts == 4:
            lead = (4, 6) + (4,) * (depth - 2)
        else:
            lead = (6,) + (4,) * (depth - 1 - number)
        shapes.append(pltpu.VMEM(lead + (half, lanes), later if number else first))
    return shapes


def row_sums_kernel(part, out, *scratch):
    held = scratch[0:3]
    accs = scratch[12:15]
    send, recv, local = scratch[15:]
    place = my_place()
    copies = [
        pltpu.make_async_copy(part.at[:, :, :, :, pl.ds(*lanes)], held[k], local.at[k])
        for k, lanes in enumerate(LANE_PARTS)
    ]
    for copy in copies:
        copy.start()
    greet(neighbours(place, core=False))
    for copy in copies:
        copy.wait()
    net = Net(send, recv)
    streams = [
        start_scatter(
            net,
            place,
            order,
            held[k],
            scratch[3 + 3 * k : 6 + 3 * k],
            out.at[:, pl.ds(*lanes)],
            accs[k],
            1,
        )
        for k, (order, lanes) in enumerate(zip(ORDERS, LANE_PARTS))
    ]
    send_whole(streams)
    finish_whole(streams)
    net.finish()


def scatter_rows(part):
    scratch = [pltpu.VMEM((4, 4, 4, 32, lanes), part.dtype) for _, lanes in LANE_PARTS]
    for _, lanes in LANE_PARTS:
        scratch += got_shapes(3, 32, lanes, part.dtype, F32, 1)
    scratch += [pltpu.VMEM((4, 4, 32, lanes), F32) for _, lanes in LANE_PARTS]
    scratch += [
        pltpu.SemaphoreType.DMA((54,)),
        pltpu.SemaphoreType.DMA((54,)),
        pltpu.SemaphoreType.DMA((3,)),
    ]
    return pl.pallas_call(
        row_sums_kernel,
        out_shape=jax.ShapeDtypeStruct((32, DP), F32),
        in_specs=[ANY],
        out_specs=VMEM,
        scratch_shapes=scratch,
        compiler_params=pltpu.CompilerParams(
            collective_id=3, has_side_effects=True, vmem_limit_bytes=40 << 20
        ),
        name="scatter_rows",
    )(part)


GRAD_ORDERS = (("y", "x", "z"), ("y", "z", "x"), ("x", "z", "y"))


def grads_kernel(dx, ids, di, do, dg, dd, out, weights_out, *scratch):
    rows, table, chosen = scratch[:3]
    held = scratch[3:6]
    gots = scratch[6:10]
    weight_gots = scratch[10:19]
    accs = scratch[19:22]
    send, recv, local = scratch[22:]
    place = my_place()
    moves = [(dx, rows.at[place["y"], place["c"]])]
    for y in range(4):
        lanes = pl.ds(y * 128, 128)
        for z in range(4):
            for half in range(2):
                moves.append(
                    (
                        dg.at[z // 2, half, z % 2, :, :, lanes],
                        held[half].at[z, :, y, pl.ds(0, 160)],
                    )
                )
        for x in range(4):
            moves.append((dd.at[x % 2, :, x // 2, :, lanes], held[2].at[:, x, y, pl.ds(0, 160)]))
            moves.append((do.at[x // 2, :, x % 2, :, lanes], held[0].at[:, x, y, pl.ds(160, 64)]))
        for z in range(4):
            moves.append((di.at[z, :, pl.ds(0, 64), lanes], held[1].at[z, :, y, pl.ds(160, 64)]))
            moves.append((di.at[z, :, pl.ds(64, 48), lanes], held[2].at[z, :, y, pl.ds(160, 48)]))
    copies = [pltpu.make_async_copy(src, dst, local.at[k]) for k, (src, dst) in enumerate(moves)]
    copies[0].start()
    greet(neighbours(place))
    copies[0].wait()

    def in_rows(sel, part):
        return rows.at[pick(sel["y"]), sel["c"], pl.ds(*part)]

    net = Net(send, recv)
    spread = Spread(net, place, ("y",), [(in_rows, ((0, 128), (128, 128)))], True)
    spread.begin()
    for copy in copies[1:]:
        copy.start()
    held[2][:, :, :, 208:224, :] = jnp.zeros((4, 4, 4, 16, 128), BF16)
    spread.relay()
    for copy in copies[1:]:
        copy.wait()
    weights = [
        start_scatter(
            net,
            place,
            order,
            held[k],
            weight_gots[3 * k : 3 * k + 3],
            weights_out.at[k],
            accs[k],
            1,
        )
        for k, order in enumerate(GRAD_ORDERS)
    ]
    spread.near()
    spread.far()
    send_whole(weights)
    spread.end()
    base = (place["y"] * 2 + place["c"]) * 16

    def parts(count, place_of):
        @pl.loop(0, count)
        def _(k):
            z, x = place_of(k)
            start = (base + z * 4 + x) * 384

            @pl.loop(0, 24)
            def _(r):
                row = pl.multiple_of(r * 16, 16)
                number = lax.broadcasted_iota(jnp.int32, (16, 2048), 0) + (start + row)
                chosen[pl.ds(row, 16), :] = (number == ids[...]).astype(F32).astype(BF16)

            @pl.loop(0, 4)
            def _(l):
                lanes = pl.ds(pl.multiple_of(l * 256, 256), 256)
                values = rows[:, :, :, lanes].reshape(2048, 256)
                total = jnp.dot(chosen[...], values, preferred_element_type=F32)
                table[z, x, :, lanes] = total.astype(BF16)

    def further(axis, step):
        return lax.rem(place[axis] + step, 4)

    streams = [
        start_scatter(
            net,
            place,
            order,
            table.at[:, :, pl.ds(192 * k, 192)],
            gots[2 * k : 2 * k + 2],
            out.at[pl.ds(192 * k, 192)],
        )
        for k, order in enumerate((("x", "z"), ("z", "x")))
    ]
    by_x, by_z = streams[0]["first"], streams[1]["first"]
    parts(4, lambda k: (further("z", 2), further("x", k + 2)))
    for step in FAR_FIRST:
        by_z[step].send_across()
    by_x[2].send_across()
    parts(3, lambda k: (further("z", k + 3), further("x", 2)))
    for step in (1, 3, 0):
        by_x[step].send_across()
    by_x[2].send_up()
    by_x[2].send_down()
    by_z[2].send_up()
    by_z[2].send_down()
    third = lambda dz: parts(3, lambda k: (further("z", dz), further("x", k + 3)))
    third(1)
    for ring in (by_x[1], by_z[1], by_z[3], by_z[0]):
        ring.send_up()
    by_x[1].send_down()
    for ring in (by_x[2], by_z[2], by_x[1]):
        ring.pass_on()
    pass_rest(weights, 0)
    third(3)
    for ring in (by_x[3], by_z[1], by_z[3], by_z[0]):
        ring.send_down()
    by_x[3].send_up()
    for ring in (by_z[1], by_x[3], by_z[3], by_z[0]):
        ring.pass_on()
    close_rest(weights, 0)
    third(0)
    by_x[0].send_up()
    by_x[0].send_down()
    by_x[0].pass_on()
    close_first(streams)
    pass_rest(weights, 1)
    close_rest(weights, 1)
    pass_rest(streams, 0)
    pass_rest(weights, 2)
    close_rest(streams, 0)
    close_rest(weights, 2)
    net.finish()


def scatter_grads(dx, ids, di, do, dg, dd):
    count = 3 * 18 + 2 * 30 + 14
    scratch = [
        pltpu.VMEM((4, 2, 256, DP), BF16),
        pltpu.VMEM((4, 4, 384, DP), BF16),
        pltpu.VMEM((384, 2048), BF16),
    ]
    scratch += [pltpu.VMEM((4, 4, 4, 224, 128), BF16)] * 3
    scratch += got_shapes(2, 192, DP, BF16, BF16) * 2
    scratch += got_shapes(3, 224, 128, BF16, F32, 1) * 3
    scratch += [pltpu.VMEM((4, 4, 224, 128), F32)] * 3
    scratch += [
        pltpu.SemaphoreType.DMA((count,)),
        pltpu.SemaphoreType.DMA((count,)),
        pltpu.SemaphoreType.DMA((97,)),
    ]
    return pl.pallas_call(
        grads_kernel,
        out_shape=[
            jax.ShapeDtypeStruct((384, DP), F32),
            jax.ShapeDtypeStruct((3, 224, 128), F32),
        ],
        in_specs=[ANY, VMEM] + [ANY] * 4,
        out_specs=[VMEM, VMEM],
        scratch_shapes=scratch,
        compiler_params=pltpu.CompilerParams(
            collective_id=2, has_side_effects=True, vmem_limit_bytes=60 << 20
        ),
        name="scatter_grads",
    )(dx, ids, di, do, dg, dd)


def lanes_of_wide(y, c):
    return pl.ds(pl.multiple_of((y * 2 + c) * 128, 128), 128)


def keys_kernel(own, out, send, recv, local):
    place = my_place()
    copy = pltpu.make_async_copy(own, out.at[:, :, lanes_of_wide(place["y"], place["c"])], local)
    copy.start()
    greet(neighbours(place, ("y",)))
    copy.wait()

    def region(sel, rows):
        return out.at[:, pl.ds(*rows), lanes_of_wide(sel["y"], sel["c"])]

    net = Net(send, recv)
    gather_streams(net, place, [(("y",), [(region, ((0, 160), (160, 160)))])], True)
    net.finish()


def gather_keys(own):
    return pl.pallas_call(
        keys_kernel,
        out_shape=jax.ShapeDtypeStruct((4, 320, SEQ), BF16),
        in_specs=[VMEM],
        out_specs=VMEM,
        scratch_shapes=[
            pltpu.SemaphoreType.DMA((14,)),
            pltpu.SemaphoreType.DMA((14,)),
            pltpu.SemaphoreType.DMA,
        ],
        compiler_params=pltpu.CompilerParams(
            collective_id=6, has_side_effects=True, vmem_limit_bytes=16 << 20
        ),
        name="gather_keys",
    )(own)


def key_sums_kernel(*refs):
    parts, out = refs[:4], refs[4]
    theirs, held, got, send, recv = refs[5:]
    place = my_place()
    greet(neighbours(place, ("y",)))
    net = Net(send, recv)
    swaps = [
        [
            net.put(
                part.at[:, lanes_of_wide(at_step(place, "y", step)["y"], 1 - place["c"])],
                theirs.at[at_step(place, "y", step)["y"], k],
                other_core(place),
            )
            for k, part in enumerate(parts)
        ]
        for step in FAR_FIRST
    ]
    ring = Ring(
        net,
        place,
        "y",
        lambda k, half: held.at[k, pl.ds(2 * half, 2)],
        lambda k: got.at[k],
        lambda half: out.at[pl.ds(2 * half, 2)],
    )
    for step, swap in zip(FAR_FIRST, swaps):
        y = at_step(place, "y", step)["y"]
        for k, part in enumerate(parts):
            swap[k].wait_recv()
            own = part[:, lanes_of_wide(y, place["c"])]
            held[y, k] = (own + theirs[y, k]).astype(BF16)
        if step == 2:
            ring.send_across()
        if step == 1:
            ring.send_up()
        if step == 3:
            ring.send_down()
    ring.pass_on()
    ring.close()
    net.finish()


def sum_keys(parts):
    return pl.pallas_call(
        key_sums_kernel,
        out_shape=jax.ShapeDtypeStruct((4, 320, 128), F32),
        in_specs=[VMEM] * 4,
        out_specs=VMEM,
        scratch_shapes=[
            pltpu.VMEM((4, 4, 320, 128), F32),
            pltpu.VMEM((4, 4, 320, 128), BF16),
            pltpu.VMEM((6, 2, 320, 128), BF16),
            pltpu.SemaphoreType.DMA((22,)),
            pltpu.SemaphoreType.DMA((22,)),
        ],
        compiler_params=pltpu.CompilerParams(
            collective_id=8, has_side_effects=True, vmem_limit_bytes=32 << 20
        ),
        name="sum_keys",
    )(*parts)


def gram_kernel(own, moments, grads, summed, new, chosen, gram, turned, part, *scratch):
    gots = scratch[:4]
    held, narrow_slots, wide_slots, send, recv = scratch[4:]
    place = my_place()
    plane, column = small_peers(place)
    greet(plane + column)
    net = Net(send, recv)
    total = combine_all(net, place, jnp.add, own, held, narrow_slots, wide_slots)
    summed[...] = total
    count = total[24:25, 3:4] * (1.0 / 128.0)
    squares = total[24:25, 0:1] + jnp.sum(total[:24] * total[:24], keepdims=True)
    factor = jnp.minimum(1.0, CLIP_NORM / (jnp.sqrt(squares) / count)) / count

    @pl.loop(0, 4)
    def _(k):
        new[k] = MOMENTUM * moments[k] + factor * grads[k]

    def lanes_from(y, c):
        return pl.ds(pl.multiple_of((c * 4 + y) * 128, 128), 128)

    mine = lanes_from(place["y"], place["c"])
    arrivals = []
    for step in (2, 1, 3):
        who = at_step(place, "y", step)
        arrivals.append(net.put(new.at[who["y"]], turned.at[:, mine], who))
    turned[:, mine] = new[place["y"]]
    for arrival in arrivals:
        arrival.wait_recv()
    half = turned.at[:, pl.ds(pl.multiple_of(place["c"] * 512, 512), 512)]
    net.put(half, half, other_core(place)).wait_recv()
    chosen[...] = turned[pl.ds(pl.multiple_of(place["c"] * 160, 160), 160), :]
    @pl.loop(0, 4)
    def _(k):
        rows = pl.ds(pl.multiple_of(place["c"] * 512 + k * 128, 128), 128)
        left = turned[:, rows].T
        for l in range(2):
            lanes = pl.ds(l * 512, 512)
            product = jnp.dot(left, turned[:, lanes], precision=HIGHEST, preferred_element_type=F32)
            for m in range(4):
                part[k, m, :, lanes] = product[m * 32 : m * 32 + 32]

    orders = (("x", "z"), ("z", "x"))
    lanes = (pl.ds(0, 512), pl.ds(512, 512))
    mine = gram.at[place["c"], place["z"], place["x"]]
    streams = [
        start_scatter(
            net,
            place,
            order,
            part.at[:, :, :, lane],
            gots[2 * k : 2 * k + 2],
            mine.at[:, lane],
            None,
            1,
        )
        for k, (order, lane) in enumerate(zip(orders, lanes))
    ]
    send_whole(streams)
    finish_whole(streams)

    def in_gram(lane):
        def region(sel, rows):
            return gram.at[sel["c"], pick(sel["z"]), pick(sel["x"]), pl.ds(*rows), lane]

        return region

    streams = [
        (order[::-1], [(in_gram(lane), ((0, 16), (16, 16)))]) for order, lane in zip(orders, lanes)
    ]
    gather_streams(net, place, streams, True)
    net.finish()


def gram_of(packed, moments, grads):
    count = 22 + 4 + 2 * 12 + 40
    scratch = [pltpu.VMEM((320, DP), F32), pltpu.VMEM((4, 4, 32, DP), F32)]
    scratch += got_shapes(2, 32, 512, F32, F32, 1) * 2
    scratch += [
        pltpu.VMEM((32, 128), F32),
        pltpu.VMEM((16, 32, 128), F32),
        pltpu.VMEM((8, 32, 128), F32),
        pltpu.SemaphoreType.DMA((count,)),
        pltpu.SemaphoreType.DMA((count,)),
    ]
    return pl.pallas_call(
        gram_kernel,
        out_shape=[
            jax.ShapeDtypeStruct((32, 128), F32),
            jax.ShapeDtypeStruct((4, 320, 128), F32),
            jax.ShapeDtypeStruct((160, DP), F32),
            jax.ShapeDtypeStruct((2, 4, 4, 32, DP), F32),
        ],
        in_specs=[VMEM] * 3,
        out_specs=[VMEM] * 4,
        scratch_shapes=scratch,
        compiler_params=pltpu.CompilerParams(
            collective_id=7, has_side_effects=True, vmem_limit_bytes=40 << 20
        ),
        name="gram_sums",
    )(packed, moments, grads)


def split(value, count):
    parts = []
    for _ in range(count):
        parts.append(value.astype(BF16))
        value = value - parts[-1].astype(F32)
    return parts


def product(left, right):
    count = len(left)
    total = None
    for order in range(count):
        for k in range(order + 1):
            term = jnp.dot(left[k], right[order - k], preferred_element_type=F32)
            total = term if total is None else total + term
    return total


def newton_kernel(gram, turned, out, power, *scratch):
    a_parts, q_parts, t_parts = scratch[0:3], scratch[3:6], scratch[6:8]

    def blocks(k):
        return pl.ds(pl.multiple_of(k * 256, 256), 256)

    def put(parts, i, j, value, count, mirror=True):
        for ref, part in zip(parts, split(value, count)):
            ref[blocks(i), blocks(j)] = part
            if mirror:
                ref[blocks(j), blocks(i)] = part.T

    def mirrored(left, right, count, emit):
        @pl.loop(0, 2)
        def _(half):
            for k in range(5):
                p = half * 5 + k
                i = sum((p >= edge).astype(jnp.int32) for edge in (4, 7, 9))
                j = p - lax.div(i * (7 - i), 2)
                value = product(
                    [ref[blocks(i), :] for ref in left[:count]],
                    [ref[:, blocks(j)] for ref in right[:count]],
                )
                emit(i, j, value)

    def diagonal(i, j):
        rows = lax.broadcasted_iota(jnp.int32, (256, 256), 0) + i * 256
        columns = lax.broadcasted_iota(jnp.int32, (256, 256), 1) + j * 256
        return rows == columns

    trace = jnp.zeros((), F32)
    for k in range(4):
        block = gram[k * 256 : (k + 1) * 256, k * 256 : (k + 1) * 256]
        trace = trace + jnp.sum(jnp.where(diagonal(0, 0), block, 0.0))
    scale = 1.0 / (jnp.sqrt(jnp.full((1, 1), trace, F32)) + 1e-07)

    @pl.loop(0, 16)
    def _(p):
        i, j = lax.div(p, 4), lax.rem(p, 4)
        value = gram[blocks(i), blocks(j)] * scale * scale
        power[blocks(i), blocks(j)] = value
        put(a_parts, i, j, value, 3, False)

    out[...] = turned[...] * scale

    def emit_step(count):
        def emit(i, j, value):
            value = NS_B * power[blocks(i), blocks(j)] + NS_C * value
            put(q_parts, i, j, value + jnp.where(diagonal(i, j), NS_A, 0.0), count)

        return emit

    def emit_half(i, j, value):
        put(t_parts, i, j, value, 2)

    def emit_power(i, j, value):
        power[blocks(i), blocks(j)] = value
        put(a_parts, i, j, value, 2)

    def applied(target, rows, source, matrix):
        current = split(source, 2)

        @pl.loop(0, 4)
        def _(j):
            target[rows, blocks(j)] = product(current, [ref[:, blocks(j)] for ref in matrix[:2]])

    everything = pl.ds(0, 160)

    def advance(count):
        mirrored(a_parts, a_parts, 2, emit_step(count))
        mirrored(q_parts, a_parts, count, emit_half)
        mirrored(t_parts, q_parts, 2, emit_power)
        applied(out, everything, out[...], q_parts)

    advance(3)

    @pl.loop(0, ITERS - 3)
    def _(_step):
        advance(2)

    mirrored(a_parts, a_parts, 2, emit_step(2))
    applied(out, everything, out[...], q_parts)
    once, twice, work = pl.ds(0, 160), pl.ds(160, 160), pl.ds(320, 160)
    for source, result in ((None, once), (once, twice)):
        applied(power, work, out[...] if source is None else power[source, :], q_parts)
        applied(power, result, power[work, :], a_parts)
        applied(power, result, power[result, :], q_parts)
    out[...] = NS_A * out[...] + NS_B * power[once, :] + NS_C * power[twice, :]


def newton(gram, turned):
    return pl.pallas_call(
        newton_kernel,
        out_shape=jax.ShapeDtypeStruct((160, DP), F32),
        in_specs=[VMEM, VMEM],
        out_specs=VMEM,
        scratch_shapes=[pltpu.VMEM((DP, DP), F32)] + [pltpu.VMEM((DP, DP), BF16)] * 8,
        compiler_params=pltpu.CompilerParams(vmem_limit_bytes=48 << 20),
        name="newton",
    )(gram, turned)


def pad_features(values):
    lead = values.shape[:-1]
    blocks = values.reshape(lead + (4, 2, 2, 60))
    blocks = jnp.moveaxis(blocks, -3, -4)
    blocks = jnp.pad(blocks, [(0, 0)] * (len(lead) + 3) + [(0, 4)])
    return blocks.reshape(lead + (DP,))


def unpad_features(values):
    blocks = values.reshape(values.shape[0], 2, 4, 2, 64)[..., :60]
    return blocks.transpose(0, 2, 1, 3, 4).reshape(values.shape[0], D)


def feature_table():
    feature = lax.broadcasted_iota(jnp.int32, (D, DP), 0)
    place = lax.broadcasted_iota(jnp.int32, (D, DP), 1)
    wide, rest = feature // 120, feature % 120
    where = ((wide % 2) * 4 + wide // 2) * 128 + (rest // 60) * 64 + rest % 60
    return (where == place).astype(BF16)


def column_table():
    column = lax.broadcasted_iota(jnp.int32, (QKV, 16 * RI), 0)
    place = lax.broadcasted_iota(jnp.int32, (QKV, 16 * RI), 1)
    return ((column // 100) * RI + column % 100 == place).astype(BF16)


def to_shard(matrix, rows):
    columns = matrix.shape[1]
    turned = matrix.T.reshape(columns, 2, 60)
    turned = jnp.pad(turned, ((0, rows - columns), (0, 0), (0, 4)))
    return turned.reshape(rows, 128)


def from_shard(shard, columns):
    return shard[:columns].reshape(columns, 2, 64)[:, :, :60].reshape(columns, 120).T


def dot(left, right, left_axis, right_axis, precision=None):
    return lax.dot_general(
        left,
        right,
        (((left_axis,), (right_axis,)), ((), ())),
        preferred_element_type=F32,
        precision=precision,
    )


def rms_norm(values, gain_row):
    mean = jnp.sum(values * values, axis=-1, keepdims=True) * (1.0 / D)
    return values * lax.rsqrt(mean + NORM_EPS) * gain_row


def rotate(values, places):
    half_width = HD // 2
    frequency = ROPE_THETA ** (-2.0 * jnp.arange(half_width).astype(F32) / HD)
    angles = places.astype(F32)[:, None] * frequency[None, :]
    cosine = jnp.concatenate([jnp.cos(angles), jnp.cos(angles)], axis=-1)[:, None, :]
    sine_part = jnp.concatenate([jnp.sin(angles), jnp.sin(angles)], axis=-1)[:, None, :]
    turned = jnp.concatenate([-values[..., half_width:], values[..., :half_width]], axis=-1)
    return values * cosine + turned * sine_part


def gated(gate_up):
    return gate_up[:, :FF] * jax.nn.sigmoid(gate_up[:, :FF]) * gate_up[:, FF:]


def adam_update(weight, first_moment, second_moment, gradient, step_rate, decay_rate):
    first_new = BETA_ONE * first_moment + (1.0 - BETA_ONE) * gradient
    second_new = BETA_TWO * second_moment + (1.0 - BETA_TWO) * gradient * gradient
    update = (
        first_new
        / (1.0 - BETA_ONE**STEP)
        / (jnp.sqrt(second_new / (1.0 - BETA_TWO**STEP)) + ADAM_EPS)
    )
    return (first_new, second_new, weight * (1.0 - step_rate * decay_rate) - step_rate * update)


def partner(value):
    return lax.ppermute(value, "wide", [(k, k ^ 1) for k in range(8)])


def body(
    token_ids,
    target_ids,
    prefix_lengths,
    loss_positions,
    w_input,
    w_output,
    w_gate_up,
    w_down,
    norm_gains,
    embed_table,
    moment_input,
    moment_output,
    moment_gate_up,
    moment_down,
    table_first,
    table_second,
    gains_first,
    gains_second,
):
    wide = lax.axis_index("wide")
    narrow = lax.axis_index("narrow")
    core = wide % 2
    masters = (w_input[0], w_output[0], w_gate_up[0], w_down[0])
    moments = (moment_input[0], moment_output[0], moment_gate_up[0], moment_down[0])
    group_size = H // KVH
    kv_width = KVH * HD
    scale_factor = HD ** (-0.5)
    features = feature_table()
    columns = column_table()
    gains = pad_features(norm_gains)
    own_places = wide * ROWS + jnp.arange(ROWS)
    key_places = jnp.arange(SEQ)
    tokens = token_ids[:, 0]
    targets = target_ids[:, 0]
    prefixes = prefix_lengths[:, 0]
    positions = loss_positions[:, 0]

    own_positions = lax.dynamic_slice_in_dim(positions, wide * PICK, PICK, axis=1)
    own_targets = jnp.take_along_axis(targets, own_positions, axis=1).reshape(MB * PICK)
    own_counted = (own_positions >= prefixes[:, None]).astype(jnp.int32).reshape(MB * PICK)
    meta = jnp.pad(jnp.stack([own_targets, own_counted]), ((0, 6), (0, 128 - MB * PICK)))

    table_low = dot(embed_table.astype(BF16), features, 1, 0).astype(BF16)
    table_other = partner(table_low)

    shards = [
        to_shard(master.astype(BF16), rows) for master, rows in zip(masters, (RI, RO, RG, RD))
    ]
    ordered = tokens.reshape(MB, 8, ROWS).swapaxes(0, 1).reshape(2048)
    by_core = tokens.reshape(MB, 4, 2, ROWS).transpose(2, 1, 0, 3).reshape(2048)
    local_ids = by_core - wide * (16 * 384)
    holder, row = local_ids // 384, local_ids % 384
    swapped = holder % 4 * 4 + holder // 4
    found = jnp.where(row < 192, holder * 192 + row, (15 + swapped) * 192 + row)
    found = jnp.where((local_ids >= 0) & (local_ids < 16 * 384), found, 6144).astype(jnp.int32)
    wi, wo, wg, wd, info, x0 = fetch(
        *shards, meta, table_low.reshape(384, 8, 128), found
    )
    x0 = x0.reshape(256, DP).astype(F32)
    wi = wi.reshape(16, RI, DP)[:, :100].reshape(QKV, DP)
    wo = wo.reshape(DP, DP)
    wg = wg.reshape(2 * FF, DP)
    wd = wd.reshape(FF, DP)
    info = info.reshape(128, 8, 128)
    all_targets = info[:, 0, : MB * PICK].reshape(4096)
    all_counted = info[:, 1, : MB * PICK].reshape(4096).astype(F32)

    a = rms_norm(x0, gains[0]).astype(BF16)
    projected = dot(a, wi, 1, 1)
    places_all = jnp.concatenate([own_places, own_places])
    rows_count = MB * ROWS
    query = rotate(projected[:, : H * HD].reshape(rows_count, H, HD), places_all).astype(BF16)
    key_own = rotate(
        projected[:, H * HD : H * HD + kv_width].reshape(rows_count, KVH, HD), places_all
    ).astype(BF16)
    value_own = projected[:, H * HD + kv_width :].astype(BF16)
    kv_own = [
        part.reshape(MB, ROWS, kv_width).swapaxes(1, 2)
        for part in (key_own.reshape(rows_count, kv_width), value_own)
    ]
    kv_all = gather_keys(jnp.concatenate(kv_own)).reshape(4, KVH, HD, SEQ)

    def allowed_of(batch):
        return (key_places[None, :] <= own_places[:, None]) | (
            key_places[None, :] < prefixes[batch]
        )

    kept = []
    mixed_parts = []
    for batch in range(MB):
        q = query.reshape(MB, ROWS, KVH, group_size, HD)[batch]
        k, v = kv_all[batch], kv_all[MB + batch]
        scores = jnp.einsum("qkgd,kdt->kgqt", q, k, preferred_element_type=F32) * scale_factor
        scores = jnp.where(allowed_of(batch), scores, NEGATIVE)
        highest = jnp.max(scores, axis=-1, keepdims=True)
        exp_part = jnp.exp(scores - highest)
        exp_total = jnp.sum(exp_part, axis=-1, keepdims=True)
        log_total = highest + jnp.log(exp_total)
        probs = (exp_part / exp_total).astype(BF16)
        mixed = jnp.einsum("kgqt,kdt->qkgd", probs, v, preferred_element_type=F32)
        mixed_parts.append(mixed.reshape(ROWS, H * HD).astype(BF16))
        kept.append((q, k, v, log_total))
    o_pad = dot(jnp.concatenate(mixed_parts), features, 1, 0).astype(BF16)
    x1 = x0 + dot(o_pad, wo, 1, 1)

    b = rms_norm(x1, gains[1]).astype(BF16)
    gate_up = dot(b, wg, 1, 1)
    activated = gated(gate_up).astype(BF16)
    x2 = x1 + dot(activated, wd, 1, 0)

    final = rms_norm(x2, gains[2]).astype(BF16)
    own_offsets = (own_positions - wide * ROWS + jnp.arange(MB)[:, None] * ROWS).reshape(-1)
    all_rows = gather_rows(final[own_offsets]).reshape(4096, DP)
    logits = dot(all_rows, table_low, 1, 1)
    vocab_start = (wide * 16 + narrow) * 384
    hit = jnp.arange(384)[None, :] == (all_targets - vocab_start)[:, None]
    highest = jnp.max(logits, axis=-1)
    exp_total = jnp.sum(jnp.exp(logits - highest[:, None]), axis=-1)
    stats = jnp.stack([highest.reshape(32, 128), exp_total.reshape(32, 128)])
    log_total = small_all(stats, combine_stats, log_of_stats, (32, 128), 4, "row_totals")
    log_total = log_total.reshape(4096)
    hit_sum = jnp.sum(jnp.where(hit, logits, 0.0) * all_counted[:, None])
    logit_sum = jnp.sum(logits * all_counted[:, None])
    token_count = jnp.sum(all_counted)
    loss_known = jnp.sum(all_counted * (log_total + ZLOSS_WEIGHT * log_total * log_total))
    d_logits = (
        all_counted[:, None]
        * (
            (1.0 + 2.0 * ZLOSS_WEIGHT * log_total)[:, None] * jnp.exp(logits - log_total[:, None])
            - (1.0 - SMOOTH) * hit.astype(F32)
            - SMOOTH / V
        )
    ).astype(BF16)
    table_grad_rows = lax.optimization_barrier(dot(d_logits, all_rows, 0, 0))
    d_by_core = d_logits.reshape(64, 2, 32, 384)
    d_mine = lax.dynamic_index_in_dim(d_by_core, core, 1, keepdims=False).reshape(2048, 384)
    d_theirs = lax.dynamic_index_in_dim(d_by_core, 1 - core, 1, keepdims=False).reshape(2048, 384)
    d_theirs = partner(d_theirs)
    row_part = dot(d_mine, table_low, 1, 0) + dot(d_theirs, table_other, 1, 0)
    d_rows = scatter_rows(row_part.astype(BF16).reshape(4, 4, 4, 32, DP))

    d_final = jnp.zeros((rows_count, DP), F32).at[own_offsets].add(d_rows)
    d_x2, d_gain_final = jax.vjp(rms_norm, x2, gains[2])[1](d_final)
    d_branch = d_x2.astype(BF16)
    d_activated = dot(d_branch, wd, 1, 1)
    d_gate_up = jax.vjp(gated, gate_up)[1](d_activated)[0].astype(BF16)
    d_b = dot(d_gate_up, wg, 1, 0)
    d_x1_part, d_gain_mlp = jax.vjp(rms_norm, x1, gains[1])[1](d_b)
    d_x1 = d_x2 + d_x1_part
    d_out = d_x1.astype(BF16)
    d_mixed_pad = dot(d_out, wo, 1, 0).astype(BF16)
    d_mixed = dot(d_mixed_pad, features, 1, 1).astype(BF16)
    d_queries, d_kv = [], []
    for batch in range(MB):
        q, k, v, log_sum = kept[batch]
        d_m = d_mixed.reshape(MB, ROWS, KVH, group_size, HD)[batch]
        scores = jnp.einsum("qkgd,kdt->kgqt", q, k, preferred_element_type=F32) * scale_factor
        scores = jnp.where(allowed_of(batch), scores, NEGATIVE)
        probs = jnp.exp(scores - log_sum)
        d_probs = jnp.einsum("qkgd,kdt->kgqt", d_m, v, preferred_element_type=F32)
        d_scores = (
            probs * (d_probs - jnp.sum(probs * d_probs, axis=-1, keepdims=True))
        ).astype(BF16)
        d_q = jnp.einsum("kgqt,kdt->qkgd", d_scores, k, preferred_element_type=F32) * scale_factor
        d_k = jnp.einsum("kgqt,qkgd->kdt", d_scores, q, preferred_element_type=F32) * scale_factor
        d_v = jnp.einsum(
            "kgqt,qkgd->kdt", probs.astype(BF16), d_m, preferred_element_type=F32
        )
        d_queries.append(d_q.reshape(ROWS, H, HD))
        d_kv.append((d_k.reshape(kv_width, SEQ), d_v.reshape(kv_width, SEQ)))
    d_kv_own = sum_keys([d_kv[0][0], d_kv[1][0], d_kv[0][1], d_kv[1][1]])
    d_kv_own = d_kv_own.swapaxes(1, 2).reshape(2, rows_count, kv_width)

    def unrotate(gradient, heads):
        primal = jnp.zeros((rows_count, heads, HD), F32)
        return jax.vjp(lambda values: rotate(values, places_all), primal)[1](gradient)[0]

    d_projected = jnp.concatenate(
        [
            unrotate(jnp.concatenate(d_queries), H).reshape(rows_count, H * HD),
            unrotate(d_kv_own[0].reshape(rows_count, KVH, HD), KVH).reshape(
                rows_count, kv_width
            ),
            d_kv_own[1],
        ],
        axis=1,
    ).astype(BF16)
    d_a = dot(d_projected, wi, 1, 0)
    d_x0_part, d_gain_attn = jax.vjp(rms_norm, x0, gains[0])[1](d_a)
    d_x0 = (d_x1 + d_x0_part).astype(BF16)

    def half_pair(value):
        mine = lax.dynamic_slice_in_dim(value, core * 512, 512, axis=1)
        theirs = lax.dynamic_slice_in_dim(value, (1 - core) * 512, 512, axis=1)
        return jnp.concatenate([mine, partner(theirs)])

    def both(value):
        return jnp.concatenate([value, partner(value)])

    d_projected_pad = dot(d_projected, columns, 1, 0).astype(BF16)
    grad_wd = dot(both(activated), half_pair(d_branch), 0, 0).astype(BF16)
    grad_wg = dot(both(d_gate_up), half_pair(b), 0, 0).astype(BF16)
    grad_wo = dot(both(d_out), half_pair(o_pad), 0, 0).astype(BF16)
    grad_wi = dot(both(d_projected_pad), half_pair(a), 0, 0).astype(BF16)
    table_grad, summed_grads = scatter_grads(
        d_x0,
        ordered[None, :],
        grad_wi.reshape(4, 4, RI, 512),
        grad_wo.reshape(2, 4, 2, RO, 512),
        grad_wg.reshape(2, 2, 2, 4, 160, 512),
        grad_wd.reshape(2, 4, 2, 160, 512),
    )
    grad_shards = (
        jnp.concatenate([summed_grads[1, 160:224], summed_grads[2, 160:208]]),
        summed_grads[0, 160:224],
        jnp.concatenate([summed_grads[0, :160], summed_grads[1, :160]]),
        summed_grads[2, :160],
    )

    def stacked(shards):
        return jnp.stack([jnp.pad(s, ((0, 320 - s.shape[0]), (0, 0))) for s in shards])

    table_grad = table_grad + table_grad_rows
    squares = jnp.sum(summed_grads * summed_grads) + jnp.sum(table_grad * table_grad)
    table_grad = dot(table_grad, features, 1, 1, HIGH)
    gain_grads = jnp.stack([d_gain_attn, d_gain_mlp, d_gain_final]).reshape(24, 128)
    scalars = jnp.pad(jnp.stack([squares, hit_sum, logit_sum, token_count]), (0, 124))
    packed = jnp.pad(jnp.concatenate([gain_grads, scalars[None]]), ((0, 7), (0, 0)))
    old_moments = stacked([to_shard(m, rows) for m, rows in zip(moments, (RI, RO, RG, RD))])

    summed, new_shards, turned, gram = gram_of(packed, old_moments, stacked(grad_shards))
    gain_grad = unpad_features(summed[:24].reshape(3, DP))
    loss_total = loss_known - (1.0 - SMOOTH) * summed[24, 1] - SMOOTH / V * summed[24, 2]
    grad_norm = jnp.sqrt(summed[24, 0] + jnp.sum(gain_grad * gain_grad)) / token_count
    factor = jnp.minimum(1.0, CLIP_NORM / grad_norm) / token_count
    gram = gram.reshape(DP, DP)
    current = newton(gram, turned)
    pieces = current.reshape(160, 2, 4, 128).transpose(2, 1, 0, 3).reshape(8, 160, 128)
    pieces = lax.all_to_all(pieces, "wide", split_axis=0, concat_axis=0)
    pieces = pieces.reshape(4, 320, 128)
    new_moments, new_weights = [], []
    for kind, rows in enumerate((RI, RO, RG, RD)):
        count = masters[kind].shape[1]
        ortho = pieces[kind, :rows]
        new_moments.append(from_shard(new_shards[kind], count)[None])
        new_weights.append(
            (
                masters[kind] * (1.0 - MUON_RATE * WEIGHT_DECAY)
                - MUON_RATE * 0.2 * math.sqrt(count * 16) * from_shard(ortho, count)
            )[None]
        )
    table_m, table_v, table_new = adam_update(
        embed_table, table_first, table_second, factor * table_grad, TABLE_RATE, WEIGHT_DECAY
    )
    gains_m, gains_v, gains_new = adam_update(
        norm_gains, gains_first, gains_second, factor * gain_grad, GAIN_RATE, 0.0
    )
    return (
        loss_total,
        token_count,
        grad_norm,
        *new_moments,
        *new_weights,
        *[weight.astype(BF16) for weight in new_weights],
        table_m,
        table_v,
        table_new,
        table_new.astype(BF16),
        gains_m,
        gains_v,
        gains_new,
    )


def solution(mesh):
    whole = P()
    by_sequence = P(None, "narrow", None)
    matrix = P(None, "wide", "narrow")
    table = P(("wide", "narrow"), None)
    return jax.shard_map(
        body,
        mesh=mesh,
        in_specs=(
            (by_sequence, by_sequence, P(None, "narrow"), by_sequence)
            + (matrix,) * 4
            + (whole, table)
            + (matrix,) * 4
            + (table, table, whole, whole)
        ),
        out_specs=(whole,) * 3 + (matrix,) * 12 + (table,) * 4 + (whole,) * 3,
        check_vma=False,
    )
```
